256 devices in a mesh: dp: 16 (over x_lo, z), mp: 16 (over x_hi, y, core).
Axes of the slice: x: 4 (x_hi: 2, x_lo: 2; x = x_hi * 2 + x_lo), y: 4, z: 8, core: 2. Of those that a mesh axis runs over, the one named last changes fastest.
Arguments:
- x_in: bfloat16 [64, 8, 8, 3072], P('dp', None, None, 'mp'), may hold values from -6 to 6
- dw_weight: float32 [7, 7, 3072], P(None, None, 'mp'), may hold values from -0.875 to 0.875
- dw_bias: float32 [3072], P('mp'), may hold values from -3 to 3
- ln_gain: float32 [3072], replicated, may hold values from 0.3 to 3
- ln_bias: float32 [3072], replicated, may hold values from -3 to 3
- w_in: bfloat16 [3072, 12288], P(None, 'mp'), may hold values from -0.109375 to 0.109375
- b_in: float32 [12288], P('mp'), may hold values from -3 to 3
- w_out: bfloat16 [12288, 3072], P('mp'), may hold values from -0.0546875 to 0.0546875
- b_out: float32 [3072], P('mp'), may hold values from -3 to 3
- layer_scale: float32 [3072], P('mp'), may hold values from 0.2 to 2
- head_gain: float32 [3072], P('mp'), may hold values from 0.3 to 3
- head_bias: float32 [3072], P('mp'), may hold values from -3 to 3
- projection: bfloat16 [3072, 1024], P('mp'), may hold values from -0.109375 to 0.109375
- text_emb: float32 [64, 1024], P('dp'), may hold values from -6 to 6
- labels: int32 [64], P('dp'), may hold values from 0 to 63, each once
Outputs:
- grad_input: float32 [64, 8, 8, 3072], P('dp', None, None, 'mp')
- grad_text: float32 [64, 1024], P('dp')
The draws below stay inside these ranges and needn't reach their ends.
Inputs may be any that keep to these rules, and one draw needn't show every extreme that they name: `labels`: a permutation: every text index appears exactly once.
All inputs are finite; a program needn't handle non-finite values.
Results may differ from the reference program's by a relative error of at most 0.028.
Values may be sent and summed in bfloat16 or wider, within the bound.
No kernel may reach another device: no remote copies, remote signals or barrier semaphores. Data moves between devices by JAX's collectives and lax.ppermute only.
A program may use at most 64 MiB of HBM per device.

```python
import math
import jax
import jax.numpy as jnp
from jax import lax

C = 3072
HID = 12288
E = 1024
KSIZE = 7
SIDE = 8
PAIRS = 64


def levels(stream_key, dims, shards, low, largest):
    gain = 1.0
    for axis_at, parts in shards:
        draws = jax.random.uniform(jax.random.fold_in(jax.random.fold_in(stream_key, 6), axis_at), (parts,), jnp.float32, low / len(shards), largest / len(shards))
        gain = gain * jnp.repeat(jnp.exp(draws), dims[axis_at] // parts).reshape((-1,) + (1,) * (len(dims) - 1 - axis_at))
    return gain


def bell_draw(stream_key, shape, deviation, limit, split=(), held_as=jnp.bfloat16):
    drawn = deviation * jax.random.normal(stream_key, shape, jnp.float32)
    if split:
        drawn = drawn * levels(stream_key, shape, split, -0.22, 0.18)
    return jnp.clip(drawn, -limit, limit).astype(held_as)


def setup_inputs(seed: int = 0) -> dict:
    arg_keys = jax.random.split(jax.random.key(seed), 16)
    x_in = bell_draw(arg_keys[0], (PAIRS, SIDE, SIDE, C), 1.0, 6.0, ((0, 16), (3, 16)))
    dw_weight = bell_draw(arg_keys[1], (KSIZE, KSIZE, C), (KSIZE * KSIZE) ** -0.5, 0.875, ((2, 16),), jnp.float32)
    dw_bias = bell_draw(arg_keys[2], (C,), 0.5, 3.0, ((0, 16),), jnp.float32)
    ln_gain = jnp.clip(jnp.exp(jax.random.uniform(arg_keys[3], (C,), jnp.float32, math.log(0.3), math.log(3.0))), 0.3, 3.0)
    ln_bias = bell_draw(arg_keys[4], (C,), 0.5, 3.0, (), jnp.float32)
    w_in = bell_draw(arg_keys[5], (C, HID), C ** -0.5, 0.109375, ((1, 16),))
    b_in = bell_draw(arg_keys[6], (HID,), 0.5, 3.0, ((0, 16),), jnp.float32)
    w_out = bell_draw(arg_keys[7], (HID, C), HID ** -0.5, 0.0546875, ((0, 16),))
    b_out = bell_draw(arg_keys[8], (C,), 0.5, 3.0, ((0, 16),), jnp.float32)
    layer_scale = jnp.clip(jnp.exp(math.log(2.0) - 2.3025851 * jax.random.uniform(arg_keys[9], (C,), jnp.float32) ** levels(arg_keys[9], (C,), ((0, 16),), -0.2, 0.2)), 0.2, 2.0)
    head_gain = jnp.clip(jnp.exp(math.log(3.0) - 2.3025851 * jax.random.uniform(arg_keys[10], (C,), jnp.float32) ** levels(arg_keys[10], (C,), ((0, 16),), -0.2, 0.2)), 0.3, 3.0)
    head_bias = bell_draw(arg_keys[11], (C,), 0.5, 3.0, ((0, 16),), jnp.float32)
    projection = bell_draw(arg_keys[12], (C, E), C ** -0.5, 0.109375, ((0, 16),))
    text_emb = jnp.clip(jax.random.uniform(arg_keys[13], (PAIRS, E), jnp.float32, -6.0, 6.0) * levels(arg_keys[13], (PAIRS, E), ((0, 16),), -0.4, 0.0), -6.0, 6.0)
    labels = jax.random.permutation(arg_keys[14], PAIRS).astype(jnp.int32)
    return {"x_in": x_in, "dw_weight": dw_weight, "dw_bias": dw_bias, "ln_gain": ln_gain, "ln_bias": ln_bias, "w_in": w_in, "b_in": b_in, "w_out": w_out, "b_out": b_out, "layer_scale": layer_scale, "head_gain": head_gain, "head_bias": head_bias, "projection": projection, "text_emb": text_emb, "labels": labels}


eps = 1e-06
logit_scale = 20.0
loss_scale = 512.0
root_half = 0.7071067811865476
inv_root_two_pi = 0.3989422804014327

def depthwise(source, kernel):
    extent = source.shape[1]
    reach = kernel.shape[0] // 2
    padded = jnp.pad(source, ((0, 0), (reach, reach), (reach, reach), (0, 0)))
    summed = jnp.zeros(source.shape, jnp.float32)
    for offset_row in range(kernel.shape[0]):
        for offset_col in range(kernel.shape[1]):
            summed = summed + padded[:, offset_row:offset_row + extent, offset_col:offset_col + extent, :] * kernel[offset_row, offset_col]
    return summed

def gelu_value(pre_act):
    return 0.5 * pre_act * (1.0 + jax.scipy.special.erf(pre_act * root_half))

def gelu_slope(pre_act):
    return 0.5 * (1.0 + jax.scipy.special.erf(pre_act * root_half)) + pre_act * jnp.exp(-0.5 * pre_act * pre_act) * inv_root_two_pi

def layer_stats(values):
    average = lax.optimization_barrier(jnp.mean(values, axis=-1, keepdims=True))
    squares = lax.optimization_barrier(jnp.mean(values * values, axis=-1, keepdims=True))
    return (average, lax.rsqrt(squares - average * average + eps))

def reference(x_in, dw_weight, dw_bias, ln_gain, ln_bias, w_in, b_in, w_out, b_out, layer_scale, head_gain, head_bias, projection, text_emb, labels):
    images = x_in.shape[0]
    side_len = x_in.shape[1]
    channels = x_in.shape[3]
    positions = side_len * side_len
    all_rows = images * positions
    highest = lax.Precision.HIGHEST
    conv_out = (depthwise(x_in.astype(jnp.float32), dw_weight) + dw_bias).astype(jnp.bfloat16)
    conv_rows = conv_out.reshape(all_rows, channels).astype(jnp.float32)
    average, inverse = layer_stats(conv_rows)
    centred = (conv_rows - average) * inverse
    normed = (centred * ln_gain + ln_bias).astype(jnp.bfloat16)
    hidden_pre = jnp.dot(normed, w_in, preferred_element_type=jnp.float32) + b_in
    activation = gelu_value(hidden_pre).astype(jnp.bfloat16)
    mixed = jnp.dot(activation, w_out, preferred_element_type=jnp.float32)
    mixed_mean = lax.optimization_barrier(jnp.mean(mixed.reshape(images, positions, channels), axis=1))
    input_mean = lax.optimization_barrier(jnp.mean(x_in.astype(jnp.float32).reshape(images, positions, channels), axis=1))
    pooled = input_mean + layer_scale * (mixed_mean + b_out)
    head_mean, head_inverse = layer_stats(pooled)
    head_centred = (pooled - head_mean) * head_inverse
    head_normed = (head_centred * head_gain + head_bias).astype(jnp.bfloat16)
    image_emb = jnp.dot(head_normed, projection, preferred_element_type=jnp.float32)
    image_len = jnp.sqrt(lax.optimization_barrier(jnp.sum(image_emb * image_emb, axis=1, keepdims=True)) + eps)
    image_unit = image_emb / image_len
    text_len = jnp.sqrt(lax.optimization_barrier(jnp.sum(text_emb * text_emb, axis=1, keepdims=True)) + eps)
    text_unit = text_emb / text_len
    logits = logit_scale * jnp.dot(image_unit, text_unit.T, precision=highest)
    weights = jnp.exp(logits)
    row_total = lax.optimization_barrier(jnp.sum(weights, axis=1))
    column_total = lax.optimization_barrier(jnp.sum(weights, axis=0))
    matched = (labels[:, None] == jnp.arange(images, dtype=jnp.int32)[None, :]).astype(jnp.float32)
    grad_logits = loss_scale * (0.5 * (weights / row_total[:, None] + weights / column_total[None, :]) - matched)
    grad_image_unit = logit_scale * jnp.dot(grad_logits, text_unit, precision=highest)
    grad_text_unit = logit_scale * jnp.dot(grad_logits.T, image_unit, precision=highest)
    grad_text = (grad_text_unit - text_unit * lax.optimization_barrier(jnp.sum(text_unit * grad_text_unit, axis=1, keepdims=True))) / text_len
    grad_image = ((grad_image_unit - image_unit * lax.optimization_barrier(jnp.sum(image_unit * grad_image_unit, axis=1, keepdims=True))) / image_len).astype(jnp.bfloat16)
    grad_head = jnp.dot(grad_image, projection.T, preferred_element_type=jnp.float32)
    head_scaled = grad_head * head_gain
    grad_pooled = head_inverse * (head_scaled - lax.optimization_barrier(jnp.mean(head_scaled, axis=1, keepdims=True)) - head_centred * lax.optimization_barrier(jnp.mean(head_scaled * head_centred, axis=1, keepdims=True)))
    grad_block = grad_pooled / positions
    grad_mixed = (grad_block * layer_scale).astype(jnp.bfloat16)
    grad_act = jnp.dot(grad_mixed, w_out.T, preferred_element_type=jnp.float32)
    hidden_width = w_in.shape[1]
    grad_pre = (grad_act[:, None, :] * gelu_slope(hidden_pre).reshape(images, positions, hidden_width)).reshape(all_rows, hidden_width).astype(jnp.bfloat16)
    grad_normed = jnp.dot(grad_pre, w_in.T, preferred_element_type=jnp.float32)
    normed_scaled = grad_normed * ln_gain
    grad_conv = inverse * (normed_scaled - lax.optimization_barrier(jnp.mean(normed_scaled, axis=1, keepdims=True)) - centred * lax.optimization_barrier(jnp.mean(normed_scaled * centred, axis=1, keepdims=True)))
    grad_field = grad_conv.reshape(images, side_len, side_len, channels)
    grad_input = grad_block[:, None, None, :] + depthwise(grad_field, dw_weight[::-1, ::-1])
    return (grad_input, grad_text)
```

```python
import jax
import jax.numpy as jnp
from jax import lax
from jax.sharding import PartitionSpec as P

eps = 1e-06
logit_scale = 20.0
loss_scale = 512.0
root_half = 0.7071067811865476
inv_root_two_pi = 0.3989422804014327
f32 = jnp.float32
bf16 = jnp.bfloat16
highest = lax.Precision.HIGHEST


def core_swap(array):
    length = lax.axis_size("mp")
    return lax.ppermute(array, "mp", [(i, i ^ 1) for i in range(length)])


def chip_exchange(array):
    length = lax.axis_size("mp")
    groups = [[i for i in range(core, length, 2)] for core in range(2)]
    return lax.all_to_all(array, "mp", 0, 0, axis_index_groups=groups)


def chip_gather(array):
    count = lax.axis_size("mp") // 2
    return chip_exchange(jnp.broadcast_to(array, (count,) + array.shape))


def dp_gather(array):
    count = lax.axis_size("dp")
    return lax.all_to_all(jnp.broadcast_to(array, (count,) + array.shape), "dp", 0, 0)


def own_first(array, core):
    first, second = array[..., 0, :], array[..., 1, :]
    return jnp.where(core == 0, jnp.stack([first, second]), jnp.stack([second, first]))


def split_two(array):
    high = lax.reduce_precision(array, 8, 7)
    return high, array - high


def depthwise(source, kernel):
    extent = source.shape[1]
    reach = kernel.shape[0] // 2
    padded = jnp.pad(source, ((0, 0), (reach, reach), (reach, reach), (0, 0)))
    summed = jnp.zeros(source.shape, f32)
    for offset_row in range(kernel.shape[0]):
        for offset_col in range(kernel.shape[1]):
            summed = (
                summed
                + padded[:, offset_row : offset_row + extent, offset_col : offset_col + extent, :]
                * kernel[offset_row, offset_col]
            )
    return summed


def gelu_value(pre_act):
    return 0.5 * pre_act * (1.0 + lax.erf(pre_act * root_half))


def gelu_slope(pre_act):
    return (
        0.5 * (1.0 + lax.erf(pre_act * root_half))
        + pre_act * jnp.exp(-0.5 * pre_act * pre_act) * inv_root_two_pi
    )


def body(
    x_in,
    dw_weight,
    dw_bias,
    ln_gain,
    ln_bias,
    w_in,
    b_in,
    w_out,
    b_out,
    layer_scale,
    head_gain,
    head_bias,
    projection,
    text_emb,
    labels,
):
    images, side = x_in.shape[0], x_in.shape[1]
    shard = x_in.shape[3]
    channels, hidden = w_in.shape
    positions = side * side
    rows = images * positions
    index = lax.axis_index("mp")
    core = index % 2
    chips = lax.axis_size("mp") // 2
    width = text_emb.shape[1]
    pairs = text_emb.shape[0]
    batch = pairs * lax.axis_size("dp")
    home = lax.axis_index("dp")

    text_block = jnp.concatenate(
        [text_emb, jnp.pad(labels.astype(f32)[None, :], ((0, 3), (0, width - pairs)))]
    )
    text_all = dp_gather(text_block)

    source = x_in.astype(f32)
    conv = (depthwise(source, dw_weight) + dw_bias).astype(bf16).reshape(rows, shard)
    conv_mine = chip_gather(conv.T)
    conv_other = core_swap(conv_mine)
    whole = jnp.stack([conv_mine, conv_other]).reshape(channels, rows).astype(f32)
    average = jnp.sum(whole, axis=0) / channels
    inverse = lax.rsqrt(jnp.sum(whole * whole, axis=0) / channels - average * average + eps)
    gain_own = own_first(ln_gain.reshape(chips, 2, shard), core).reshape(channels)
    bias_own = own_first(ln_bias.reshape(chips, 2, shard), core).reshape(channels)
    weight_pairs = w_in.reshape(chips, 2, shard, hidden)
    weight_own = jnp.where(
        core == 0,
        jnp.swapaxes(weight_pairs, 0, 1),
        jnp.swapaxes(weight_pairs[:, ::-1], 0, 1),
    ).reshape(channels, hidden)
    normed = (
        ((whole - average) * inverse) * gain_own[:, None] + bias_own[:, None]
    ).astype(bf16)
    hidden_pre = (
        lax.dot_general(normed, weight_own, (((0,), (0,)), ((), ())), preferred_element_type=f32)
        + b_in
    )
    activation = gelu_value(hidden_pre).reshape(images, positions, hidden)
    act_mean = jnp.mean(activation, axis=1)

    high, low = split_two(act_mean)
    mixed = jnp.dot(
        jnp.concatenate([high, low]).astype(bf16), w_out, preferred_element_type=f32
    )
    mixed = own_first((mixed[:images] + mixed[images:]).reshape(images, chips, 2, shard), core)
    mixed = mixed[0] + core_swap(mixed[1])
    mixed_mean = jnp.sum(chip_exchange(jnp.swapaxes(mixed, 0, 1)), axis=0)

    input_mean = jnp.mean(source.reshape(images, positions, shard), axis=1)
    pooled = input_mean + layer_scale * (mixed_mean + b_out)

    stats = jnp.concatenate([jnp.sum(pooled, axis=1), jnp.sum(pooled * pooled, axis=1)])
    stacked = jnp.concatenate([pooled * head_gain, head_gain[None], head_bias[None]])
    sums = jnp.concatenate(
        [
            jnp.dot(stacked, projection.astype(f32), precision=highest),
            jnp.pad(stats[None, :], ((0, 1), (0, width - 2 * images))),
        ]
    )
    sums = jnp.sum(chip_gather(sums + core_swap(sums)), axis=0)
    head_mean = sums[images + 2, :images] / channels
    head_inverse = lax.rsqrt(
        sums[images + 2, images : 2 * images] / channels - head_mean * head_mean + eps
    )
    head_centred = (pooled - head_mean[:, None]) * head_inverse[:, None]
    emb = (
        head_inverse[:, None] * (sums[:images] - head_mean[:, None] * sums[images])
        + sums[images + 1]
    )

    emb_all = dp_gather(emb).reshape(batch, width)
    text_raw = text_all[:, :pairs].reshape(batch, width)
    labels_all = text_all[:, pairs, :pairs].reshape(batch)
    image_len = jnp.sqrt(jnp.sum(emb_all * emb_all, axis=1, keepdims=True) + eps)
    image_unit = emb_all / image_len
    text_len = jnp.sqrt(jnp.sum(text_raw * text_raw, axis=1, keepdims=True) + eps)
    text_unit = text_raw / text_len
    logits = logit_scale * jnp.dot(image_unit, text_unit.T, precision=highest)
    weights = jnp.exp(logits)
    matched = (labels_all[:, None] == jnp.arange(batch, dtype=f32)[None, :]).astype(f32)
    grad_logits = loss_scale * (
        0.5
        * (
            weights / jnp.sum(weights, axis=1, keepdims=True)
            + weights / jnp.sum(weights, axis=0, keepdims=True)
        )
        - matched
    )

    def own(array, axis):
        return lax.dynamic_slice_in_dim(array, home * pairs, pairs, axis)

    grad_image_unit = logit_scale * jnp.dot(own(grad_logits, 0), text_unit, precision=highest)
    grad_text_unit = logit_scale * jnp.dot(own(grad_logits, 1).T, image_unit, precision=highest)
    own_text, own_image = own(text_unit, 0), own(image_unit, 0)
    grad_text = (
        grad_text_unit - own_text * jnp.sum(own_text * grad_text_unit, axis=1, keepdims=True)
    ) / own(text_len, 0)
    grad_image = (
        (
            grad_image_unit
            - own_image * jnp.sum(own_image * grad_image_unit, axis=1, keepdims=True)
        )
        / own(image_len, 0)
    ).astype(bf16)

    grad_head = jnp.dot(grad_image, projection.T, preferred_element_type=f32)
    block = jnp.concatenate([grad_head * head_gain, head_centred, layer_scale[None]])
    block_mine = chip_gather(block)
    block_all = jnp.stack([block_mine, core_swap(block_mine)])
    scaled_all = block_all[:, :, :images]
    centred_all = block_all[:, :, images : 2 * images]
    scale_all = block_all[:, :, 2 * images :]
    mean_scaled = jnp.sum(scaled_all, axis=(0, 1, 3)) / channels
    mean_product = jnp.sum(scaled_all * centred_all, axis=(0, 1, 3)) / channels

    def to_pooled(scaled, centred):
        return (head_inverse[:, None] / positions) * (
            scaled - mean_scaled[:, None] - centred * mean_product[:, None]
        )

    grad_block = to_pooled(block[:images], head_centred)
    grad_mixed = (to_pooled(scaled_all, centred_all) * scale_all).astype(bf16)
    grad_mixed = jnp.where(core == 0, grad_mixed, grad_mixed[::-1])
    grad_mixed = grad_mixed.transpose(2, 1, 0, 3).reshape(images, channels)
    grad_act = lax.dot_general(
        grad_mixed, w_out, (((1,), (1,)), ((), ())), preferred_element_type=f32
    )
    grad_pre = (
        (grad_act[:, None, :] * gelu_slope(hidden_pre).reshape(images, positions, hidden))
        .reshape(rows, hidden)
        .astype(bf16)
    )
    gain_high, gain_low = split_two(gain_own)
    bias_high, bias_low = split_two(bias_own)
    through = jnp.dot(
        jnp.stack([gain_high, gain_low, bias_high, bias_low]).astype(bf16),
        weight_own,
        preferred_element_type=f32,
    )
    through_gain = through[0] + through[1]
    through_bias = through[2] + through[3] + b_in
    grad_float = grad_pre.astype(f32)
    row_sums = jnp.stack(
        [
            jnp.sum(grad_float * through_gain, axis=1),
            jnp.sum(grad_float * (hidden_pre - through_bias), axis=1),
        ]
    )
    grad_part = lax.dot_general(
        weight_own, grad_pre, (((1,), (1,)), ((), ())), preferred_element_type=f32
    ).astype(bf16)
    half = channels // 2

    def as_rows(sums):
        return jnp.pad(jnp.concatenate(split_two(sums)), ((0, 12), (0, 0))).astype(bf16)

    passed = core_swap(jnp.concatenate([grad_part[half:], as_rows(row_sums)]))
    passed_float = passed.astype(f32)
    pair = (grad_part[:half].astype(f32) + passed_float[:half]).astype(bf16)
    pair_sums = row_sums + passed_float[half : half + 2] + passed_float[half + 2 : half + 4]
    blocks = jnp.concatenate(
        [
            pair.reshape(chips, shard, rows),
            jnp.broadcast_to(as_rows(pair_sums), (chips, 16, rows)),
        ],
        axis=1,
    )
    total = jnp.sum(chip_exchange(blocks).astype(f32), axis=0)
    sum_first = total[shard] + total[shard + 2]
    sum_second = total[shard + 1] + total[shard + 3]
    gain_local = lax.dynamic_slice_in_dim(ln_gain, index * shard, shard, 0)
    normed_scaled = total[:shard].T * gain_local
    centred = (conv.astype(f32) - average[:, None]) * inverse[:, None]
    grad_conv = inverse[:, None] * (
        normed_scaled - sum_first[:, None] / channels - centred * sum_second[:, None] / channels
    )
    grad_field = grad_conv.reshape(images, side, side, shard)
    grad_input = grad_block[:, None, None, :] + depthwise(grad_field, dw_weight[::-1, ::-1])
    return (grad_input, grad_text)


def solution(mesh):
    return jax.shard_map(
        body,
        mesh=mesh,
        in_specs=(
            P("dp", None, None, "mp"),
            P(None, None, "mp"),
            P("mp"),
            P(),
            P(),
            P(None, "mp"),
            P("mp"),
            P("mp", None),
            P("mp"),
            P("mp"),
            P("mp"),
            P("mp"),
            P("mp", None),
            P("dp", None),
            P("dp"),
        ),
        out_specs=(P("dp", None, None, "mp"), P("dp", None)),
        check_vma=False,
    )
```

```python
import jax
import jax.numpy as jnp
from jax import lax
from jax.sharding import PartitionSpec as P

eps = 1e-06
logit_scale = 20.0
loss_scale = 512.0
root_half = 0.7071067811865476
inv_root_two_pi = 0.3989422804014327
f32 = jnp.float32
bf16 = jnp.bfloat16
highest = lax.Precision.HIGHEST


def core_swap(array):
    length = lax.axis_size("mp")
    return lax.ppermute(array, "mp", [(i, i ^ 1) for i in range(length)])


def x_swap(array):
    dp_len, mp_len = lax.axis_size("dp"), lax.axis_size("mp")
    pairs = []
    for d in range(dp_len):
        for m in range(mp_len):
            there = (d + dp_len // 2) % dp_len * mp_len + (m + mp_len // 2) % mp_len
            pairs.append((d * mp_len + m, there))
    return lax.ppermute(array, ("dp", "mp"), pairs)


def y_shift(array, by):
    length = lax.axis_size("mp")
    half = length // 2
    return lax.ppermute(
        array, "mp", [(i, i // half * half + (i % half + 2 * by) % half) for i in range(length)]
    )


def chip_exchange(array):
    length = lax.axis_size("mp")
    groups = [[i for i in range(core, length, 2)] for core in range(2)]
    return lax.all_to_all(array, "mp", 0, 0, axis_index_groups=groups)


def chip_gather(array):
    count = lax.axis_size("mp") // 2
    return chip_exchange(jnp.broadcast_to(array, (count,) + array.shape))


def dp_gather(array):
    count = lax.axis_size("dp")
    return lax.all_to_all(jnp.broadcast_to(array, (count,) + array.shape), "dp", 0, 0)


def own_first(array, core):
    first, second = array[..., 0, :], array[..., 1, :]
    return jnp.where(core == 0, jnp.stack([first, second]), jnp.stack([second, first]))


def split_two(array):
    high = lax.reduce_precision(array, 8, 7)
    return high, array - high


def depthwise(source, kernel):
    extent = source.shape[1]
    reach = kernel.shape[0] // 2
    padded = jnp.pad(source, ((0, 0), (reach, reach), (reach, reach), (0, 0)))
    summed = jnp.zeros(source.shape, f32)
    for offset_row in range(kernel.shape[0]):
        for offset_col in range(kernel.shape[1]):
            summed = (
                summed
                + padded[:, offset_row : offset_row + extent, offset_col : offset_col + extent, :]
                * kernel[offset_row, offset_col]
            )
    return summed


def gelu_value(pre_act):
    return 0.5 * pre_act * (1.0 + lax.erf(pre_act * root_half))


def gelu_slope(pre_act):
    return (
        0.5 * (1.0 + lax.erf(pre_act * root_half))
        + pre_act * jnp.exp(-0.5 * pre_act * pre_act) * inv_root_two_pi
    )


def body(
    x_in,
    dw_weight,
    dw_bias,
    ln_gain,
    ln_bias,
    w_in,
    b_in,
    w_out,
    b_out,
    layer_scale,
    head_gain,
    head_bias,
    projection,
    text_emb,
    labels,
):
    images, side = x_in.shape[0], x_in.shape[1]
    shard = x_in.shape[3]
    channels, hidden = w_in.shape
    positions = side * side
    rows = images * positions
    index = lax.axis_index("mp")
    core = index % 2
    chips = lax.axis_size("mp") // 2
    width = text_emb.shape[1]
    pairs = text_emb.shape[0]
    batch = pairs * lax.axis_size("dp")
    home = lax.axis_index("dp")

    near = jnp.stack([projection, x_swap(projection)])
    below, above = y_shift(near, 1), y_shift(near, -1)
    far_first, far_second = y_shift(above[0], -1), y_shift(below[1], 1)
    project = jnp.concatenate([near, below, above, far_first[None], far_second[None]])
    project = project.reshape(channels // 2, width)
    chip = index // 2
    x_half, y_place = chip // 4, chip % 4
    order = [(x_half ^ dx) * 4 + (y_place + dy) % 4 for dy in (0, 3, 1, 2) for dx in (0, 1)]

    def place_of(c):
        away = (c % 4 - y_place) % 4
        slot = jnp.where(away == 0, 0, jnp.where(away == 3, 1, jnp.where(away == 1, 2, 3)))
        return slot * 2 + ((c // 4) ^ x_half)

    source = x_in.astype(f32)
    conv = (depthwise(source, dw_weight) + dw_bias).astype(bf16).reshape(rows, shard)
    conv_mine = chip_gather(conv.T)
    conv_other = core_swap(conv_mine)
    whole = jnp.stack([conv_mine, conv_other]).reshape(channels, rows).astype(f32)
    average = jnp.sum(whole, axis=0) / channels
    inverse = lax.rsqrt(jnp.sum(whole * whole, axis=0) / channels - average * average + eps)
    gain_own = own_first(ln_gain.reshape(chips, 2, shard), core).reshape(channels)
    bias_own = own_first(ln_bias.reshape(chips, 2, shard), core).reshape(channels)
    weight_pairs = w_in.reshape(chips, 2, shard, hidden)
    weight_own = jnp.where(
        core == 0,
        jnp.swapaxes(weight_pairs, 0, 1),
        jnp.swapaxes(weight_pairs[:, ::-1], 0, 1),
    ).reshape(channels, hidden)
    normed = (
        ((whole - average) * inverse) * gain_own[:, None] + bias_own[:, None]
    ).astype(bf16)
    hidden_pre = (
        lax.dot_general(normed, weight_own, (((0,), (0,)), ((), ())), preferred_element_type=f32)
        + b_in
    )
    activation = gelu_value(hidden_pre).reshape(images, positions, hidden)
    act_mean = jnp.mean(activation, axis=1)

    high, low = split_two(act_mean)
    mixed = jnp.dot(
        jnp.concatenate([high, low]).astype(bf16), w_out, preferred_element_type=f32
    )
    mixed = own_first((mixed[:images] + mixed[images:]).reshape(images, chips, 2, shard), core)
    mixed = mixed[0] + core_swap(mixed[1])
    input_mean = jnp.mean(source.reshape(images, positions, shard), axis=1)
    vectors = jnp.stack([layer_scale, b_out, head_gain, head_bias])
    got = chip_gather(
        jnp.concatenate([mixed.reshape(images * chips, shard), input_mean, vectors])
    )
    mixed_mean = jnp.sum(got[:, : images * chips], axis=0).reshape(images, chips, shard)
    vectors = got[:, images * chips :]
    head_rows = jnp.concatenate([jnp.swapaxes(mixed_mean, 0, 1), vectors], axis=1)
    head_rows = jnp.stack([lax.dynamic_index_in_dim(head_rows, c, 0, False) for c in order])
    head_rows = jnp.swapaxes(head_rows, 0, 1).reshape(3 * images, channels // 2)
    mixed_mean, input_mean = head_rows[:images], head_rows[images : 2 * images]
    scale_half, bout_half, gain_half, hbias_half = (
        head_rows[2 * images + i][None] for i in range(4)
    )
    pooled = input_mean + scale_half * (mixed_mean + bout_half)

    stats = jnp.concatenate([jnp.sum(pooled, axis=1), jnp.sum(pooled * pooled, axis=1)])
    stacked = jnp.concatenate([pooled * gain_half, gain_half, hbias_half])
    terms = stacked.shape[0]
    high, rest = split_two(stacked)
    middle, low = split_two(rest)
    product = jnp.dot(
        jnp.concatenate([high, middle, low]).astype(bf16), project, preferred_element_type=f32
    )
    sums = jnp.concatenate(
        [
            product[:terms] + (product[terms : 2 * terms] + product[2 * terms :]),
            jnp.pad(stats[None, :], ((0, 1), (0, width - 2 * images))),
        ]
    )
    sums = sums + core_swap(sums)
    head_mean = sums[images + 2, :images] / channels
    head_inverse = lax.rsqrt(
        sums[images + 2, images : 2 * images] / channels - head_mean * head_mean + eps
    )
    emb = (
        head_inverse[:, None] * (sums[:images] - head_mean[:, None] * sums[images])
        + sums[images + 1]
    )
    head_own = jnp.concatenate([pooled, gain_half, scale_half])
    head_both = jnp.stack([head_own, core_swap(head_own)])
    centred_both = (head_both[:, :images] - head_mean[:, None]) * head_inverse[:, None]

    tail = jnp.pad(labels.astype(f32)[:, None], ((images, 0), (0, 127)))
    pair_all = dp_gather(jnp.concatenate([jnp.concatenate([emb, text_emb]), tail], axis=1))
    emb_all = pair_all[:, :images, :width].reshape(batch, width)
    text_raw = pair_all[:, images:, :width].reshape(batch, width)
    labels_all = pair_all[:, images:, width].reshape(batch)
    image_len = jnp.sqrt(jnp.sum(emb_all * emb_all, axis=1, keepdims=True) + eps)
    image_unit = emb_all / image_len
    text_len = jnp.sqrt(jnp.sum(text_raw * text_raw, axis=1, keepdims=True) + eps)
    text_unit = text_raw / text_len
    logits = logit_scale * jnp.dot(image_unit, text_unit.T, precision=highest)
    weights = jnp.exp(logits)
    matched = (labels_all[:, None] == jnp.arange(batch, dtype=f32)[None, :]).astype(f32)
    grad_logits = loss_scale * (
        0.5
        * (
            weights / jnp.sum(weights, axis=1, keepdims=True)
            + weights / jnp.sum(weights, axis=0, keepdims=True)
        )
        - matched
    )

    def own(array, axis):
        return lax.dynamic_slice_in_dim(array, home * pairs, pairs, axis)

    grad_image_unit = logit_scale * jnp.dot(own(grad_logits, 0), text_unit, precision=highest)
    grad_text_unit = logit_scale * jnp.dot(own(grad_logits, 1).T, image_unit, precision=highest)
    own_text, own_image = own(text_unit, 0), own(image_unit, 0)
    grad_text = (
        grad_text_unit - own_text * jnp.sum(own_text * grad_text_unit, axis=1, keepdims=True)
    ) / own(text_len, 0)
    grad_image = (
        (
            grad_image_unit
            - own_image * jnp.sum(own_image * grad_image_unit, axis=1, keepdims=True)
        )
        / own(image_len, 0)
    ).astype(bf16)

    grad_head = lax.dot_general(
        grad_image, project, (((1,), (1,)), ((), ())), preferred_element_type=f32
    )
    scaled_both = jnp.stack([grad_head, core_swap(grad_head)]) * head_both[:, images : images + 1]
    mean_scaled = jnp.sum(scaled_both, axis=(0, 2)) / channels
    mean_product = jnp.sum(scaled_both * centred_both, axis=(0, 2)) / channels
    grad_blocks = (head_inverse[:, None] / positions) * (
        scaled_both - mean_scaled[:, None] - centred_both * mean_product[:, None]
    )
    grad_block = grad_blocks[0, :, :shard]
    grad_mixed = (grad_blocks * head_both[:, images + 1 :]).astype(bf16)
    grad_mixed = jnp.where(core == 0, grad_mixed, grad_mixed[::-1])
    grad_mixed = grad_mixed.reshape(2, images, chips, shard).transpose(2, 1, 0, 3)
    grad_mixed = jnp.stack(
        [lax.dynamic_index_in_dim(grad_mixed, place_of(c), 0, False) for c in range(chips)], axis=1
    ).reshape(images, channels)
    grad_act = lax.dot_general(
        grad_mixed, w_out, (((1,), (1,)), ((), ())), preferred_element_type=f32
    )
    grad_pre = (
        (grad_act[:, None, :] * gelu_slope(hidden_pre).reshape(images, positions, hidden))
        .reshape(rows, hidden)
        .astype(bf16)
    )
    gain_high, gain_low = split_two(gain_own)
    bias_high, bias_low = split_two(bias_own)
    through = jnp.dot(
        jnp.stack([gain_high, gain_low, bias_high, bias_low]).astype(bf16),
        weight_own,
        preferred_element_type=f32,
    )
    through_gain = through[0] + through[1]
    through_bias = through[2] + through[3] + b_in
    grad_float = grad_pre.astype(f32)
    row_sums = jnp.stack(
        [
            jnp.sum(grad_float * through_gain, axis=1),
            jnp.sum(grad_float * (hidden_pre - through_bias), axis=1),
        ]
    )
    grad_part = lax.dot_general(
        weight_own, grad_pre, (((1,), (1,)), ((), ())), preferred_element_type=f32
    ).astype(bf16)
    half = channels // 2

    def as_rows(sums):
        return jnp.pad(jnp.concatenate(split_two(sums)), ((0, 12), (0, 0))).astype(bf16)

    passed = core_swap(jnp.concatenate([grad_part[half:], as_rows(row_sums)]))
    passed_float = passed.astype(f32)
    pair = (grad_part[:half].astype(f32) + passed_float[:half]).astype(bf16)
    pair_sums = row_sums + passed_float[half : half + 2] + passed_float[half + 2 : half + 4]
    blocks = jnp.concatenate(
        [
            pair.reshape(chips, shard, rows),
            jnp.broadcast_to(as_rows(pair_sums), (chips, 16, rows)),
        ],
        axis=1,
    )
    total = jnp.sum(chip_exchange(blocks).astype(f32), axis=0)
    sum_first = total[shard] + total[shard + 2]
    sum_second = total[shard + 1] + total[shard + 3]
    gain_local = lax.dynamic_slice_in_dim(ln_gain, index * shard, shard, 0)
    normed_scaled = total[:shard].T * gain_local
    centred = (conv.astype(f32) - average[:, None]) * inverse[:, None]
    grad_conv = inverse[:, None] * (
        normed_scaled - sum_first[:, None] / channels - centred * sum_second[:, None] / channels
    )
    grad_field = grad_conv.reshape(images, side, side, shard)
    grad_input = grad_block[:, None, None, :] + depthwise(grad_field, dw_weight[::-1, ::-1])
    return (grad_input, grad_text)


def solution(mesh):
    return jax.shard_map(
        body,
        mesh=mesh,
        in_specs=(
            P("dp", None, None, "mp"),
            P(None, None, "mp"),
            P("mp"),
            P(),
            P(),
            P(None, "mp"),
            P("mp"),
            P("mp", None),
            P("mp"),
            P("mp"),
            P("mp"),
            P("mp"),
            P("mp", None),
            P("dp", None),
            P("dp"),
        ),
        out_specs=(P("dp", None, None, "mp"), P("dp", None)),
        check_vma=False,
    )
```

```python
import functools
import jax
import jax.numpy as jnp
from jax import lax
from jax.experimental import pallas as pl
from jax.experimental.pallas import tpu as pltpu
from jax.sharding import PartitionSpec as P

eps = 1e-06
logit_scale = 20.0
loss_scale = 512.0
root_half = 0.7071067811865476
inv_root_two_pi = 0.3989422804014327
f32 = jnp.float32
bf16 = jnp.bfloat16
highest = lax.Precision.HIGHEST
MIB = 1 << 20
CHIPS = 8
HALVES = 2
BLOCKS = 16


def core_swap(array):
    return lax.ppermute(array, "mp", [(i, i ^ 1) for i in range(BLOCKS)])


def x_swap(array):
    return lax.ppermute(array, "mp", [(i, i ^ CHIPS) for i in range(BLOCKS)])


def chip_exchange(array):
    groups = [[i for i in range(core, BLOCKS, 2)] for core in range(2)]
    return lax.all_to_all(array, "mp", 0, 0, axis_index_groups=groups)


def half_gather(array):
    groups = [[half * CHIPS + i for i in range(CHIPS)] for half in range(HALVES)]
    return lax.all_gather(array, "mp", axis_index_groups=groups, tiled=True)


def run(kernel, outs, *operands, scratch=(), limit=24, flops=0):
    specs = [
        pl.BlockSpec(memory_space=pltpu.SMEM if a.dtype == jnp.int32 else pltpu.VMEM)
        for a in operands
    ]
    size = sum(a.size * a.dtype.itemsize for a in operands)
    return pl.pallas_call(
        kernel,
        out_shape=outs,
        in_specs=specs,
        out_specs=[pl.BlockSpec(memory_space=pltpu.VMEM) for _ in outs],
        scratch_shapes=list(scratch),
        compiler_params=pltpu.CompilerParams(vmem_limit_bytes=limit * MIB),
        cost_estimate=pl.CostEstimate(flops=flops, bytes_accessed=size, transcendentals=0),
    )(*operands)


def shape(*dims, dtype=f32):
    return jax.ShapeDtypeStruct(dims, dtype)


def iota(dims, axis):
    return lax.broadcasted_iota(jnp.int32, dims, axis)


def to_terms(array):
    high = array.astype(bf16).astype(f32)
    return high, array - high


def taps(x, w_ref, flip):
    side, _, shard = x.shape
    size = w_ref.shape[0]
    reach = size // 2
    column = iota((side, side, shard), 1)
    acc = [jnp.zeros((side, shard), f32) for _ in range(side)]
    for b in range(size):
        by = b - reach
        if by:
            moved = jnp.where(
                (column + by >= 0) & (column + by < side), pltpu.roll(x, (-by) % side, 1), 0.0
            )
        else:
            moved = x
        for a in range(size):
            wa, wb = (size - 1 - a, size - 1 - b) if flip else (a, b)
            weight = w_ref[wa, wb : wb + 1, :]
            for p in range(side):
                if 0 <= p + a - reach < side:
                    acc[p] = acc[p] + moved[p + a - reach] * weight
    return acc


def conv_kernel(x_ref, w_ref, b_ref, copies_ref, conv_ref, mean_ref, rows_ref):
    images, side = x_ref.shape[:2]
    positions = side * side

    def image(n, carry):
        x = x_ref[n].astype(f32)
        total = jnp.sum(jnp.sum(x, axis=0), axis=0, keepdims=True)
        mean_ref[pl.ds(n, 1), :] = total / positions
        for p, row in enumerate(taps(x, w_ref, False)):
            rows_ref[pl.ds(pl.multiple_of(n * positions + p * side, side), side), :] = row
        return carry

    lax.fori_loop(0, images, image, 0)
    turned = (rows_ref[...] + b_ref[...]).T.astype(bf16)
    conv_ref[...] = turned
    for j in range(CHIPS):
        copies_ref[j] = turned


def forward_kernel(
    place_ref,
    mine_ref,
    other_ref,
    own_ref,
    vec_ref,
    w_ref,
    b_ref,
    wout_ref,
    slope_ref,
    hidden_ref,
    through_ref,
    stat_ref,
    mixed_ref,
    turned_ref,
    normed_ref,
):
    shard, rows = mine_ref.shape[1:]
    channels, hidden = w_ref.shape
    images = mixed_ref.shape[1]
    positions = rows // images
    core = place_ref[0]
    first = jnp.zeros((1, rows), f32)
    second = jnp.zeros((1, rows), f32)
    for ref in (mine_ref, other_ref):
        for j in range(CHIPS):
            value = ref[j].astype(f32)
            first = first + jnp.sum(value, axis=0, keepdims=True)
            second = second + jnp.sum(value * value, axis=0, keepdims=True)
    average = first / channels
    inverse = lax.rsqrt(second / channels - average * average + eps)
    stat_ref[0:1, :] = average
    stat_ref[1:2, :] = inverse
    own = own_ref[...].T
    for h, ref in enumerate((mine_ref, other_ref)):
        for j in range(CHIPS):
            k = h * CHIPS + j
            value = (ref[j].astype(f32) - average) * inverse
            value = value * own[:, k : k + 1] + own[:, BLOCKS + k : BLOCKS + k + 1]
            start = (2 * j + (core if h == 0 else 1 - core)) * shard
            turned_ref[pl.ds(pl.multiple_of(start, 64), shard), :] = value.astype(bf16)
    step = 256
    for c in range(channels // step):
        normed_ref[0:rows, c * step : (c + 1) * step] = turned_ref[c * step : (c + 1) * step, :].T
    normed_ref[rows : rows + 16, :] = vec_ref[...].astype(bf16)
    total = [None] * images
    for t in range(hidden // step):
        at = slice(t * step, (t + 1) * step)
        product = jnp.dot(normed_ref[...], w_ref[:, at], preferred_element_type=f32)
        through_ref[:, at] = product[rows:]
        pre = product[:rows] + b_ref[:, at]
        hidden_ref[:, at] = pre
        gate = 0.5 + 0.5 * lax.erf(pre * root_half)
        slope_ref[:, at] = gate + pre * jnp.exp(-0.5 * pre * pre) * inv_root_two_pi
        active = pre * gate
        sums = [
            jnp.sum(active[n * positions : (n + 1) * positions], axis=0, keepdims=True) / positions
            for n in range(images)
        ]
        sums = jnp.concatenate(sums + [jnp.zeros((8 - images, step), f32)], axis=0)
        high, low = to_terms(sums)
        part = jnp.dot(
            jnp.concatenate([high, low], axis=0).astype(bf16),
            wout_ref[at, :],
            preferred_element_type=f32,
        )
        part = part[:8] + part[8:]
        mixed = part if t == 0 else mixed + part
    for k in range(BLOCKS):
        mixed_ref[k] = mixed[:images, k * shard : (k + 1) * shard]


def payload_kernel(place_ref, mine_ref, other_ref, out_ref):
    core = place_ref[0]
    for half in range(HALVES):
        for b in range(CHIPS):
            value = mine_ref[half * CHIPS + b] + other_ref[half * CHIPS + b]
            for j in range(4):
                out_ref[half * 4 + j, b] = value
    for i in range(2):
        for j in range(CHIPS):
            out_ref[j, CHIPS + 2 * core + i] = mine_ref[BLOCKS + i]
            out_ref[j, CHIPS + 2 * (1 - core) + i] = other_ref[BLOCKS + i]


def head_kernel(place_ref, got_ref, project_ref, out_ref, head_ref):
    images, shard = got_ref.shape[2:]
    width = project_ref.shape[1]
    half = place_ref[1]
    product = jnp.zeros((24, width), f32)
    first = jnp.zeros((8, 1), f32)
    second = jnp.zeros((8, 1), f32)
    row = iota((8, shard), 0)
    for k in range(CHIPS):
        source = half * 4 + k // 2
        mixed = got_ref[0, k]
        for j in range(1, CHIPS):
            mixed = mixed + got_ref[j, k]
        vectors = got_ref[source, CHIPS + 2 * (k % 2) + 1]
        pooled = got_ref[source, CHIPS + 2 * (k % 2)] + vectors[0:1] * (mixed + vectors[1:2])
        head_ref[k, 0:images, :] = pooled
        head_ref[k, images:, :] = vectors
        value = head_ref[k]
        first = first + jnp.sum(value, axis=1, keepdims=True)
        second = second + jnp.sum(value * value, axis=1, keepdims=True)
        value = jnp.where(row < images, value * vectors[2:3], value)
        high, rest = to_terms(value)
        middle, low = to_terms(rest)
        product = product + jnp.dot(
            jnp.concatenate([high, middle, low], axis=0).astype(bf16),
            project_ref[k * shard : (k + 1) * shard, :],
            preferred_element_type=f32,
        )
    out_ref[:, :width] = product[:8] + (product[8:16] + product[16:])
    lane = iota((8, 128), 1)
    out_ref[:, width:] = jnp.where(lane == 0, first, jnp.where(lane == 1, second, 0.0))


def embed_kernel(channels, mine_ref, other_ref, text_ref, tail_ref, out_ref, stat_ref):
    width = text_ref.shape[1]
    sums = mine_ref[...] + other_ref[...]
    mean = sums[:, width : width + 1] / channels
    inverse = lax.rsqrt(sums[:, width + 1 : width + 2] / channels - mean * mean + eps)
    emb = inverse * (sums[:, :width] - mean * sums[6:7, :width]) + sums[7:8, :width]
    both = jnp.where(iota((8, width), 0) < 4, emb, text_ref[...])
    for d in range(out_ref.shape[0]):
        out_ref[d, :, :width] = both
        out_ref[d, :, width:] = tail_ref[...]
    stat_ref[0] = jnp.broadcast_to(mean, (8, 128))
    stat_ref[1] = jnp.broadcast_to(inverse, (8, 128))


def loss_kernel(place_ref, got_ref, project_ref, text_ref, back_ref, unit_ref, len_ref, both_ref):
    width = project_ref.shape[1]
    count = got_ref.shape[0] * 8
    shard = back_ref.shape[2]
    home = pl.ds(pl.multiple_of(place_ref[3] * 8, 8), 8)
    raw = got_ref[:, :, :width].reshape(count, width)
    length = jnp.sqrt(jnp.sum(raw * raw, axis=1, keepdims=True) + eps)
    unit = raw / length
    unit_ref[...] = unit
    len_ref[...] = jnp.broadcast_to(length, (count, 128))
    logits = logit_scale * lax.dot_general(
        unit, unit, (((1,), (1,)), ((), ())), precision=highest, preferred_element_type=f32
    )
    column = iota((count, count), 1)
    valid = (iota((count, count), 0) % 8 < 4) & (column % 8 >= 4)
    weights = jnp.where(valid, jnp.exp(jnp.where(valid, logits, 0.0)), 0.0)
    row_total = jnp.sum(weights, axis=1, keepdims=True)
    col_total = jnp.sum(weights, axis=0, keepdims=True)
    target = got_ref[:, :, width:].reshape(count, 128)[:, 0:1]
    matched = jnp.where(target == column.astype(f32), 1.0, 0.0)
    grads = loss_scale * (0.5 * (weights / row_total + weights / col_total) - matched)
    grads = jnp.where(valid, grads, 0.0)
    both_ref[...] = grads + grads.T
    grad_unit = logit_scale * jnp.dot(
        both_ref[home, :], unit, precision=highest, preferred_element_type=f32
    )
    own = unit_ref[home, :]
    grad = (grad_unit - own * jnp.sum(own * grad_unit, axis=1, keepdims=True)) / len_ref[home, 0:1]
    text_ref[...] = grad[4:]
    back = lax.dot_general(
        grad.astype(bf16),
        project_ref[...],
        (((1,), (1,)), ((), ())),
        preferred_element_type=f32,
    )
    for k in range(CHIPS):
        back_ref[k] = back[:4, k * shard : (k + 1) * shard]


def backward_kernel(
    place_ref,
    gh_mine_ref,
    gh_other_ref,
    head_mine_ref,
    head_other_ref,
    head_stat_ref,
    wout_ref,
    slope_ref,
    hidden_ref,
    w_ref,
    through_ref,
    b_ref,
    other_ref,
    turned_ref,
    sums_ref,
    block_ref,
    mixed_ref,
    pre_ref,
):
    images, shard = gh_mine_ref.shape[1:]
    rows, hidden = slope_ref.shape
    channels = w_ref.shape[0]
    positions = rows // images
    core, half, spot = place_ref[0], place_ref[1], place_ref[2]
    mean = head_stat_ref[0][:images, 0:1]
    inverse = head_stat_ref[1][:images, 0:1]
    first = jnp.zeros((images, 1), f32)
    second = jnp.zeros((images, 1), f32)

    def parts(gh_ref, head_ref, k):
        head = head_ref[k]
        return gh_ref[k] * head[6:7], (head[:images] - mean) * inverse, head[4:5]

    for refs in ((gh_mine_ref, head_mine_ref), (gh_other_ref, head_other_ref)):
        for k in range(CHIPS):
            scaled, centred, _ = parts(*refs, k)
            first = first + jnp.sum(scaled, axis=1, keepdims=True)
            second = second + jnp.sum(scaled * centred, axis=1, keepdims=True)
    first = first / channels
    second = second / channels

    def block(gh_ref, head_ref, k):
        scaled, centred, scale = parts(gh_ref, head_ref, k)
        grad = (inverse / positions) * (scaled - first - centred * second)
        return grad, grad * scale

    block_ref[...] = block(gh_mine_ref, head_mine_ref, spot)[0]
    mixed_ref[...] = jnp.zeros_like(mixed_ref)
    for k in range(CHIPS):
        mine = block(gh_mine_ref, head_mine_ref, k)[1]
        other = block(gh_other_ref, head_other_ref, k)[1]
        low, high = jnp.where(half == 0, mine, other), jnp.where(half == 0, other, mine)
        mixed_ref[0:images, k * shard : (k + 1) * shard] = low
        mixed_ref[0:images, (CHIPS + k) * shard : (CHIPS + k + 1) * shard] = high
    act = lax.dot_general(
        mixed_ref[...].astype(bf16),
        wout_ref[...],
        (((1,), (1,)), ((), ())),
        preferred_element_type=f32,
    )
    step = 256
    one = jnp.zeros((rows, 1), f32)
    two = jnp.zeros((rows, 1), f32)
    for t in range(hidden // step):
        at = slice(t * step, (t + 1) * step)
        for n in range(images):
            span = slice(n * positions, (n + 1) * positions)
            pre_ref[span, :] = (act[n : n + 1, at] * slope_ref[span, at]).astype(bf16).astype(f32)
        value = pre_ref[...]
        gain = through_ref[0:1, at] + through_ref[1:2, at]
        bias = through_ref[2:3, at] + through_ref[3:4, at] + b_ref[:, at]
        one = one + jnp.sum(value * gain, axis=1, keepdims=True)
        two = two + jnp.sum(value * (hidden_ref[:, at] - bias), axis=1, keepdims=True)
        turned_ref[at, :] = value.T.astype(bf16)
    lane = iota((rows, 128), 1)
    sums = jnp.where(lane == 0, one, jnp.where(lane == 1, two, 0.0)).T[:8]
    sums_ref[...] = sums
    high, low = to_terms(sums)
    other_ref[channels // 2 :, :] = jnp.concatenate([high, low], axis=0).astype(bf16)
    for j in range(CHIPS):
        start = pl.multiple_of((2 * j + 1 - core) * shard, 64)
        other_ref[j * shard : (j + 1) * shard, :] = jnp.dot(
            w_ref[pl.ds(start, shard), :], turned_ref[...], preferred_element_type=f32
        ).astype(bf16)


def mine_kernel(place_ref, w_ref, turned_ref, mine_ref):
    shard = w_ref.shape[0] // BLOCKS
    for j in range(CHIPS):
        start = pl.multiple_of((2 * j + place_ref[0]) * shard, 64)
        mine_ref[j * shard : (j + 1) * shard, :] = jnp.dot(
            w_ref[pl.ds(start, shard), :], turned_ref[...], preferred_element_type=f32
        ).astype(bf16)


def pair_kernel(mine_ref, got_ref, sums_ref, out_ref):
    half = mine_ref.shape[0]
    shard = half // CHIPS
    for j in range(CHIPS):
        span = slice(j * shard, (j + 1) * shard)
        out_ref[j, :shard, :] = (mine_ref[span, :].astype(f32) + got_ref[span, :].astype(f32)).astype(
            bf16
        )
    tail = got_ref[half:, :].astype(f32)
    high, low = to_terms(sums_ref[...] + (tail[:8] + tail[8:]))
    tail = jnp.concatenate([high, low], axis=0).astype(bf16)
    for j in range(CHIPS):
        out_ref[j, shard:, :] = tail


def final_kernel(
    channels, got_ref, conv_ref, stat_ref, gain_ref, w_ref, block_ref, out_ref, rows_ref
):
    shard = conv_ref.shape[0]
    images, side = out_ref.shape[:2]
    positions = side * side
    total = got_ref[0].astype(f32)
    for j in range(1, CHIPS):
        total = total + got_ref[j].astype(f32)
    first = (total[shard : shard + 1] + total[shard + 8 : shard + 9]) / channels
    second = (total[shard + 1 : shard + 2] + total[shard + 9 : shard + 10]) / channels
    average, inverse = stat_ref[0:1, :], stat_ref[1:2, :]
    centred = (conv_ref[...].astype(f32) - average) * inverse
    grad = inverse * (total[:shard] * gain_ref[...].T[:, 0:1] - first - centred * second)
    rows_ref[...] = grad.T

    def image(n, carry):
        span = pl.ds(pl.multiple_of(n * positions, positions), positions)
        x = rows_ref[span, :].reshape(side, side, shard)
        base = block_ref[pl.ds(n, 1), :]
        for p, row in enumerate(taps(x, w_ref, True)):
            out_ref[n, p] = row + base
        return carry

    lax.fori_loop(0, images, image, 0)


def body(
    x_in,
    dw_weight,
    dw_bias,
    ln_gain,
    ln_bias,
    w_in,
    b_in,
    w_out,
    b_out,
    layer_scale,
    head_gain,
    head_bias,
    projection,
    text_emb,
    labels,
):
    images, side, _, shard = x_in.shape
    channels, hidden = w_in.shape
    rows = images * side * side
    pairs, width = text_emb.shape
    shards = lax.axis_size("dp")
    index = lax.axis_index("mp")
    core = index % 2
    place = jnp.stack(
        [core, index // CHIPS, index % CHIPS, lax.axis_index("dp")]
    ).astype(jnp.int32)
    project = half_gather(projection)

    def own_first(vector):
        pair = vector.reshape(CHIPS, 2, shard)
        mine = jnp.where(core == 0, pair[:, 0], pair[:, 1])
        other = jnp.where(core == 0, pair[:, 1], pair[:, 0])
        return jnp.concatenate([mine, other])

    own = jnp.concatenate([own_first(ln_gain), own_first(ln_bias)])
    terms = []
    for vector in (ln_gain, ln_bias):
        high = lax.reduce_precision(vector, 8, 7)
        terms += [high, vector - high]
    vec = jnp.pad(jnp.stack(terms), ((0, 12), (0, 0)))
    gain_local = lax.dynamic_slice_in_dim(ln_gain, index * shard, shard, 0)
    gain_local = jnp.broadcast_to(gain_local[None, :], (8, shard))
    b_row = b_in[None, :]
    target = (labels // pairs) * 8 + 4 + labels % pairs
    tail = jnp.pad(target.astype(f32)[:, None], ((0, 8 - pairs), (0, 127)))
    text_low = jnp.pad(text_emb, ((8 - pairs, 0), (0, 0)))

    copies, conv, input_mean = run(
        conv_kernel,
        [
            shape(CHIPS, shard, rows, dtype=bf16),
            shape(shard, rows, dtype=bf16),
            shape(images, shard),
        ],
        x_in,
        dw_weight,
        dw_bias[None, :],
        scratch=[pltpu.VMEM((rows, shard), f32)],
        flops=2 * 49 * rows * shard,
    )
    conv_mine = chip_exchange(copies)
    conv_other = core_swap(conv_mine)
    slope, hidden_pre, through, row_stat, mixed = run(
        forward_kernel,
        [
            shape(rows, hidden),
            shape(rows, hidden),
            shape(16, hidden),
            shape(8, rows),
            shape(BLOCKS, images, shard),
        ],
        place,
        conv_mine,
        conv_other,
        own,
        vec,
        w_in,
        b_row,
        w_out,
        scratch=[pltpu.VMEM((channels, rows), bf16), pltpu.VMEM((rows + 16, channels), bf16)],
        limit=32,
        flops=2 * rows * channels * hidden,
    )
    vectors = jnp.stack([layer_scale, b_out, head_gain, head_bias])
    partial = jnp.concatenate([mixed, input_mean[None], vectors[None]])
    (payload,) = run(
        payload_kernel,
        [shape(CHIPS, CHIPS + 4, images, shard)],
        place,
        partial,
        core_swap(partial),
    )
    sums, head = run(
        head_kernel,
        [shape(8, width + 128), shape(CHIPS, 8, shard)],
        place,
        chip_exchange(payload),
        project,
    )
    pair_block, head_stat = run(
        functools.partial(embed_kernel, channels),
        [shape(shards, 8, width + 128), shape(2, 8, 128)],
        sums,
        x_swap(sums),
        text_low,
        tail,
    )
    head_other = x_swap(head)
    grad_text, back = run(
        loss_kernel,
        [shape(pairs, width), shape(CHIPS, images, shard)],
        place,
        lax.all_to_all(pair_block, "dp", 0, 0),
        project,
        scratch=[
            pltpu.VMEM((shards * 8, width), f32),
            pltpu.VMEM((shards * 8, 128), f32),
            pltpu.VMEM((shards * 8, shards * 8), f32),
        ],
    )
    other, turned, row_sums, grad_block = run(
        backward_kernel,
        [
            shape(channels // 2 + 16, rows, dtype=bf16),
            shape(hidden, rows, dtype=bf16),
            shape(8, rows),
            shape(images, shard),
        ],
        place,
        back,
        x_swap(back),
        head,
        head_other,
        head_stat,
        w_out,
        slope,
        hidden_pre,
        w_in,
        through,
        b_row,
        scratch=[pltpu.VMEM((8, channels), f32), pltpu.VMEM((rows, 256), f32)],
        limit=32,
        flops=rows * channels * hidden,
    )
    passed = core_swap(other)
    (mine,) = run(
        mine_kernel,
        [shape(channels // 2, rows, dtype=bf16)],
        place,
        w_in,
        turned,
        flops=rows * channels * hidden,
    )
    (blocks,) = run(
        pair_kernel, [shape(CHIPS, shard + 16, rows, dtype=bf16)], mine, passed, row_sums
    )
    (grad_input,) = run(
        functools.partial(final_kernel, channels),
        [shape(images, side, side, shard)],
        chip_exchange(blocks),
        conv,
        row_stat,
        gain_local,
        dw_weight,
        grad_block,
        scratch=[pltpu.VMEM((rows, shard), f32)],
        flops=2 * 49 * rows * shard,
    )
    return (grad_input, grad_text)


def solution(mesh):
    return jax.shard_map(
        body,
        mesh=mesh,
        in_specs=(
            P("dp", None, None, "mp"),
            P(None, None, "mp"),
            P("mp"),
            P(),
            P(),
            P(None, "mp"),
            P("mp"),
            P("mp", None),
            P("mp"),
            P("mp"),
            P("mp"),
            P("mp"),
            P("mp", None),
            P("dp", None),
            P("dp"),
        ),
        out_specs=(P("dp", None, None, "mp"), P("dp", None)),
        check_vma=False,
    )
```

```python
import jax
import jax.numpy as jnp
from jax import lax
from jax.experimental import pallas as pl
from jax.experimental.pallas import tpu as pltpu
from jax.sharding import PartitionSpec as P

eps = 1e-06
logit_scale = 20.0
loss_scale = 512.0
root_half = 0.7071067811865476
inv_root_two_pi = 0.3989422804014327
f32 = jnp.float32
bf16 = jnp.bfloat16
highest = lax.Precision.HIGHEST
MIB = 1 << 20
CHIPS = 8
BLOCKS = 16
SHARD = 192


def core_swap(array):
    return lax.ppermute(array, "mp", [(i, i ^ 1) for i in range(BLOCKS)])


def chip_exchange(array):
    groups = [[i for i in range(core, BLOCKS, 2)] for core in range(2)]
    return lax.all_to_all(array, "mp", 0, 0, axis_index_groups=groups)


def shard_exchange(array):
    return lax.all_to_all(array, "mp", 0, 0)


def run(kernel, outs, *operands, scratch=(), limit=24, flops=0):
    specs = [
        pl.BlockSpec(memory_space=pltpu.SMEM if a.dtype == jnp.int32 else pltpu.VMEM)
        for a in operands
    ]
    size = sum(a.size * a.dtype.itemsize for a in operands)
    return pl.pallas_call(
        kernel,
        out_shape=outs,
        in_specs=specs,
        out_specs=[pl.BlockSpec(memory_space=pltpu.VMEM) for _ in outs],
        scratch_shapes=list(scratch),
        compiler_params=pltpu.CompilerParams(vmem_limit_bytes=limit * MIB),
        cost_estimate=pl.CostEstimate(flops=flops, bytes_accessed=size, transcendentals=0),
    )(*operands)


def shape(*dims, dtype=f32):
    return jax.ShapeDtypeStruct(dims, dtype)


def iota(dims, axis):
    return lax.broadcasted_iota(jnp.int32, dims, axis)


def to_terms(array):
    high = array.astype(bf16).astype(f32)
    return high, array - high


def taps(x, w_ref, flip):
    side, _, shard = x.shape
    size = w_ref.shape[0]
    reach = size // 2
    column = iota((side, side, shard), 1)
    acc = [jnp.zeros((side, shard), f32) for _ in range(side)]
    for b in range(size):
        by = b - reach
        if by:
            moved = jnp.where(
                (column + by >= 0) & (column + by < side), pltpu.roll(x, (-by) % side, 1), 0.0
            )
        else:
            moved = x
        for a in range(size):
            wa, wb = (size - 1 - a, size - 1 - b) if flip else (a, b)
            weight = w_ref[wa, wb : wb + 1, :]
            for p in range(side):
                if 0 <= p + a - reach < side:
                    acc[p] = acc[p] + moved[p + a - reach] * weight
    return acc


def conv_kernel(x_ref, w_ref, b_ref, copies_ref, conv_ref, mean_ref, rows_ref):
    images, side = x_ref.shape[:2]
    positions = side * side

    def image(n, carry):
        x = x_ref[n].astype(f32)
        total = jnp.sum(jnp.sum(x, axis=0), axis=0, keepdims=True)
        mean_ref[pl.ds(n, 1), :] = total / positions
        for p, row in enumerate(taps(x, w_ref, False)):
            rows_ref[pl.ds(pl.multiple_of(n * positions + p * side, side), side), :] = row
        return carry

    lax.fori_loop(0, images, image, 0)
    turned = (rows_ref[...] + b_ref[...]).T.astype(bf16)
    conv_ref[...] = turned
    for j in range(CHIPS):
        copies_ref[j] = turned


def forward_kernel(
    mine_ref,
    other_ref,
    gain_ref,
    bias_ref,
    w_ref,
    b_ref,
    wout_ref,
    slope_ref,
    hidden_ref,
    through_ref,
    stat_ref,
    mixed_ref,
    turned_ref,
    normed_ref,
    own_ref,
    vec_ref,
):
    shard, rows = mine_ref.shape[1:]
    channels, hidden = w_ref.shape
    images = mixed_ref.shape[1]
    positions = rows // images
    core = lax.axis_index("mp") % 2
    vec_ref[...] = jnp.zeros_like(vec_ref)
    for i, ref in enumerate((gain_ref, bias_ref)):
        vec_ref[i : i + 1, :] = ref[...]
        for j in range(CHIPS):
            low = ref[:, 2 * j * shard : (2 * j + 1) * shard]
            high = ref[:, (2 * j + 1) * shard : (2 * j + 2) * shard]
            at = i * BLOCKS + j
            own_ref[at : at + 1, :] = jnp.where(core == 0, low, high)
            own_ref[at + CHIPS : at + CHIPS + 1, :] = jnp.where(core == 0, high, low)
    first = jnp.zeros((1, rows), f32)
    second = jnp.zeros((1, rows), f32)
    for ref in (mine_ref, other_ref):
        for j in range(CHIPS):
            value = ref[j].astype(f32)
            first = first + jnp.sum(value, axis=0, keepdims=True)
            second = second + jnp.sum(value * value, axis=0, keepdims=True)
    average = first / channels
    inverse = lax.rsqrt(second / channels - average * average + eps)
    stat_ref[0:1, :] = average
    stat_ref[1:2, :] = inverse
    own = own_ref[...].T
    for h, ref in enumerate((mine_ref, other_ref)):
        for j in range(CHIPS):
            k = h * CHIPS + j
            value = (ref[j].astype(f32) - average) * inverse
            value = value * own[:, k : k + 1] + own[:, BLOCKS + k : BLOCKS + k + 1]
            start = (2 * j + (core if h == 0 else 1 - core)) * shard
            turned_ref[pl.ds(pl.multiple_of(start, 64), shard), :] = value.astype(bf16)
    step = 256
    for c in range(channels // step):
        normed_ref[0:rows, c * step : (c + 1) * step] = turned_ref[c * step : (c + 1) * step, :].T
    normed_ref[rows : rows + 16, :] = jnp.concatenate(to_terms(vec_ref[...]), axis=0).astype(bf16)
    b_row = b_ref[...][None, :]
    for t in range(hidden // step):
        at = slice(t * step, (t + 1) * step)
        product = jnp.dot(normed_ref[...], w_ref[:, at], preferred_element_type=f32)
        through_ref[:, at] = product[rows:]
        pre = product[:rows] + b_row[:, at]
        hidden_ref[:, at] = pre
        gate = 0.5 + 0.5 * lax.erf(pre * root_half)
        slope_ref[:, at] = gate + pre * jnp.exp(-0.5 * pre * pre) * inv_root_two_pi
        active = pre * gate
        sums = [
            jnp.sum(active[n * positions : (n + 1) * positions], axis=0, keepdims=True) / positions
            for n in range(images)
        ]
        sums = jnp.concatenate(sums + [jnp.zeros((8 - images, step), f32)], axis=0)
        high, low = to_terms(sums)
        part = jnp.dot(
            jnp.concatenate([high, low], axis=0).astype(bf16),
            wout_ref[at, :],
            preferred_element_type=f32,
        )
        part = part[:8] + part[8:]
        mixed = part if t == 0 else mixed + part
    for k in range(BLOCKS):
        mixed_ref[k] = mixed[:images, k * shard : (k + 1) * shard]


def head_kernel(
    got_ref, mean_ref, scale_ref, bout_ref, gain_ref, bias_ref, project_ref, out_ref
):
    images, shard = got_ref.shape[1:]
    width = project_ref.shape[1]
    mixed = got_ref[0]
    for j in range(1, BLOCKS):
        mixed = mixed + got_ref[j]
    scale, bias_out = scale_ref[...], bout_ref[...]
    gain, bias = gain_ref[...], bias_ref[...]
    head = jnp.concatenate(
        [mean_ref[...] + scale * (mixed + bias_out), scale, bias_out, gain, bias], axis=0
    )
    first = jnp.sum(head, axis=1, keepdims=True)
    second = jnp.sum(head * head, axis=1, keepdims=True)
    value = jnp.where(iota((8, shard), 0) < images, head * gain, head)
    high, rest = to_terms(value)
    middle, low = to_terms(rest)
    product = jnp.dot(
        jnp.concatenate([high, middle, low], axis=0).astype(bf16),
        project_ref[...],
        preferred_element_type=f32,
    )
    out_ref[:, :width] = product[:8] + (product[8:16] + product[16:])
    lane = iota((8, 128), 1)
    out_ref[:, width : width + 128] = jnp.where(
        lane == 0, first, jnp.where(lane == 1, second, 0.0)
    )
    out_ref[:, width + 128 : width + 128 + shard] = head


def pair_sum_kernel(mine_ref, other_ref, out_ref):
    cut = out_ref.shape[2] - 2 * SHARD
    block = jnp.concatenate(
        [
            mine_ref[:, :cut] + other_ref[:, :cut],
            mine_ref[:, cut : cut + SHARD],
            other_ref[:, cut : cut + SHARD],
        ],
        axis=1,
    )
    for j in range(CHIPS):
        out_ref[j] = block


def embed_kernel(got_ref, text_ref, labels_ref, out_ref, head_ref, stat_ref):
    pairs, width = text_ref.shape
    cut = width + 128
    core = lax.axis_index("mp") % 2
    channels = BLOCKS * SHARD
    for j in range(CHIPS):
        head_ref[2 * j + core] = got_ref[j, :, cut : cut + SHARD]
        head_ref[2 * j + 1 - core] = got_ref[j, :, cut + SHARD :]
    sums = got_ref[0, :, :cut]
    for j in range(1, CHIPS):
        sums = sums + got_ref[j, :, :cut]
    mean = sums[:, width : width + 1] / channels
    inverse = lax.rsqrt(sums[:, width + 1 : width + 2] / channels - mean * mean + eps)
    emb = inverse * (sums[:, :width] - mean * sums[6:7, :width]) + sums[7:8, :width]
    row = iota((8, 128), 0)
    tail = jnp.zeros((8, 128), f32)
    for r in range(pairs):
        label = labels_ref[r]
        target = (label // pairs) * 8 + 4 + label % pairs
        tail = jnp.where(row == r, target.astype(f32), tail)
    block = jnp.concatenate([emb[:4], text_ref[...]], axis=0)
    for d in range(out_ref.shape[0]):
        out_ref[d, :, :width] = block
        out_ref[d, :, width:] = tail
    stat_ref[0] = jnp.broadcast_to(mean, (8, 128))
    stat_ref[1] = jnp.broadcast_to(inverse, (8, 128))


def loss_kernel(got_ref, project_ref, text_ref, back_ref, unit_ref, len_ref, both_ref):
    width = project_ref.shape[1]
    count = got_ref.shape[0] * 8
    home = pl.ds(pl.multiple_of(lax.axis_index("dp") * 8, 8), 8)
    raw = got_ref[:, :, :width].reshape(count, width)
    length = jnp.sqrt(jnp.sum(raw * raw, axis=1, keepdims=True) + eps)
    unit = raw / length
    unit_ref[...] = unit
    len_ref[...] = jnp.broadcast_to(length, (count, 128))
    logits = logit_scale * lax.dot_general(
        unit, unit, (((1,), (1,)), ((), ())), precision=highest, preferred_element_type=f32
    )
    column = iota((count, count), 1)
    valid = (iota((count, count), 0) % 8 < 4) & (column % 8 >= 4)
    weights = jnp.where(valid, jnp.exp(jnp.where(valid, logits, 0.0)), 0.0)
    row_total = jnp.sum(weights, axis=1, keepdims=True)
    col_total = jnp.sum(weights, axis=0, keepdims=True)
    target = got_ref[:, :, width:].reshape(count, 128)[:, 0:1]
    matched = jnp.where(target == column.astype(f32), 1.0, 0.0)
    grads = loss_scale * (0.5 * (weights / row_total + weights / col_total) - matched)
    grads = jnp.where(valid, grads, 0.0)
    both_ref[...] = grads + grads.T
    grad_unit = logit_scale * jnp.dot(
        both_ref[home, :], unit, precision=highest, preferred_element_type=f32
    )
    own = unit_ref[home, :]
    grad = (grad_unit - own * jnp.sum(own * grad_unit, axis=1, keepdims=True)) / len_ref[home, 0:1]
    text_ref[...] = grad[4:]
    back = lax.dot_general(
        grad.astype(bf16),
        project_ref[...],
        (((1,), (1,)), ((), ())),
        preferred_element_type=f32,
    )
    for k in range(BLOCKS):
        back_ref[k] = back[:4]


def backward_kernel(
    back_ref,
    head_ref,
    head_stat_ref,
    wout_ref,
    slope_ref,
    hidden_ref,
    w_ref,
    through_ref,
    b_ref,
    other_ref,
    turned_ref,
    sums_ref,
    block_ref,
    mixed_ref,
    pre_ref,
):
    images, shard = back_ref.shape[1:]
    rows, hidden = slope_ref.shape
    channels = w_ref.shape[0]
    positions = rows // images
    index = lax.axis_index("mp")
    core = index % 2
    mean = head_stat_ref[0][:images, 0:1]
    inverse = head_stat_ref[1][:images, 0:1]
    first = jnp.zeros((images, 1), f32)
    second = jnp.zeros((images, 1), f32)

    def parts(k):
        head = head_ref[k]
        return back_ref[k] * head[6:7], (head[:images] - mean) * inverse, head[4:5]

    for k in range(BLOCKS):
        scaled, centred, _ = parts(k)
        first = first + jnp.sum(scaled, axis=1, keepdims=True)
        second = second + jnp.sum(scaled * centred, axis=1, keepdims=True)
    first = first / channels
    second = second / channels

    def block(k):
        scaled, centred, scale = parts(k)
        grad = (inverse / positions) * (scaled - first - centred * second)
        return grad, grad * scale

    block_ref[...] = block(index)[0]
    mixed_ref[...] = jnp.zeros_like(mixed_ref)
    for k in range(BLOCKS):
        mixed_ref[0:images, k * shard : (k + 1) * shard] = block(k)[1]
    act = lax.dot_general(
        mixed_ref[...].astype(bf16),
        wout_ref[...],
        (((1,), (1,)), ((), ())),
        preferred_element_type=f32,
    )
    b_row = b_ref[...][None, :]
    step = 256
    one = jnp.zeros((rows, 1), f32)
    two = jnp.zeros((rows, 1), f32)
    for t in range(hidden // step):
        at = slice(t * step, (t + 1) * step)
        for n in range(images):
            span = slice(n * positions, (n + 1) * positions)
            pre_ref[span, :] = (act[n : n + 1, at] * slope_ref[span, at]).astype(bf16).astype(f32)
        value = pre_ref[...]
        gain = through_ref[0:1, at] + through_ref[8:9, at]
        bias = through_ref[1:2, at] + through_ref[9:10, at] + b_row[:, at]
        one = one + jnp.sum(value * gain, axis=1, keepdims=True)
        two = two + jnp.sum(value * (hidden_ref[:, at] - bias), axis=1, keepdims=True)
        turned_ref[at, :] = value.T.astype(bf16)
    lane = iota((rows, 128), 1)
    sums = jnp.where(lane == 0, one, jnp.where(lane == 1, two, 0.0)).T[:8]
    sums_ref[...] = sums
    high, low = to_terms(sums)
    other_ref[channels // 2 :, :] = jnp.concatenate([high, low], axis=0).astype(bf16)
    for j in range(CHIPS):
        start = pl.multiple_of((2 * j + 1 - core) * shard, 64)
        other_ref[j * shard : (j + 1) * shard, :] = jnp.dot(
            w_ref[pl.ds(start, shard), :], turned_ref[...], preferred_element_type=f32
        ).astype(bf16)


def mine_kernel(w_ref, turned_ref, mine_ref):
    shard = w_ref.shape[0] // BLOCKS
    core = lax.axis_index("mp") % 2
    for j in range(CHIPS):
        start = pl.multiple_of((2 * j + core) * shard, 64)
        mine_ref[j * shard : (j + 1) * shard, :] = jnp.dot(
            w_ref[pl.ds(start, shard), :], turned_ref[...], preferred_element_type=f32
        ).astype(bf16)


def pair_kernel(mine_ref, got_ref, sums_ref, out_ref):
    half = mine_ref.shape[0]
    shard = half // CHIPS
    for j in range(CHIPS):
        span = slice(j * shard, (j + 1) * shard)
        out_ref[j, :shard, :] = (mine_ref[span, :].astype(f32) + got_ref[span, :].astype(f32)).astype(
            bf16
        )
    tail = got_ref[half:, :].astype(f32)
    high, low = to_terms(sums_ref[...] + (tail[:8] + tail[8:]))
    tail = jnp.concatenate([high, low], axis=0).astype(bf16)
    for j in range(CHIPS):
        out_ref[j, shard:, :] = tail


def final_kernel(got_ref, conv_ref, stat_ref, gain_ref, w_ref, block_ref, out_ref, rows_ref):
    shard = conv_ref.shape[0]
    channels = shard * BLOCKS
    index = lax.axis_index("mp")
    gain = jnp.zeros((1, shard), f32)
    for k in range(BLOCKS):
        gain = jnp.where(index == k, gain_ref[:, k * shard : (k + 1) * shard], gain)
    gain = jnp.broadcast_to(gain, (8, shard)).T[:, 0:1]
    images, side = out_ref.shape[:2]
    positions = side * side
    total = got_ref[0].astype(f32)
    for j in range(1, CHIPS):
        total = total + got_ref[j].astype(f32)
    first = (total[shard : shard + 1] + total[shard + 8 : shard + 9]) / channels
    second = (total[shard + 1 : shard + 2] + total[shard + 9 : shard + 10]) / channels
    average, inverse = stat_ref[0:1, :], stat_ref[1:2, :]
    centred = (conv_ref[...].astype(f32) - average) * inverse
    grad = inverse * (total[:shard] * gain - first - centred * second)
    rows_ref[...] = grad.T

    def image(n, carry):
        span = pl.ds(pl.multiple_of(n * positions, positions), positions)
        x = rows_ref[span, :].reshape(side, side, shard)
        base = block_ref[pl.ds(n, 1), :]
        for p, row in enumerate(taps(x, w_ref, True)):
            out_ref[n, p] = row + base
        return carry

    lax.fori_loop(0, images, image, 0)


def body(
    x_in,
    dw_weight,
    dw_bias,
    ln_gain,
    ln_bias,
    w_in,
    b_in,
    w_out,
    b_out,
    layer_scale,
    head_gain,
    head_bias,
    projection,
    text_emb,
    labels,
):
    images, side, _, shard = x_in.shape
    channels, hidden = w_in.shape
    rows = images * side * side
    pairs, width = text_emb.shape
    shards = lax.axis_size("dp")
    copies, conv, input_mean = run(
        conv_kernel,
        [
            shape(CHIPS, shard, rows, dtype=bf16),
            shape(shard, rows, dtype=bf16),
            shape(images, shard),
        ],
        x_in,
        dw_weight,
        dw_bias[None, :],
        scratch=[pltpu.VMEM((rows, shard), f32)],
        flops=2 * 49 * rows * shard,
    )
    conv_mine = chip_exchange(copies)
    conv_other = core_swap(conv_mine)
    slope, hidden_pre, through, row_stat, mixed = run(
        forward_kernel,
        [
            shape(rows, hidden),
            shape(rows, hidden),
            shape(16, hidden),
            shape(8, rows),
            shape(BLOCKS, images, shard),
        ],
        conv_mine,
        conv_other,
        ln_gain[None, :],
        ln_bias[None, :],
        w_in,
        b_in,
        w_out,
        scratch=[
            pltpu.VMEM((channels, rows), bf16),
            pltpu.VMEM((rows + 16, channels), bf16),
            pltpu.VMEM((2 * BLOCKS, shard), f32),
            pltpu.VMEM((8, channels), f32),
        ],
        flops=2 * rows * channels * hidden,
    )
    (sums,) = run(
        head_kernel,
        [shape(8, width + 128 + 256)],
        shard_exchange(mixed),
        input_mean,
        layer_scale[None, :],
        b_out[None, :],
        head_gain[None, :],
        head_bias[None, :],
        projection,
    )
    (blocks,) = run(
        pair_sum_kernel, [shape(CHIPS, 8, width + 128 + 2 * shard)], sums, core_swap(sums)
    )
    pair_block, head, head_stat = run(
        embed_kernel,
        [shape(shards, 8, width + 128), shape(BLOCKS, 8, shard), shape(2, 8, 128)],
        chip_exchange(blocks),
        text_emb,
        labels,
    )
    grad_text, back = run(
        loss_kernel,
        [shape(pairs, width), shape(BLOCKS, images, shard)],
        lax.all_to_all(pair_block, "dp", 0, 0),
        projection,
        scratch=[
            pltpu.VMEM((shards * 8, width), f32),
            pltpu.VMEM((shards * 8, 128), f32),
            pltpu.VMEM((shards * 8, shards * 8), f32),
        ],
    )
    other, turned, row_sums, grad_block = run(
        backward_kernel,
        [
            shape(channels // 2 + 16, rows, dtype=bf16),
            shape(hidden, rows, dtype=bf16),
            shape(8, rows),
            shape(images, shard),
        ],
        shard_exchange(back),
        head,
        head_stat,
        w_out,
        slope,
        hidden_pre,
        w_in,
        through,
        b_in,
        scratch=[pltpu.VMEM((8, channels), f32), pltpu.VMEM((rows, 256), f32)],
        flops=rows * channels * hidden,
    )
    passed = core_swap(other)
    (mine,) = run(
        mine_kernel,
        [shape(channels // 2, rows, dtype=bf16)],
        w_in,
        turned,
        flops=rows * channels * hidden,
    )
    (blocks,) = run(
        pair_kernel, [shape(CHIPS, shard + 16, rows, dtype=bf16)], mine, passed, row_sums
    )
    (grad_input,) = run(
        final_kernel,
        [shape(images, side, side, shard)],
        chip_exchange(blocks),
        conv,
        row_stat,
        ln_gain[None, :],
        dw_weight,
        grad_block,
        scratch=[pltpu.VMEM((rows, shard), f32)],
        flops=2 * 49 * rows * shard,
    )
    return (grad_input, grad_text)


def solution(mesh):
    return jax.shard_map(
        body,
        mesh=mesh,
        in_specs=(
            P("dp", None, None, "mp"),
            P(None, None, "mp"),
            P("mp"),
            P(),
            P(),
            P(None, "mp"),
            P("mp"),
            P("mp", None),
            P("mp"),
            P("mp"),
            P("mp"),
            P("mp"),
            P("mp", None),
            P("dp", None),
            P("dp"),
        ),
        out_specs=(P("dp", None, None, "mp"), P("dp", None)),
        check_vma=False,
    )
```

```python
import jax
import jax.numpy as jnp
from jax import lax
from jax.experimental import pallas as pl
from jax.experimental.pallas import tpu as pltpu
from jax.sharding import PartitionSpec as P

eps = 1e-06
logit_scale = 20.0
loss_scale = 512.0
root_half = 0.7071067811865476
inv_root_two_pi = 0.3989422804014327
f32 = jnp.float32
bf16 = jnp.bfloat16
highest = lax.Precision.HIGHEST
MIB = 1 << 20
CONV_LIMIT = 50 * MIB
CONV_FLOPS = 16 * 10**9
CHIPS = 8
BLOCKS = 16
SHARD = 192


def core_swap(array):
    return lax.ppermute(array, "mp", [(i, i ^ 1) for i in range(BLOCKS)])


def chip_exchange(array):
    groups = [[i for i in range(core, BLOCKS, 2)] for core in range(2)]
    return lax.all_to_all(array, "mp", 0, 0, axis_index_groups=groups)


def shard_exchange(array):
    return lax.all_to_all(array, "mp", 0, 0)


class Far:
    def __init__(self, array):
        self.array = array


def run(kernel, outs, *operands, scratch=(), limit=24 * MIB, flops=0):
    def spec(a):
        if isinstance(a, Far):
            return pl.BlockSpec(memory_space=pltpu.HBM)
        return pl.BlockSpec(memory_space=pltpu.SMEM if a.dtype == jnp.int32 else pltpu.VMEM)

    arrays = [a.array if isinstance(a, Far) else a for a in operands]
    return pl.pallas_call(
        kernel,
        out_shape=outs,
        in_specs=[spec(a) for a in operands],
        out_specs=[pl.BlockSpec(memory_space=pltpu.VMEM) for _ in outs],
        scratch_shapes=list(scratch),
        compiler_params=pltpu.CompilerParams(vmem_limit_bytes=limit),
        cost_estimate=pl.CostEstimate(
            flops=flops,
            bytes_accessed=sum(a.size * a.dtype.itemsize for a in arrays),
            transcendentals=0,
        ),
    )(*arrays)


def shape(*dims, dtype=f32):
    return jax.ShapeDtypeStruct(dims, dtype)


def iota(dims, axis):
    return lax.broadcasted_iota(jnp.int32, dims, axis)


def to_terms(array):
    high = array.astype(bf16).astype(f32)
    return high, array - high


def taps(x, w_ref, flip):
    side, _, shard = x.shape
    size = w_ref.shape[0]
    reach = size // 2
    column = iota((side, side, shard), 1)
    acc = [jnp.zeros((side, shard), f32) for _ in range(side)]
    for b in range(size):
        by = b - reach
        if by:
            moved = jnp.where(
                (column + by >= 0) & (column + by < side), pltpu.roll(x, (-by) % side, 1), 0.0
            )
        else:
            moved = x
        for a in range(size):
            wa, wb = (size - 1 - a, size - 1 - b) if flip else (a, b)
            weight = w_ref[wa, wb : wb + 1, :]
            for p in range(side):
                if 0 <= p + a - reach < side:
                    acc[p] = acc[p] + moved[p + a - reach] * weight
    return acc


def conv_kernel(
    x_far, dw_far, bias_far, copies_ref, conv_ref, mean_ref, x_ref, dw_ref, bias_ref, rows_ref, sems
):
    images, side = x_ref.shape[:2]
    positions = side * side
    loads = ((x_far, x_ref), (dw_far, dw_ref), (bias_far, bias_ref))
    loads = [pltpu.make_async_copy(far, near, sems.at[i]) for i, (far, near) in enumerate(loads)]
    for copy in loads:
        copy.start()
    for copy in loads:
        copy.wait()

    def image(n, carry):
        x = x_ref[n].astype(f32)
        total = jnp.sum(jnp.sum(x, axis=0), axis=0, keepdims=True)
        mean_ref[pl.ds(n, 1), :] = total / positions
        for p, row in enumerate(taps(x, dw_ref, False)):
            rows_ref[pl.ds(pl.multiple_of(n * positions + p * side, side), side), :] = row
        return carry

    lax.fori_loop(0, images, image, 0)
    turned = (rows_ref[...] + bias_ref[...]).T.astype(bf16)
    conv_ref[...] = turned
    for j in range(CHIPS):
        copies_ref[j] = turned


def forward_kernel(
    mine_ref,
    other_ref,
    gain_ref,
    bias_ref,
    w_ref,
    b_ref,
    wout_ref,
    slope_ref,
    hidden_ref,
    through_ref,
    stat_ref,
    mixed_ref,
    turned_ref,
    normed_ref,
    own_ref,
    vec_ref,
):
    shard, rows = mine_ref.shape[1:]
    channels, hidden = w_ref.shape
    images = mixed_ref.shape[1]
    positions = rows // images
    core = lax.axis_index("mp") % 2
    vec_ref[...] = jnp.zeros_like(vec_ref)
    for i, ref in enumerate((gain_ref, bias_ref)):
        vec_ref[i : i + 1, :] = ref[...]
        for j in range(CHIPS):
            low = ref[:, 2 * j * shard : (2 * j + 1) * shard]
            high = ref[:, (2 * j + 1) * shard : (2 * j + 2) * shard]
            at = i * BLOCKS + j
            own_ref[at : at + 1, :] = jnp.where(core == 0, low, high)
            own_ref[at + CHIPS : at + CHIPS + 1, :] = jnp.where(core == 0, high, low)
    first = jnp.zeros((1, rows), f32)
    second = jnp.zeros((1, rows), f32)
    for ref in (mine_ref, other_ref):
        for j in range(CHIPS):
            value = ref[j].astype(f32)
            first = first + jnp.sum(value, axis=0, keepdims=True)
            second = second + jnp.sum(value * value, axis=0, keepdims=True)
    average = first / channels
    inverse = lax.rsqrt(second / channels - average * average + eps)
    stat_ref[0:1, :] = average
    stat_ref[1:2, :] = inverse
    own = own_ref[...].T
    for h, ref in enumerate((mine_ref, other_ref)):
        for j in range(CHIPS):
            k = h * CHIPS + j
            value = (ref[j].astype(f32) - average) * inverse
            value = value * own[:, k : k + 1] + own[:, BLOCKS + k : BLOCKS + k + 1]
            start = (2 * j + (core if h == 0 else 1 - core)) * shard
            turned_ref[pl.ds(pl.multiple_of(start, 64), shard), :] = value.astype(bf16)
    step = 256
    for c in range(channels // step):
        normed_ref[0:rows, c * step : (c + 1) * step] = turned_ref[c * step : (c + 1) * step, :].T
    normed_ref[rows : rows + 16, :] = jnp.concatenate(to_terms(vec_ref[...]), axis=0).astype(bf16)
    b_row = b_ref[...][None, :]
    for t in range(hidden // step):
        at = slice(t * step, (t + 1) * step)
        product = jnp.dot(normed_ref[...], w_ref[:, at], preferred_element_type=f32)
        through_ref[:, at] = product[rows:]
        pre = product[:rows] + b_row[:, at]
        hidden_ref[:, at] = pre
        gate = 0.5 + 0.5 * lax.erf(pre * root_half)
        slope_ref[:, at] = gate + pre * jnp.exp(-0.5 * pre * pre) * inv_root_two_pi
        active = pre * gate
        sums = [
            jnp.sum(active[n * positions : (n + 1) * positions], axis=0, keepdims=True) / positions
            for n in range(images)
        ]
        sums = jnp.concatenate(sums + [jnp.zeros((8 - images, step), f32)], axis=0)
        high, low = to_terms(sums)
        part = jnp.dot(
            jnp.concatenate([high, low], axis=0).astype(bf16),
            wout_ref[at, :],
            preferred_element_type=f32,
        )
        part = part[:8] + part[8:]
        mixed = part if t == 0 else mixed + part
    for k in range(BLOCKS):
        mixed_ref[k] = mixed[:images, k * shard : (k + 1) * shard]


def head_kernel(
    got_ref, mean_ref, scale_ref, bout_ref, gain_ref, bias_ref, project_ref, out_ref
):
    images, shard = got_ref.shape[1:]
    width = project_ref.shape[1]
    mixed = got_ref[0]
    for j in range(1, BLOCKS):
        mixed = mixed + got_ref[j]
    scale, bias_out = scale_ref[...], bout_ref[...]
    gain, bias = gain_ref[...], bias_ref[...]
    head = jnp.concatenate(
        [mean_ref[...] + scale * (mixed + bias_out), scale, bias_out, gain, bias], axis=0
    )
    first = jnp.sum(head, axis=1, keepdims=True)
    second = jnp.sum(head * head, axis=1, keepdims=True)
    value = jnp.where(iota((8, shard), 0) < images, head * gain, head)
    high, rest = to_terms(value)
    middle, low = to_terms(rest)
    product = jnp.dot(
        jnp.concatenate([high, middle, low], axis=0).astype(bf16),
        project_ref[...],
        preferred_element_type=f32,
    )
    out_ref[:, :width] = product[:8] + (product[8:16] + product[16:])
    lane = iota((8, 128), 1)
    out_ref[:, width : width + 128] = jnp.where(
        lane == 0, first, jnp.where(lane == 1, second, 0.0)
    )
    out_ref[:, width + 128 : width + 128 + shard] = head


def pair_sum_kernel(mine_ref, other_ref, out_ref):
    cut = out_ref.shape[2] - 2 * SHARD
    block = jnp.concatenate(
        [
            mine_ref[:, :cut] + other_ref[:, :cut],
            mine_ref[:, cut : cut + SHARD],
            other_ref[:, cut : cut + SHARD],
        ],
        axis=1,
    )
    for j in range(CHIPS):
        out_ref[j] = block


def embed_kernel(got_ref, text_ref, labels_ref, out_ref, own_ref, head_ref, stat_ref):
    pairs, width = text_ref.shape
    cut = width + 128
    core = lax.axis_index("mp") % 2
    channels = BLOCKS * SHARD
    for j in range(CHIPS):
        head_ref[2 * j + core] = got_ref[j, :, cut : cut + SHARD]
        head_ref[2 * j + 1 - core] = got_ref[j, :, cut + SHARD :]
    sums = got_ref[0, :, :cut]
    for j in range(1, CHIPS):
        sums = sums + got_ref[j, :, :cut]
    mean = sums[:, width : width + 1] / channels
    inverse = lax.rsqrt(sums[:, width + 1 : width + 2] / channels - mean * mean + eps)
    emb = inverse * (sums[:, :width] - mean * sums[6:7, :width]) + sums[7:8, :width]
    row = iota((8, 128), 0)
    tail = jnp.zeros((8, 128), f32)
    for r in range(pairs):
        label = labels_ref[r]
        target = (label // pairs) * 8 + 4 + label % pairs
        tail = jnp.where(row == r, target.astype(f32), tail)
    block = jnp.concatenate([emb[:4], text_ref[...]], axis=0)
    own_ref[...] = block
    half = width // 2
    block = jnp.concatenate([block[:, :half], block[:, half:]], axis=0).astype(bf16)
    tail = jnp.concatenate([tail, tail], axis=0).astype(bf16)
    for d in range(out_ref.shape[0]):
        out_ref[d, :, :half] = block
        out_ref[d, :, half:] = tail
    stat_ref[0] = jnp.broadcast_to(mean, (8, 128))
    stat_ref[1] = jnp.broadcast_to(inverse, (8, 128))


def loss_kernel(got_ref, own_ref, project_ref, text_ref, back_ref, both_ref):
    width = project_ref.shape[1]
    count = got_ref.shape[0] * 8
    home = pl.ds(pl.multiple_of(lax.axis_index("dp") * 8, 8), 8)
    half = width // 2
    got = got_ref[...].astype(f32)
    raw = jnp.concatenate(
        [got[:, :8, :half].reshape(count, half), got[:, 8:, :half].reshape(count, half)], axis=1
    )
    unit = raw / jnp.sqrt(jnp.sum(raw * raw, axis=1, keepdims=True) + eps)
    logits = logit_scale * lax.dot_general(
        unit, unit, (((1,), (1,)), ((), ())), precision=highest, preferred_element_type=f32
    )
    column = iota((count, count), 1)
    valid = (iota((count, count), 0) % 8 < 4) & (column % 8 >= 4)
    weights = jnp.where(valid, jnp.exp(jnp.where(valid, logits, 0.0)), 0.0)
    row_total = jnp.sum(weights, axis=1, keepdims=True)
    col_total = jnp.sum(weights, axis=0, keepdims=True)
    target = got[:, :8, half:].reshape(count, 128)[:, 0:1]
    matched = jnp.where(target == column.astype(f32), 1.0, 0.0)
    grads = loss_scale * (0.5 * (weights / row_total + weights / col_total) - matched)
    grads = jnp.where(valid, grads, 0.0)
    both_ref[...] = grads + grads.T
    grad_unit = logit_scale * jnp.dot(
        both_ref[home, :], unit, precision=highest, preferred_element_type=f32
    )
    own = own_ref[...]
    length = jnp.sqrt(jnp.sum(own * own, axis=1, keepdims=True) + eps)
    own = own / length
    grad = (grad_unit - own * jnp.sum(own * grad_unit, axis=1, keepdims=True)) / length
    text_ref[...] = grad[4:]
    back = lax.dot_general(
        grad.astype(bf16),
        project_ref[...],
        (((1,), (1,)), ((), ())),
        preferred_element_type=f32,
    )
    for k in range(BLOCKS):
        back_ref[k] = back[:4]


def backward_kernel(
    back_ref,
    head_ref,
    head_stat_ref,
    wout_ref,
    slope_ref,
    hidden_ref,
    w_ref,
    through_ref,
    b_ref,
    other_ref,
    turned_ref,
    sums_ref,
    block_ref,
    mixed_ref,
    pre_ref,
):
    images, shard = back_ref.shape[1:]
    rows, hidden = slope_ref.shape
    channels = w_ref.shape[0]
    positions = rows // images
    index = lax.axis_index("mp")
    core = index % 2
    mean = head_stat_ref[0][:images, 0:1]
    inverse = head_stat_ref[1][:images, 0:1]
    first = jnp.zeros((images, 1), f32)
    second = jnp.zeros((images, 1), f32)

    def parts(k):
        head = head_ref[k]
        return back_ref[k] * head[6:7], (head[:images] - mean) * inverse, head[4:5]

    for k in range(BLOCKS):
        scaled, centred, _ = parts(k)
        first = first + jnp.sum(scaled, axis=1, keepdims=True)
        second = second + jnp.sum(scaled * centred, axis=1, keepdims=True)
    first = first / channels
    second = second / channels

    def block(k):
        scaled, centred, scale = parts(k)
        grad = (inverse / positions) * (scaled - first - centred * second)
        return grad, grad * scale

    block_ref[...] = block(index)[0]
    mixed_ref[...] = jnp.zeros_like(mixed_ref)
    for k in range(BLOCKS):
        mixed_ref[0:images, k * shard : (k + 1) * shard] = block(k)[1]
    act = lax.dot_general(
        mixed_ref[...].astype(bf16),
        wout_ref[...],
        (((1,), (1,)), ((), ())),
        preferred_element_type=f32,
    )
    b_row = b_ref[...][None, :]
    step = 256
    one = jnp.zeros((rows, 1), f32)
    two = jnp.zeros((rows, 1), f32)
    for t in range(hidden // step):
        at = slice(t * step, (t + 1) * step)
        for n in range(images):
            span = slice(n * positions, (n + 1) * positions)
            pre_ref[span, :] = (act[n : n + 1, at] * slope_ref[span, at]).astype(bf16).astype(f32)
        value = pre_ref[...]
        gain = through_ref[0:1, at] + through_ref[8:9, at]
        bias = through_ref[1:2, at] + through_ref[9:10, at] + b_row[:, at]
        one = one + jnp.sum(value * gain, axis=1, keepdims=True)
        two = two + jnp.sum(value * (hidden_ref[:, at] - bias), axis=1, keepdims=True)
        turned_ref[at, :] = value.T.astype(bf16)
    lane = iota((rows, 128), 1)
    sums = jnp.where(lane == 0, one, jnp.where(lane == 1, two, 0.0)).T[:8]
    sums_ref[...] = sums
    high, low = to_terms(sums)
    other_ref[channels // 2 :, :] = jnp.concatenate([high, low], axis=0).astype(bf16)
    for j in range(CHIPS):
        start = pl.multiple_of((2 * j + 1 - core) * shard, 64)
        other_ref[j * shard : (j + 1) * shard, :] = jnp.dot(
            w_ref[pl.ds(start, shard), :], turned_ref[...], preferred_element_type=f32
        ).astype(bf16)


def mine_kernel(w_ref, turned_ref, mine_ref):
    shard = w_ref.shape[0] // BLOCKS
    core = lax.axis_index("mp") % 2
    for j in range(CHIPS):
        start = pl.multiple_of((2 * j + core) * shard, 64)
        mine_ref[j * shard : (j + 1) * shard, :] = jnp.dot(
            w_ref[pl.ds(start, shard), :], turned_ref[...], preferred_element_type=f32
        ).astype(bf16)


def pair_kernel(mine_ref, got_ref, sums_ref, out_ref):
    half = mine_ref.shape[0]
    shard = half // CHIPS
    for j in range(CHIPS):
        span = slice(j * shard, (j + 1) * shard)
        out_ref[j, :shard, :] = (mine_ref[span, :].astype(f32) + got_ref[span, :].astype(f32)).astype(
            bf16
        )
    tail = got_ref[half:, :].astype(f32)
    high, low = to_terms(sums_ref[...] + (tail[:8] + tail[8:]))
    tail = jnp.concatenate([high, low], axis=0).astype(bf16)
    for j in range(CHIPS):
        out_ref[j, shard:, :] = tail


def final_kernel(got_ref, conv_ref, stat_ref, gain_ref, w_ref, block_ref, out_ref, rows_ref):
    shard = conv_ref.shape[0]
    channels = shard * BLOCKS
    index = lax.axis_index("mp")
    pair = gain_ref[:, pl.ds(pl.multiple_of(index // 2 * 2 * shard, 128), 2 * shard)]
    gain = jnp.where(index % 2 == 0, pair[:, :shard], pair[:, shard:])
    gain = jnp.broadcast_to(gain, (8, shard)).T[:, 0:1]
    images, side = out_ref.shape[:2]
    positions = side * side
    total = got_ref[0].astype(f32)
    for j in range(1, CHIPS):
        total = total + got_ref[j].astype(f32)
    first = (total[shard : shard + 1] + total[shard + 8 : shard + 9]) / channels
    second = (total[shard + 1 : shard + 2] + total[shard + 9 : shard + 10]) / channels
    average, inverse = stat_ref[0:1, :], stat_ref[1:2, :]
    centred = (conv_ref[...].astype(f32) - average) * inverse
    grad = inverse * (total[:shard] * gain - first - centred * second)
    rows_ref[...] = grad.T

    def image(n, carry):
        span = pl.ds(pl.multiple_of(n * positions, positions), positions)
        x = rows_ref[span, :].reshape(side, side, shard)
        base = block_ref[pl.ds(n, 1), :]
        for p, row in enumerate(taps(x, w_ref, True)):
            out_ref[n, p] = row + base
        return carry

    lax.fori_loop(0, images, image, 0)


def body(
    x_in,
    dw_weight,
    dw_bias,
    ln_gain,
    ln_bias,
    w_in,
    b_in,
    w_out,
    b_out,
    layer_scale,
    head_gain,
    head_bias,
    projection,
    text_emb,
    labels,
):
    images, side, _, shard = x_in.shape
    channels, hidden = w_in.shape
    rows = images * side * side
    pairs, width = text_emb.shape
    shards = lax.axis_size("dp")
    copies, conv, input_mean = run(
        conv_kernel,
        [
            shape(CHIPS, shard, rows, dtype=bf16),
            shape(shard, rows, dtype=bf16),
            shape(images, shard),
        ],
        Far(x_in),
        Far(dw_weight),
        Far(dw_bias[None, :]),
        scratch=[
            pltpu.VMEM(x_in.shape, bf16),
            pltpu.VMEM(dw_weight.shape, f32),
            pltpu.VMEM((1, shard), f32),
            pltpu.VMEM((rows, shard), f32),
            pltpu.SemaphoreType.DMA((3,)),
        ],
        limit=CONV_LIMIT,
        flops=CONV_FLOPS,
    )
    conv_mine = chip_exchange(copies)
    conv_other = core_swap(conv_mine)
    slope, hidden_pre, through, row_stat, mixed = run(
        forward_kernel,
        [
            shape(rows, hidden),
            shape(rows, hidden),
            shape(16, hidden),
            shape(8, rows),
            shape(BLOCKS, images, shard),
        ],
        conv_mine,
        conv_other,
        ln_gain[None, :],
        ln_bias[None, :],
        w_in,
        b_in,
        w_out,
        scratch=[
            pltpu.VMEM((channels, rows), bf16),
            pltpu.VMEM((rows + 16, channels), bf16),
            pltpu.VMEM((2 * BLOCKS, shard), f32),
            pltpu.VMEM((8, channels), f32),
        ],
        flops=2 * rows * channels * hidden,
    )
    (sums,) = run(
        head_kernel,
        [shape(8, width + 128 + 256)],
        shard_exchange(mixed),
        input_mean,
        layer_scale[None, :],
        b_out[None, :],
        head_gain[None, :],
        head_bias[None, :],
        projection,
    )
    (blocks,) = run(
        pair_sum_kernel, [shape(CHIPS, 8, width + 128 + 2 * shard)], sums, core_swap(sums)
    )
    pair_block, own_block, head, head_stat = run(
        embed_kernel,
        [
            shape(shards, 16, width // 2 + 128, dtype=bf16),
            shape(8, width),
            shape(BLOCKS, 8, shard),
            shape(2, 8, 128),
        ],
        chip_exchange(blocks),
        text_emb,
        labels,
    )
    grad_text, back = run(
        loss_kernel,
        [shape(pairs, width), shape(BLOCKS, images, shard)],
        lax.all_to_all(pair_block, "dp", 0, 0),
        own_block,
        projection,
        scratch=[pltpu.VMEM((shards * 8, shards * 8), f32)],
    )
    other, turned, row_sums, grad_block = run(
        backward_kernel,
        [
            shape(channels // 2 + 16, rows, dtype=bf16),
            shape(hidden, rows, dtype=bf16),
            shape(8, rows),
            shape(images, shard),
        ],
        shard_exchange(back),
        head,
        head_stat,
        w_out,
        slope,
        hidden_pre,
        w_in,
        through,
        b_in,
        scratch=[pltpu.VMEM((8, channels), f32), pltpu.VMEM((rows, 256), f32)],
        flops=rows * channels * hidden,
    )
    passed = core_swap(other)
    (mine,) = run(
        mine_kernel,
        [shape(channels // 2, rows, dtype=bf16)],
        w_in,
        turned,
        flops=rows * channels * hidden,
    )
    (blocks,) = run(
        pair_kernel, [shape(CHIPS, shard + 16, rows, dtype=bf16)], mine, passed, row_sums
    )
    (grad_input,) = run(
        final_kernel,
        [shape(images, side, side, shard)],
        chip_exchange(blocks),
        conv,
        row_stat,
        ln_gain[None, :],
        dw_weight,
        grad_block,
        scratch=[pltpu.VMEM((rows, shard), f32)],
        flops=2 * 49 * rows * shard,
    )
    return (grad_input, grad_text)


def solution(mesh):
    return jax.shard_map(
        body,
        mesh=mesh,
        in_specs=(
            P("dp", None, None, "mp"),
            P(None, None, "mp"),
            P("mp"),
            P(),
            P(),
            P(None, "mp"),
            P("mp"),
            P("mp", None),
            P("mp"),
            P("mp"),
            P("mp"),
            P("mp"),
            P("mp", None),
            P("dp", None),
            P("dp"),
        ),
        out_specs=(P("dp", None, None, "mp"), P("dp", None)),
        check_vma=False,
    )
```

```python
import jax
import jax.numpy as jnp
from jax import lax
from jax.experimental import pallas as pl
from jax.experimental.pallas import tpu as pltpu
from jax.sharding import PartitionSpec as P

eps = 1e-06
logit_scale = 20.0
loss_scale = 512.0
root_half = 0.7071067811865476
inv_root_two_pi = 0.3989422804014327
f32 = jnp.float32
bf16 = jnp.bfloat16
highest = lax.Precision.HIGHEST
MIB = 1 << 20
CONV_LIMIT = 50 * MIB
CONV_FLOPS = 16 * 10**9
START_FLOPS = 4 * 10**9
CHIPS = 8
BLOCKS = 16
SHARD = 192
POSITIONS = 64


def core_swap(array):
    return lax.ppermute(array, "mp", [(i, i ^ 1) for i in range(BLOCKS)])


def chip_exchange(array):
    groups = [[i for i in range(core, BLOCKS, 2)] for core in range(2)]
    return lax.all_to_all(array, "mp", 0, 0, axis_index_groups=groups)


def shard_exchange(array):
    return lax.all_to_all(array, "mp", 0, 0)


class Far:
    def __init__(self, array):
        self.array = array


def run(kernel, outs, *operands, scratch=(), limit=24 * MIB, flops=0):
    def spec(a):
        if isinstance(a, Far):
            return pl.BlockSpec(memory_space=pltpu.HBM)
        return pl.BlockSpec(memory_space=pltpu.SMEM if a.dtype == jnp.int32 else pltpu.VMEM)

    arrays = [a.array if isinstance(a, Far) else a for a in operands]
    return pl.pallas_call(
        kernel,
        out_shape=outs,
        in_specs=[spec(a) for a in operands],
        out_specs=[pl.BlockSpec(memory_space=pltpu.VMEM) for _ in outs],
        scratch_shapes=list(scratch),
        compiler_params=pltpu.CompilerParams(vmem_limit_bytes=limit),
        cost_estimate=pl.CostEstimate(
            flops=flops,
            bytes_accessed=sum(a.size * a.dtype.itemsize for a in arrays),
            transcendentals=0,
        ),
    )(*arrays)


def shape(*dims, dtype=f32):
    return jax.ShapeDtypeStruct(dims, dtype)


def iota(dims, axis):
    return lax.broadcasted_iota(jnp.int32, dims, axis)


def to_terms(array):
    high = array.astype(bf16).astype(f32)
    return high, array - high


def taps(x, w_ref, flip):
    side, _, shard = x.shape
    size = w_ref.shape[0]
    reach = size // 2
    column = iota((side, side, shard), 1)
    acc = [jnp.zeros((side, shard), f32) for _ in range(side)]
    for b in range(size):
        by = b - reach
        if by:
            moved = jnp.where(
                (column + by >= 0) & (column + by < side), pltpu.roll(x, (-by) % side, 1), 0.0
            )
        else:
            moved = x
        for a in range(size):
            wa, wb = (size - 1 - a, size - 1 - b) if flip else (a, b)
            weight = w_ref[wa, wb : wb + 1, :]
            for p in range(side):
                if 0 <= p + a - reach < side:
                    acc[p] = acc[p] + moved[p + a - reach] * weight
    return acc


def start_kernel(labels_ref, tail_ref):
    pairs = labels_ref.shape[0]
    row = iota((8, 128), 0)
    tail = jnp.zeros((8, 128), f32)
    for r in range(pairs):
        label = labels_ref[r]
        target = (label // pairs) * 8 + 4 + label % pairs
        tail = jnp.where(row == r, target.astype(f32), tail)
    tail_ref[...] = tail


def conv_kernel(
    _, x_far, dw_far, bias_far, copies_ref, conv_ref, mean_ref, x_ref, dw_ref, bias_ref, rows_ref, sems
):
    images, side = x_ref.shape[:2]
    positions = side * side
    loads = ((x_far, x_ref), (dw_far, dw_ref), (bias_far, bias_ref))
    loads = [pltpu.make_async_copy(far, near, sems.at[i]) for i, (far, near) in enumerate(loads)]
    for copy in loads:
        copy.start()
    for copy in loads:
        copy.wait()

    def image(n, carry):
        x = x_ref[n].astype(f32)
        total = jnp.sum(jnp.sum(x, axis=0), axis=0, keepdims=True)
        mean_ref[pl.ds(n, 1), :] = total / positions
        for p, row in enumerate(taps(x, dw_ref, False)):
            rows_ref[pl.ds(pl.multiple_of(n * positions + p * side, side), side), :] = row
        return carry

    lax.fori_loop(0, images, image, 0)
    turned = (rows_ref[...] + bias_ref[...]).T.astype(bf16)
    conv_ref[...] = turned
    for j in range(CHIPS):
        copies_ref[j] = turned


def ready_kernel(
    mine_ref, gain_ref, bias_ref, w_ref, rows_ref, part_ref, vec_ref, own_ref, sems
):
    shard = w_ref.shape[0] // BLOCKS
    core = lax.axis_index("mp") % 2
    moves = []
    for k in range(BLOCKS):
        place = 2 * (k % CHIPS) + (core if k < CHIPS else 1 - core)
        source = pl.ds(pl.multiple_of(place * shard, 64), shard)
        moves.append(
            pltpu.make_async_copy(
                w_ref.at[source], own_ref.at[k * shard : (k + 1) * shard], sems.at[k]
            )
        )
    for copy in moves:
        copy.start()
    half, rows = mine_ref.shape
    step = 256
    first = jnp.zeros((1, rows), f32)
    second = jnp.zeros((1, rows), f32)
    for c in range(half // step):
        at = slice(c * step, (c + 1) * step)
        rows_ref[:, at] = mine_ref[at, :].T
        value = mine_ref[at, :].astype(f32)
        first = first + jnp.sum(value, axis=0, keepdims=True)
        second = second + jnp.sum(value * value, axis=0, keepdims=True)
    part_ref[0:1, :] = first
    part_ref[1:2, :] = second
    vec_ref[...] = jnp.zeros_like(vec_ref)
    for i, ref in enumerate((gain_ref, bias_ref)):
        for j in range(CHIPS):
            low = ref[:, 2 * j * shard : (2 * j + 1) * shard]
            high = ref[:, (2 * j + 1) * shard : (2 * j + 2) * shard]
            vec_ref[i : i + 1, j * shard : (j + 1) * shard] = jnp.where(core == 0, low, high)
            vec_ref[i : i + 1, half + j * shard : half + (j + 1) * shard] = jnp.where(
                core == 0, high, low
            )
    for copy in moves:
        copy.wait()


def forward_kernel(
    rows_ref,
    other_ref,
    part_ref,
    vec_ref,
    w_ref,
    b_ref,
    wout_ref,
    slope_ref,
    hidden_ref,
    through_ref,
    stat_ref,
    mixed_ref,
    normed_ref,
):
    half, rows = other_ref.shape
    channels, hidden = w_ref.shape
    images, shard = mixed_ref.shape[1:]
    positions = rows // images
    step = 256
    first, second = part_ref[0:1, :], part_ref[1:2, :]
    for c in range(half // step):
        value = other_ref[c * step : (c + 1) * step, :].astype(f32)
        first = first + jnp.sum(value, axis=0, keepdims=True)
        second = second + jnp.sum(value * value, axis=0, keepdims=True)
    average = first / channels
    inverse = lax.rsqrt(second / channels - average * average + eps)
    lane = iota((8, rows), 0)
    stat_ref[...] = jnp.where(lane == 0, average, jnp.where(lane == 1, inverse, 0.0))
    turned = stat_ref[...].T
    average = jnp.broadcast_to(turned[:, 0:1], (rows, step))
    inverse = jnp.broadcast_to(turned[:, 1:2], (rows, step))
    for c in range(channels // step):
        at = slice(c * step, (c + 1) * step)
        if c * step < half:
            value = rows_ref[:, at]
        else:
            value = other_ref[c * step - half : (c + 1) * step - half, :].T
        value = (value.astype(f32) - average) * inverse
        normed_ref[0:rows, at] = (value * vec_ref[0:1, at] + vec_ref[1:2, at]).astype(bf16)
    normed_ref[rows : rows + 16, :] = jnp.concatenate(to_terms(vec_ref[...]), axis=0).astype(bf16)
    b_row = b_ref[...][None, :]
    for t in range(hidden // step):
        at = slice(t * step, (t + 1) * step)
        product = jnp.dot(normed_ref[...], w_ref[:, at], preferred_element_type=f32)
        through_ref[:, at] = product[rows:]
        pre = product[:rows] + b_row[:, at]
        hidden_ref[:, at] = pre
        gate = 0.5 + 0.5 * lax.erf(pre * root_half)
        slope_ref[:, at] = gate + pre * jnp.exp(-0.5 * pre * pre) * inv_root_two_pi
        active = pre * gate
        sums = [
            jnp.sum(active[n * positions : (n + 1) * positions], axis=0, keepdims=True) / positions
            for n in range(images)
        ]
        sums = jnp.concatenate(sums + [jnp.zeros((8 - images, step), f32)], axis=0)
        high, low = to_terms(sums)
        part = jnp.dot(
            jnp.concatenate([high, low], axis=0).astype(bf16),
            wout_ref[at, :],
            preferred_element_type=f32,
        )
        part = part[:8] + part[8:]
        mixed = part if t == 0 else mixed + part
    for k in range(BLOCKS):
        mixed_ref[k] = mixed[:images, k * shard : (k + 1) * shard]


def head_kernel(
    got_ref, mean_ref, scale_ref, bout_ref, gain_ref, bias_ref, project_ref, out_ref, pooled_ref
):
    images, shard = got_ref.shape[1:]
    width = project_ref.shape[1]
    mixed = got_ref[0]
    for j in range(1, BLOCKS):
        mixed = mixed + got_ref[j]
    scale, bias_out = scale_ref[...], bout_ref[...]
    gain, bias = gain_ref[...], bias_ref[...]
    pooled = mean_ref[...] + scale * (mixed + bias_out)
    pooled_ref[...] = pooled
    head = jnp.concatenate([pooled, scale, bias_out, gain, bias], axis=0)
    first = jnp.sum(head, axis=1, keepdims=True)
    second = jnp.sum(head * head, axis=1, keepdims=True)
    value = jnp.where(iota((8, shard), 0) < images, head * gain, head)
    high, rest = to_terms(value)
    middle, low = to_terms(rest)
    product = jnp.dot(
        jnp.concatenate([high, middle, low], axis=0).astype(bf16),
        project_ref[...],
        preferred_element_type=f32,
    )
    out_ref[:, :width] = product[:8] + (product[8:16] + product[16:])
    lane = iota((8, 128), 1)
    out_ref[:, width : width + 128] = jnp.where(
        lane == 0, first, jnp.where(lane == 1, second, 0.0)
    )


def pair_sum_kernel(mine_ref, other_ref, out_ref):
    block = mine_ref[...] + other_ref[...]
    for j in range(CHIPS):
        out_ref[j] = block


def embed_kernel(got_ref, text_ref, tail_ref, out_ref, own_ref, back_ref, stat_ref):
    width = text_ref.shape[1]
    channels = BLOCKS * SHARD
    sums = got_ref[0]
    for j in range(1, CHIPS):
        sums = sums + got_ref[j]
    mean = sums[:, width : width + 1] / channels
    inverse = lax.rsqrt(sums[:, width + 1 : width + 2] / channels - mean * mean + eps)
    centred = inverse * (sums[:, :width] - mean * sums[6:7, :width])
    emb = centred + sums[7:8, :width]
    back_ref[...] = jnp.concatenate([centred[:4], sums[4:, :width]], axis=0)
    tail = tail_ref[...]
    block = jnp.concatenate([emb[:4], text_ref[...]], axis=0)
    own_ref[...] = block
    half = width // 2
    block = jnp.concatenate([block[:, :half], block[:, half:]], axis=0).astype(bf16)
    tail = jnp.concatenate([tail, tail], axis=0).astype(bf16)
    for d in range(out_ref.shape[0]):
        out_ref[d, :, :half] = block
        out_ref[d, :, half:] = tail
    stat_ref[0] = jnp.broadcast_to(mean, (8, 128))
    stat_ref[1] = jnp.broadcast_to(inverse, (8, 128))


def loss_kernel(
    got_ref,
    own_ref,
    rows_ref,
    stat_ref,
    pooled_ref,
    scale_ref,
    gain_ref,
    project_ref,
    text_ref,
    block_ref,
    mixed_ref,
    both_ref,
):
    width = project_ref.shape[1]
    count = got_ref.shape[0] * 8
    home = pl.ds(pl.multiple_of(lax.axis_index("dp") * 8, 8), 8)
    half = width // 2
    got = got_ref[...].astype(f32)
    raw = jnp.concatenate(
        [got[:, :8, :half].reshape(count, half), got[:, 8:, :half].reshape(count, half)], axis=1
    )
    unit = raw / jnp.sqrt(jnp.sum(raw * raw, axis=1, keepdims=True) + eps)
    logits = logit_scale * lax.dot_general(
        unit, unit, (((1,), (1,)), ((), ())), precision=highest, preferred_element_type=f32
    )
    column = iota((count, count), 1)
    valid = (iota((count, count), 0) % 8 < 4) & (column % 8 >= 4)
    weights = jnp.where(valid, jnp.exp(jnp.where(valid, logits, 0.0)), 0.0)
    row_total = jnp.sum(weights, axis=1, keepdims=True)
    col_total = jnp.sum(weights, axis=0, keepdims=True)
    target = got[:, :8, half:].reshape(count, 128)[:, 0:1]
    matched = jnp.where(target == column.astype(f32), 1.0, 0.0)
    grads = loss_scale * (0.5 * (weights / row_total + weights / col_total) - matched)
    grads = jnp.where(valid, grads, 0.0)
    both_ref[...] = grads + grads.T
    grad_unit = logit_scale * jnp.dot(
        both_ref[home, :], unit, precision=highest, preferred_element_type=f32
    )
    own = own_ref[...]
    length = jnp.sqrt(jnp.sum(own * own, axis=1, keepdims=True) + eps)
    own = own / length
    grad = (grad_unit - own * jnp.sum(own * grad_unit, axis=1, keepdims=True)) / length
    text_ref[...] = grad[4:]
    grad = grad[:4].astype(bf16)
    back = lax.dot_general(
        jnp.concatenate([grad, jnp.zeros_like(grad)], axis=0),
        project_ref[...],
        (((1,), (1,)), ((), ())),
        preferred_element_type=f32,
    )[:4]
    channels = BLOCKS * SHARD
    grad = grad.astype(f32)
    first = jnp.sum(grad * rows_ref[6:7, :], axis=1, keepdims=True) / channels
    second = jnp.sum(grad * rows_ref[:4, :], axis=1, keepdims=True) / channels
    mean, inverse = stat_ref[0][:4, 0:1], stat_ref[1][:4, 0:1]
    centred = (pooled_ref[...] - mean) * inverse
    block = (inverse / POSITIONS) * (back * gain_ref[...] - first - centred * second)
    block_ref[...] = block
    for k in range(BLOCKS):
        mixed_ref[k] = block * scale_ref[...]


def backward_kernel(
    got_ref,
    wout_ref,
    slope_ref,
    hidden_ref,
    w_ref,
    through_ref,
    b_ref,
    other_ref,
    turned_ref,
    sums_ref,
    mixed_ref,
    pre_ref,
):
    images, shard = got_ref.shape[1:]
    rows, hidden = slope_ref.shape
    channels = w_ref.shape[0]
    positions = rows // images
    mixed_ref[...] = jnp.zeros_like(mixed_ref)
    for k in range(BLOCKS):
        mixed_ref[0:images, k * shard : (k + 1) * shard] = got_ref[k]
    act = lax.dot_general(
        mixed_ref[...].astype(bf16),
        wout_ref[...],
        (((1,), (1,)), ((), ())),
        preferred_element_type=f32,
    )
    b_row = b_ref[...][None, :]
    step = 256
    one = jnp.zeros((rows, 1), f32)
    two = jnp.zeros((rows, 1), f32)
    for t in range(hidden // step):
        at = slice(t * step, (t + 1) * step)
        for n in range(images):
            span = slice(n * positions, (n + 1) * positions)
            pre_ref[span, :] = (act[n : n + 1, at] * slope_ref[span, at]).astype(bf16).astype(f32)
        value = pre_ref[...]
        gain = through_ref[0:1, at] + through_ref[8:9, at]
        bias = through_ref[1:2, at] + through_ref[9:10, at] + b_row[:, at]
        one = one + jnp.sum(value * gain, axis=1, keepdims=True)
        two = two + jnp.sum(value * (hidden_ref[:, at] - bias), axis=1, keepdims=True)
        turned_ref[at, :] = value.T.astype(bf16)
    lane = iota((rows, 128), 1)
    sums = jnp.where(lane == 0, one, jnp.where(lane == 1, two, 0.0)).T[:8]
    sums_ref[...] = sums
    high, low = to_terms(sums)
    other_ref[channels // 2 :, :] = jnp.concatenate([high, low], axis=0).astype(bf16)
    half = channels // 2
    for c in range(half // step):
        other_ref[c * step : (c + 1) * step, :] = jnp.dot(
            w_ref[half + c * step : half + (c + 1) * step, :],
            turned_ref[...],
            preferred_element_type=f32,
        ).astype(bf16)


def mine_kernel(w_ref, turned_ref, mine_ref):
    step = 256
    for c in range(mine_ref.shape[0] // step):
        at = slice(c * step, (c + 1) * step)
        mine_ref[at, :] = jnp.dot(
            w_ref[at, :], turned_ref[...], preferred_element_type=f32
        ).astype(bf16)


def pair_kernel(mine_ref, got_ref, sums_ref, out_ref):
    half = mine_ref.shape[0]
    shard = half // CHIPS
    for j in range(CHIPS):
        span = slice(j * shard, (j + 1) * shard)
        out_ref[j, :shard, :] = (mine_ref[span, :].astype(f32) + got_ref[span, :].astype(f32)).astype(
            bf16
        )
    tail = got_ref[half:, :].astype(f32)
    high, low = to_terms(sums_ref[...] + (tail[:8] + tail[8:]))
    tail = jnp.concatenate([high, low], axis=0).astype(bf16)
    for j in range(CHIPS):
        out_ref[j, shard:, :] = tail


def final_kernel(got_ref, conv_ref, stat_ref, gain_ref, w_ref, block_ref, out_ref, rows_ref):
    shard = conv_ref.shape[0]
    channels = shard * BLOCKS
    index = lax.axis_index("mp")
    pair = gain_ref[:, pl.ds(pl.multiple_of(index // 2 * 2 * shard, 128), 2 * shard)]
    gain = jnp.where(index % 2 == 0, pair[:, :shard], pair[:, shard:])
    gain = jnp.broadcast_to(gain, (8, shard)).T[:, 0:1]
    images, side = out_ref.shape[:2]
    positions = side * side
    total = got_ref[0].astype(f32)
    for j in range(1, CHIPS):
        total = total + got_ref[j].astype(f32)
    first = (total[shard : shard + 1] + total[shard + 8 : shard + 9]) / channels
    second = (total[shard + 1 : shard + 2] + total[shard + 9 : shard + 10]) / channels
    average, inverse = stat_ref[0:1, :], stat_ref[1:2, :]
    centred = (conv_ref[...].astype(f32) - average) * inverse
    grad = inverse * (total[:shard] * gain - first - centred * second)
    rows_ref[...] = grad.T

    def image(n, carry):
        span = pl.ds(pl.multiple_of(n * positions, positions), positions)
        x = rows_ref[span, :].reshape(side, side, shard)
        base = block_ref[pl.ds(n, 1), :]
        for p, row in enumerate(taps(x, w_ref, True)):
            out_ref[n, p] = row + base
        return carry

    lax.fori_loop(0, images, image, 0)


def body(
    x_in,
    dw_weight,
    dw_bias,
    ln_gain,
    ln_bias,
    w_in,
    b_in,
    w_out,
    b_out,
    layer_scale,
    head_gain,
    head_bias,
    projection,
    text_emb,
    labels,
):
    images, side, _, shard = x_in.shape
    channels, hidden = w_in.shape
    rows = images * side * side
    pairs, width = text_emb.shape
    shards = lax.axis_size("dp")
    (tail,) = run(start_kernel, [shape(8, 128)], labels, flops=START_FLOPS)
    copies, conv, input_mean = run(
        conv_kernel,
        [
            shape(CHIPS, shard, rows, dtype=bf16),
            shape(shard, rows, dtype=bf16),
            shape(images, shard),
        ],
        Far(tail),
        Far(x_in),
        Far(dw_weight),
        Far(dw_bias[None, :]),
        scratch=[
            pltpu.VMEM(x_in.shape, bf16),
            pltpu.VMEM(dw_weight.shape, f32),
            pltpu.VMEM((1, shard), f32),
            pltpu.VMEM((rows, shard), f32),
            pltpu.SemaphoreType.DMA((3,)),
        ],
        limit=CONV_LIMIT,
        flops=CONV_FLOPS,
    )
    conv_mine = chip_exchange(copies)
    conv_other = core_swap(conv_mine)
    conv_mine = conv_mine.reshape(channels // 2, rows)
    conv_other = conv_other.reshape(channels // 2, rows)
    own_rows, part, vec, w_own = run(
        ready_kernel,
        [
            shape(rows, channels // 2, dtype=bf16),
            shape(8, rows),
            shape(8, channels),
            shape(channels, hidden, dtype=bf16),
        ],
        conv_mine,
        ln_gain[None, :],
        ln_bias[None, :],
        w_in,
        scratch=[pltpu.SemaphoreType.DMA((BLOCKS,))],
    )
    slope, hidden_pre, through, row_stat, mixed = run(
        forward_kernel,
        [
            shape(rows, hidden),
            shape(rows, hidden),
            shape(16, hidden),
            shape(8, rows),
            shape(BLOCKS, images, shard),
        ],
        own_rows,
        conv_other,
        part,
        vec,
        w_own,
        b_in,
        w_out,
        scratch=[pltpu.VMEM((rows + 16, channels), bf16)],
        flops=2 * rows * channels * hidden,
    )
    sums, pooled = run(
        head_kernel,
        [shape(8, width + 128), shape(images, shard)],
        shard_exchange(mixed),
        input_mean,
        layer_scale[None, :],
        b_out[None, :],
        head_gain[None, :],
        head_bias[None, :],
        projection,
    )
    (blocks,) = run(
        pair_sum_kernel, [shape(CHIPS, 8, width + 128)], sums, core_swap(sums)
    )
    pair_block, own_block, back_rows, head_stat = run(
        embed_kernel,
        [
            shape(shards, 16, width // 2 + 128, dtype=bf16),
            shape(8, width),
            shape(8, width),
            shape(2, 8, 128),
        ],
        chip_exchange(blocks),
        text_emb,
        tail,
    )
    grad_text, grad_block, mixed_block = run(
        loss_kernel,
        [shape(pairs, width), shape(images, shard), shape(BLOCKS, images, shard)],
        lax.all_to_all(pair_block, "dp", 0, 0),
        own_block,
        back_rows,
        head_stat,
        pooled,
        layer_scale[None, :],
        head_gain[None, :],
        projection,
        scratch=[pltpu.VMEM((shards * 8, shards * 8), f32)],
    )
    other, turned, row_sums = run(
        backward_kernel,
        [
            shape(channels // 2 + 16, rows, dtype=bf16),
            shape(hidden, rows, dtype=bf16),
            shape(8, rows),
        ],
        shard_exchange(mixed_block),
        w_out,
        slope,
        hidden_pre,
        w_own,
        through,
        b_in,
        scratch=[pltpu.VMEM((8, channels), f32), pltpu.VMEM((rows, 256), f32)],
        flops=rows * channels * hidden,
    )
    passed = core_swap(other)
    (mine,) = run(
        mine_kernel,
        [shape(channels // 2, rows, dtype=bf16)],
        w_own,
        turned,
        flops=rows * channels * hidden,
    )
    (blocks,) = run(
        pair_kernel, [shape(CHIPS, shard + 16, rows, dtype=bf16)], mine, passed, row_sums
    )
    (grad_input,) = run(
        final_kernel,
        [shape(images, side, side, shard)],
        chip_exchange(blocks),
        conv,
        row_stat,
        ln_gain[None, :],
        dw_weight,
        grad_block,
        scratch=[pltpu.VMEM((rows, shard), f32)],
        flops=2 * 49 * rows * shard,
    )
    return (grad_input, grad_text)


def solution(mesh):
    return jax.shard_map(
        body,
        mesh=mesh,
        in_specs=(
            P("dp", None, None, "mp"),
            P(None, None, "mp"),
            P("mp"),
            P(),
            P(),
            P(None, "mp"),
            P("mp"),
            P("mp", None),
            P("mp"),
            P("mp"),
            P("mp"),
            P("mp"),
            P("mp", None),
            P("dp", None),
            P("dp"),
        ),
        out_specs=(P("dp", None, None, "mp"), P("dp", None)),
        check_vma=False,
    )
```

```python
import jax
import jax.numpy as jnp
from jax import lax
from jax.experimental import pallas as pl
from jax.experimental.pallas import tpu as pltpu
from jax.sharding import PartitionSpec as P

eps = 1e-06
logit_scale = 20.0
loss_scale = 512.0
root_half = 0.7071067811865476
inv_root_two_pi = 0.3989422804014327
f32 = jnp.float32
bf16 = jnp.bfloat16
MIB = 1 << 20
CONV_LIMIT = 50 * MIB
CONV_FLOPS = 16 * 10**9
START_FLOPS = 4 * 10**9
CHIPS = 8
BLOCKS = 16
SHARD = 192
POSITIONS = 64


def core_swap(array):
    return lax.ppermute(array, "mp", [(i, i ^ 1) for i in range(BLOCKS)])


def chip_exchange(array):
    groups = [[i for i in range(core, BLOCKS, 2)] for core in range(2)]
    return lax.all_to_all(array, "mp", 0, 0, axis_index_groups=groups)


def shard_exchange(array):
    return lax.all_to_all(array, "mp", 0, 0)


class Far:
    def __init__(self, array):
        self.array = array


def run(kernel, outs, *operands, scratch=(), limit=24 * MIB, flops=0):
    def spec(a):
        if isinstance(a, Far):
            return pl.BlockSpec(memory_space=pltpu.HBM)
        return pl.BlockSpec(memory_space=pltpu.SMEM if a.dtype == jnp.int32 else pltpu.VMEM)

    arrays = [a.array if isinstance(a, Far) else a for a in operands]
    return pl.pallas_call(
        kernel,
        out_shape=[a.array if isinstance(a, Far) else a for a in outs],
        in_specs=[spec(a) for a in operands],
        out_specs=[
            pl.BlockSpec(memory_space=pltpu.HBM if isinstance(a, Far) else pltpu.VMEM)
            for a in outs
        ],
        scratch_shapes=list(scratch),
        compiler_params=pltpu.CompilerParams(vmem_limit_bytes=limit),
        cost_estimate=pl.CostEstimate(
            flops=flops,
            bytes_accessed=sum(a.size * a.dtype.itemsize for a in arrays),
            transcendentals=0,
        ),
    )(*arrays)


def shape(*dims, dtype=f32):
    return jax.ShapeDtypeStruct(dims, dtype)


def iota(dims, axis):
    return lax.broadcasted_iota(jnp.int32, dims, axis)


def to_terms(array):
    high = array.astype(bf16).astype(f32)
    return high, array - high


def taps(x, w_ref, flip):
    side, _, shard = x.shape
    size = w_ref.shape[0]
    reach = size // 2
    column = iota((side, side, shard), 1)
    acc = [jnp.zeros((side, shard), f32) for _ in range(side)]
    for b in range(size):
        by = b - reach
        if by:
            moved = jnp.where(
                (column + by >= 0) & (column + by < side), pltpu.roll(x, (-by) % side, 1), 0.0
            )
        else:
            moved = x
        for a in range(size):
            wa, wb = (size - 1 - a, size - 1 - b) if flip else (a, b)
            weight = w_ref[wa, wb : wb + 1, :]
            for p in range(side):
                if 0 <= p + a - reach < side:
                    acc[p] = acc[p] + moved[p + a - reach] * weight
    return acc


def start_kernel(out_ref):
    out_ref[...] = jnp.zeros_like(out_ref)


def conv_kernel(
    _, x_far, dw_far, bias_far, copies_ref, conv_ref, mean_ref, x_ref, dw_ref, bias_ref, rows_ref, sems
):
    images, side = x_ref.shape[:2]
    positions = side * side
    loads = ((x_far, x_ref), (dw_far, dw_ref), (bias_far, bias_ref))
    loads = [pltpu.make_async_copy(far, near, sems.at[i]) for i, (far, near) in enumerate(loads)]
    for copy in loads:
        copy.start()
    for copy in loads:
        copy.wait()

    def image(n, carry):
        x = x_ref[n].astype(f32)
        total = jnp.sum(jnp.sum(x, axis=0), axis=0, keepdims=True)
        mean_ref[pl.ds(n, 1), :] = total / positions
        for p, row in enumerate(taps(x, dw_ref, False)):
            rows_ref[pl.ds(pl.multiple_of(n * positions + p * side, side), side), :] = row
        return carry

    lax.fori_loop(0, images, image, 0)
    turned = (rows_ref[...] + bias_ref[...]).T.astype(bf16)
    conv_ref[...] = turned
    for j in range(CHIPS):
        copies_ref[j] = turned


def ready_kernel(
    mine_ref, gain_ref, bias_ref, w_ref, labels_ref, rows_ref, part_ref, vec_ref, own_ref, tail_ref, sems
):
    shard = w_ref.shape[0] // BLOCKS
    core = lax.axis_index("mp") % 2
    moves = []
    for k in range(BLOCKS):
        place = 2 * (k % CHIPS) + (core if k < CHIPS else 1 - core)
        source = pl.ds(pl.multiple_of(place * shard, 64), shard)
        moves.append(
            pltpu.make_async_copy(
                w_ref.at[source], own_ref.at[k * shard : (k + 1) * shard], sems.at[k]
            )
        )
    for copy in moves:
        copy.start()
    half, rows = mine_ref.shape
    step = 256
    first = jnp.zeros((1, rows), f32)
    second = jnp.zeros((1, rows), f32)
    for c in range(half // step):
        at = slice(c * step, (c + 1) * step)
        rows_ref[:, at] = mine_ref[at, :].T
        value = mine_ref[at, :].astype(f32)
        first = first + jnp.sum(value, axis=0, keepdims=True)
        second = second + jnp.sum(value * value, axis=0, keepdims=True)
    part_ref[0:1, :] = first
    part_ref[1:2, :] = second
    vec_ref[...] = jnp.zeros_like(vec_ref)
    for i, ref in enumerate((gain_ref, bias_ref)):
        for j in range(CHIPS):
            low = ref[:, 2 * j * shard : (2 * j + 1) * shard]
            high = ref[:, (2 * j + 1) * shard : (2 * j + 2) * shard]
            vec_ref[i : i + 1, j * shard : (j + 1) * shard] = jnp.where(core == 0, low, high)
            vec_ref[i : i + 1, half + j * shard : half + (j + 1) * shard] = jnp.where(
                core == 0, high, low
            )
    pairs = labels_ref.shape[0]
    row = iota((8, 128), 0)
    tail = jnp.zeros((8, 128), f32)
    for r in range(pairs):
        label = labels_ref[r]
        target = (label // pairs) * 8 + 4 + label % pairs
        tail = jnp.where(row == r, target.astype(f32), tail)
    tail_ref[...] = tail
    for copy in moves:
        copy.wait()


def forward_kernel(
    rows_ref,
    other_ref,
    part_ref,
    vec_ref,
    w_ref,
    b_ref,
    wout_ref,
    slope_ref,
    hidden_ref,
    through_ref,
    stat_ref,
    mixed_ref,
    normed_ref,
):
    half, rows = other_ref.shape
    channels, hidden = w_ref.shape
    images, shard = mixed_ref.shape[1:]
    positions = rows // images
    step = 256
    first, second = part_ref[0:1, :], part_ref[1:2, :]
    for c in range(half // step):
        value = other_ref[c * step : (c + 1) * step, :].astype(f32)
        first = first + jnp.sum(value, axis=0, keepdims=True)
        second = second + jnp.sum(value * value, axis=0, keepdims=True)
    average = first / channels
    inverse = lax.rsqrt(second / channels - average * average + eps)
    lane = iota((8, rows), 0)
    stat_ref[...] = jnp.where(lane == 0, average, jnp.where(lane == 1, inverse, 0.0))
    turned = stat_ref[...].T
    average = jnp.broadcast_to(turned[:, 0:1], (rows, step))
    inverse = jnp.broadcast_to(turned[:, 1:2], (rows, step))
    for c in range(channels // step):
        at = slice(c * step, (c + 1) * step)
        if c * step < half:
            value = rows_ref[:, at]
        else:
            value = other_ref[c * step - half : (c + 1) * step - half, :].T
        value = (value.astype(f32) - average) * inverse
        normed_ref[0:rows, at] = (value * vec_ref[0:1, at] + vec_ref[1:2, at]).astype(bf16)
    normed_ref[rows : rows + 16, :] = jnp.concatenate(to_terms(vec_ref[...]), axis=0).astype(bf16)
    b_row = b_ref[...][None, :]
    whole = jnp.dot(normed_ref[...], w_ref[...], preferred_element_type=f32)
    for t in range(hidden // step):
        at = slice(t * step, (t + 1) * step)
        product = whole[:, at]
        through_ref[:, at] = product[rows:]
        pre = product[:rows] + b_row[:, at]
        hidden_ref[:, at] = pre
        gate = 0.5 + 0.5 * lax.erf(pre * root_half)
        slope_ref[:, at] = gate + pre * jnp.exp(-0.5 * pre * pre) * inv_root_two_pi
        active = pre * gate
        sums = [
            jnp.sum(active[n * positions : (n + 1) * positions], axis=0, keepdims=True) / positions
            for n in range(images)
        ]
        sums = jnp.concatenate(sums + [jnp.zeros((8 - images, step), f32)], axis=0)
        high, low = to_terms(sums)
        part = jnp.dot(
            jnp.concatenate([high, low], axis=0).astype(bf16),
            wout_ref[at, :],
            preferred_element_type=f32,
        )
        part = part[:8] + part[8:]
        mixed = part if t == 0 else mixed + part
    for k in range(BLOCKS):
        mixed_ref[k] = mixed[:images, k * shard : (k + 1) * shard]


def head_kernel(
    got_ref, mean_ref, scale_ref, bout_ref, gain_ref, bias_ref, project_ref, out_ref, pooled_ref
):
    images, shard = got_ref.shape[1:]
    width = project_ref.shape[1]
    mixed = got_ref[0]
    for j in range(1, BLOCKS):
        mixed = mixed + got_ref[j]
    scale, bias_out = scale_ref[...], bout_ref[...]
    gain, bias = gain_ref[...], bias_ref[...]
    pooled = mean_ref[...] + scale * (mixed + bias_out)
    pooled_ref[...] = pooled
    head = jnp.concatenate([pooled, scale, bias_out, gain, bias], axis=0)
    first = jnp.sum(head, axis=1, keepdims=True)
    second = jnp.sum(head * head, axis=1, keepdims=True)
    value = jnp.where(iota((8, shard), 0) < images, head * gain, head)
    high, rest = to_terms(value)
    middle, low = to_terms(rest)
    product = jnp.dot(
        jnp.concatenate([high, middle, low], axis=0).astype(bf16),
        project_ref[...],
        preferred_element_type=f32,
    )
    out_ref[:, :width] = product[:8] + (product[8:16] + product[16:])
    lane = iota((8, 128), 1)
    out_ref[:, width : width + 128] = jnp.where(
        lane == 0, first, jnp.where(lane == 1, second, 0.0)
    )


def pair_sum_kernel(mine_ref, other_ref, out_ref):
    block = mine_ref[...] + other_ref[...]
    for j in range(CHIPS):
        out_ref[j] = block


def embed_kernel(got_ref, text_ref, tail_ref, out_ref, own_ref, back_ref, stat_ref):
    width = text_ref.shape[1]
    channels = BLOCKS * SHARD
    sums = got_ref[0]
    for j in range(1, CHIPS):
        sums = sums + got_ref[j]
    mean = sums[:, width : width + 1] / channels
    inverse = lax.rsqrt(sums[:, width + 1 : width + 2] / channels - mean * mean + eps)
    centred = inverse * (sums[:, :width] - mean * sums[6:7, :width])
    emb = centred + sums[7:8, :width]
    back_ref[...] = jnp.concatenate([centred[:4], sums[4:, :width]], axis=0)
    tail = tail_ref[...]
    block = jnp.concatenate([emb[:4], text_ref[...]], axis=0)
    own_ref[...] = block
    half = width // 2
    block = jnp.concatenate([block[:, :half], block[:, half:]], axis=0).astype(bf16)
    tail = jnp.concatenate([tail, tail], axis=0).astype(bf16)
    for d in range(out_ref.shape[0]):
        out_ref[d, :, :half] = block
        out_ref[d, :, half:] = tail
    stat_ref[0] = jnp.broadcast_to(mean, (8, 128))
    stat_ref[1] = jnp.broadcast_to(inverse, (8, 128))


def loss_kernel(
    got_ref,
    own_ref,
    rows_ref,
    stat_ref,
    pooled_ref,
    scale_ref,
    gain_ref,
    project_ref,
    text_far,
    block_ref,
    mixed_ref,
    both_ref,
    text_ref,
    sem,
):
    width = project_ref.shape[1]
    count = got_ref.shape[0] * 8
    home = pl.ds(pl.multiple_of(lax.axis_index("dp") * 8, 8), 8)
    half = width // 2
    got = got_ref[...].astype(f32)
    raw = jnp.concatenate(
        [got[:, :8, :half].reshape(count, half), got[:, 8:, :half].reshape(count, half)], axis=1
    ).astype(bf16)
    product = lax.dot_general(raw, raw, (((1,), (1,)), ((), ())), preferred_element_type=f32)
    same = iota((count, count), 0) == iota((count, count), 1)
    square = jnp.where(same, product, 0.0)
    row_len = jnp.sqrt(jnp.sum(square, axis=1, keepdims=True) + eps)
    col_len = jnp.sqrt(jnp.sum(square, axis=0, keepdims=True) + eps)
    logits = logit_scale * (product / (row_len * col_len))
    column = iota((count, count), 1)
    valid = (iota((count, count), 0) % 8 < 4) & (column % 8 >= 4)
    weights = jnp.where(valid, jnp.exp(jnp.where(valid, logits, 0.0)), 0.0)
    row_total = jnp.sum(weights, axis=1, keepdims=True)
    col_total = jnp.sum(weights, axis=0, keepdims=True)
    target = got[:, :8, half:].reshape(count, 128)[:, 0:1]
    matched = jnp.where(target == column.astype(f32), 1.0, 0.0)
    grads = loss_scale * (0.5 * (weights / row_total + weights / col_total) - matched)
    grads = jnp.where(valid, grads, 0.0)
    both_ref[...] = (grads + grads.T) / col_len
    high, rest = to_terms(both_ref[home, :])
    middle, low = to_terms(rest)
    grad_unit = jnp.dot(
        jnp.concatenate([high, middle, low], axis=0).astype(bf16), raw, preferred_element_type=f32
    )
    grad_unit = logit_scale * (grad_unit[:8] + (grad_unit[8:16] + grad_unit[16:]))
    own = own_ref[...]
    length = jnp.sqrt(jnp.sum(own * own, axis=1, keepdims=True) + eps)
    own = own / length
    grad = (grad_unit - own * jnp.sum(own * grad_unit, axis=1, keepdims=True)) / length
    text_ref[...] = grad[4:]
    send = pltpu.make_async_copy(text_ref, text_far, sem)
    send.start()
    grad = grad[:4].astype(bf16)
    back = lax.dot_general(
        jnp.concatenate([grad, jnp.zeros_like(grad)], axis=0),
        project_ref[...],
        (((1,), (1,)), ((), ())),
        preferred_element_type=f32,
    )[:4]
    channels = BLOCKS * SHARD
    grad = grad.astype(f32)
    first = jnp.sum(grad * rows_ref[6:7, :], axis=1, keepdims=True) / channels
    second = jnp.sum(grad * rows_ref[:4, :], axis=1, keepdims=True) / channels
    mean, inverse = stat_ref[0][:4, 0:1], stat_ref[1][:4, 0:1]
    centred = (pooled_ref[...] - mean) * inverse
    block = (inverse / POSITIONS) * (back * gain_ref[...] - first - centred * second)
    block_ref[...] = block
    for k in range(BLOCKS):
        mixed_ref[k] = block * scale_ref[...]
    send.wait()


def backward_kernel(
    got_ref,
    wout_ref,
    slope_ref,
    hidden_ref,
    w_ref,
    through_ref,
    b_ref,
    other_ref,
    turned_ref,
    sums_ref,
    mixed_ref,
    pre_ref,
):
    images, shard = got_ref.shape[1:]
    rows, hidden = slope_ref.shape
    channels = w_ref.shape[0]
    positions = rows // images
    mixed_ref[...] = jnp.zeros_like(mixed_ref)
    for k in range(BLOCKS):
        mixed_ref[0:images, k * shard : (k + 1) * shard] = got_ref[k]
    act = lax.dot_general(
        mixed_ref[...].astype(bf16),
        wout_ref[...],
        (((1,), (1,)), ((), ())),
        preferred_element_type=f32,
    )
    b_row = b_ref[...][None, :]
    step = 256
    one = jnp.zeros((rows, 1), f32)
    two = jnp.zeros((rows, 1), f32)
    for t in range(hidden // step):
        at = slice(t * step, (t + 1) * step)
        for n in range(images):
            span = slice(n * positions, (n + 1) * positions)
            pre_ref[span, :] = (act[n : n + 1, at] * slope_ref[span, at]).astype(bf16).astype(f32)
        value = pre_ref[...]
        gain = through_ref[0:1, at] + through_ref[8:9, at]
        bias = through_ref[1:2, at] + through_ref[9:10, at] + b_row[:, at]
        one = one + jnp.sum(value * gain, axis=1, keepdims=True)
        two = two + jnp.sum(value * (hidden_ref[:, at] - bias), axis=1, keepdims=True)
        turned_ref[at, :] = value.T.astype(bf16)
    lane = iota((rows, 128), 1)
    sums = jnp.where(lane == 0, one, jnp.where(lane == 1, two, 0.0)).T[:8]
    sums_ref[...] = sums
    high, low = to_terms(sums)
    other_ref[channels // 2 :, :] = jnp.concatenate([high, low], axis=0).astype(bf16)
    half = channels // 2
    other_ref[:half, :] = jnp.dot(
        w_ref[half:, :], turned_ref[...], preferred_element_type=f32
    ).astype(bf16)


def mine_kernel(w_ref, turned_ref, mine_ref):
    mine_ref[...] = jnp.dot(
        w_ref[: mine_ref.shape[0], :], turned_ref[...], preferred_element_type=f32
    ).astype(bf16)


def pair_kernel(mine_ref, got_ref, sums_ref, out_ref):
    half = mine_ref.shape[0]
    shard = half // CHIPS
    for j in range(CHIPS):
        span = slice(j * shard, (j + 1) * shard)
        out_ref[j, :shard, :] = (mine_ref[span, :].astype(f32) + got_ref[span, :].astype(f32)).astype(
            bf16
        )
    tail = got_ref[half:, :].astype(f32)
    high, low = to_terms(sums_ref[...] + (tail[:8] + tail[8:]))
    tail = jnp.concatenate([high, low], axis=0).astype(bf16)
    for j in range(CHIPS):
        out_ref[j, shard:, :] = tail


def final_kernel(
    got_ref, conv_ref, stat_ref, gain_ref, w_ref, block_ref, out_far, rows_ref, out_ref, sems
):
    shard = conv_ref.shape[0]
    channels = shard * BLOCKS
    index = lax.axis_index("mp")
    pair = gain_ref[:, pl.ds(pl.multiple_of(index // 2 * 2 * shard, 128), 2 * shard)]
    gain = jnp.where(index % 2 == 0, pair[:, :shard], pair[:, shard:])
    gain = jnp.broadcast_to(gain, (8, shard)).T[:, 0:1]
    images, side = out_ref.shape[:2]
    positions = side * side
    total = got_ref[0].astype(f32)
    for j in range(1, CHIPS):
        total = total + got_ref[j].astype(f32)
    first = (total[shard : shard + 1] + total[shard + 8 : shard + 9]) / channels
    second = (total[shard + 1 : shard + 2] + total[shard + 9 : shard + 10]) / channels
    average, inverse = stat_ref[0:1, :], stat_ref[1:2, :]
    centred = (conv_ref[...].astype(f32) - average) * inverse
    grad = inverse * (total[:shard] * gain - first - centred * second)
    rows_ref[...] = grad.T

    def image(n, carry):
        span = pl.ds(pl.multiple_of(n * positions, positions), positions)
        x = rows_ref[span, :].reshape(side, side, shard)
        base = block_ref[pl.ds(n, 1), :]
        for p, row in enumerate(taps(x, w_ref, True)):
            out_ref[n, p] = row + base
        pltpu.make_async_copy(out_ref.at[n], out_far.at[n], sems.at[n]).start()
        return carry

    lax.fori_loop(0, images, image, 0)
    for n in range(images):
        pltpu.make_async_copy(out_ref.at[n], out_far.at[n], sems.at[n]).wait()


def body(
    x_in,
    dw_weight,
    dw_bias,
    ln_gain,
    ln_bias,
    w_in,
    b_in,
    w_out,
    b_out,
    layer_scale,
    head_gain,
    head_bias,
    projection,
    text_emb,
    labels,
):
    images, side, _, shard = x_in.shape
    channels, hidden = w_in.shape
    rows = images * side * side
    pairs, width = text_emb.shape
    shards = lax.axis_size("dp")
    (begun,) = run(start_kernel, [shape(8, 128)], flops=START_FLOPS)
    copies, conv, input_mean = run(
        conv_kernel,
        [
            shape(CHIPS, shard, rows, dtype=bf16),
            shape(shard, rows, dtype=bf16),
            shape(images, shard),
        ],
        Far(begun),
        Far(x_in),
        Far(dw_weight),
        Far(dw_bias[None, :]),
        scratch=[
            pltpu.VMEM(x_in.shape, bf16),
            pltpu.VMEM(dw_weight.shape, f32),
            pltpu.VMEM((1, shard), f32),
            pltpu.VMEM((rows, shard), f32),
            pltpu.SemaphoreType.DMA((3,)),
        ],
        limit=CONV_LIMIT,
        flops=CONV_FLOPS,
    )
    conv_mine = chip_exchange(copies)
    conv_other = core_swap(conv_mine)
    conv_mine = conv_mine.reshape(channels // 2, rows)
    conv_other = conv_other.reshape(channels // 2, rows)
    own_rows, part, vec, w_own, tail = run(
        ready_kernel,
        [
            shape(rows, channels // 2, dtype=bf16),
            shape(8, rows),
            shape(8, channels),
            shape(channels, hidden, dtype=bf16),
            shape(8, 128),
        ],
        conv_mine,
        ln_gain[None, :],
        ln_bias[None, :],
        w_in,
        labels,
        scratch=[pltpu.SemaphoreType.DMA((BLOCKS,))],
    )
    slope, hidden_pre, through, row_stat, mixed = run(
        forward_kernel,
        [
            shape(rows, hidden),
            shape(rows, hidden),
            shape(16, hidden),
            shape(8, rows),
            shape(BLOCKS, images, shard),
        ],
        own_rows,
        conv_other,
        part,
        vec,
        w_own,
        b_in,
        w_out,
        scratch=[pltpu.VMEM((rows + 16, channels), bf16)],
        flops=2 * rows * channels * hidden,
    )
    sums, pooled = run(
        head_kernel,
        [shape(8, width + 128), shape(images, shard)],
        shard_exchange(mixed),
        input_mean,
        layer_scale[None, :],
        b_out[None, :],
        head_gain[None, :],
        head_bias[None, :],
        projection,
    )
    (blocks,) = run(
        pair_sum_kernel, [shape(CHIPS, 8, width + 128)], sums, core_swap(sums)
    )
    pair_block, own_block, back_rows, head_stat = run(
        embed_kernel,
        [
            shape(shards, 16, width // 2 + 128, dtype=bf16),
            shape(8, width),
            shape(8, width),
            shape(2, 8, 128),
        ],
        chip_exchange(blocks),
        text_emb,
        tail,
    )
    grad_text, grad_block, mixed_block = run(
        loss_kernel,
        [Far(shape(pairs, width)), shape(images, shard), shape(BLOCKS, images, shard)],
        lax.all_to_all(pair_block, "dp", 0, 0),
        own_block,
        back_rows,
        head_stat,
        pooled,
        layer_scale[None, :],
        head_gain[None, :],
        projection,
        scratch=[
            pltpu.VMEM((shards * 8, shards * 8), f32),
            pltpu.VMEM((pairs, width), f32),
            pltpu.SemaphoreType.DMA,
        ],
    )
    other, turned, row_sums = run(
        backward_kernel,
        [
            shape(channels // 2 + 16, rows, dtype=bf16),
            shape(hidden, rows, dtype=bf16),
            shape(8, rows),
        ],
        shard_exchange(mixed_block),
        w_out,
        slope,
        hidden_pre,
        w_own,
        through,
        b_in,
        scratch=[pltpu.VMEM((8, channels), f32), pltpu.VMEM((rows, 256), f32)],
        flops=rows * channels * hidden,
    )
    passed = core_swap(other)
    (mine,) = run(
        mine_kernel,
        [shape(channels // 2, rows, dtype=bf16)],
        w_own,
        turned,
        flops=rows * channels * hidden,
    )
    (blocks,) = run(
        pair_kernel, [shape(CHIPS, shard + 16, rows, dtype=bf16)], mine, passed, row_sums
    )
    (grad_input,) = run(
        final_kernel,
        [Far(shape(images, side, side, shard))],
        chip_exchange(blocks),
        conv,
        row_stat,
        ln_gain[None, :],
        dw_weight,
        grad_block,
        scratch=[
            pltpu.VMEM((rows, shard), f32),
            pltpu.VMEM((images, side, side, shard), f32),
            pltpu.SemaphoreType.DMA((images,)),
        ],
        flops=2 * 49 * rows * shard,
    )
    return (grad_input, grad_text)


def solution(mesh):
    return jax.shard_map(
        body,
        mesh=mesh,
        in_specs=(
            P("dp", None, None, "mp"),
            P(None, None, "mp"),
            P("mp"),
            P(),
            P(),
            P(None, "mp"),
            P("mp"),
            P("mp", None),
            P("mp"),
            P("mp"),
            P("mp"),
            P("mp"),
            P("mp", None),
            P("dp", None),
            P("dp"),
        ),
        out_specs=(P("dp", None, None, "mp"), P("dp", None)),
        check_vma=False,
    )
```

```python
import jax
import jax.numpy as jnp
from jax import lax
from jax.experimental import pallas as pl
from jax.experimental.pallas import tpu as pltpu
from jax.sharding import PartitionSpec as P

eps = 1e-06
logit_scale = 20.0
loss_scale = 512.0
root_half = 0.7071067811865476
inv_root_two_pi = 0.3989422804014327
f32 = jnp.float32
bf16 = jnp.bfloat16
MIB = 1 << 20
CONV_LIMIT = 50 * MIB
CONV_FLOPS = 16 * 10**9
START_FLOPS = 4 * 10**9
READY_FLOPS = 12 * 10**9
CHIPS = 8
BLOCKS = 16
SHARD = 192
POSITIONS = 64


def core_swap(array):
    return lax.ppermute(array, "mp", [(i, i ^ 1) for i in range(BLOCKS)])


def chip_exchange(array):
    groups = [[i for i in range(core, BLOCKS, 2)] for core in range(2)]
    return lax.all_to_all(array, "mp", 0, 0, axis_index_groups=groups)


def shard_exchange(array):
    return lax.all_to_all(array, "mp", 0, 0)


class Far:
    def __init__(self, array):
        self.array = array


def run(kernel, outs, *operands, scratch=(), limit=24 * MIB, flops=0):
    def spec(a):
        if isinstance(a, Far):
            return pl.BlockSpec(memory_space=pltpu.HBM)
        return pl.BlockSpec(memory_space=pltpu.SMEM if a.dtype == jnp.int32 else pltpu.VMEM)

    arrays = [a.array if isinstance(a, Far) else a for a in operands]
    return pl.pallas_call(
        kernel,
        out_shape=[a.array if isinstance(a, Far) else a for a in outs],
        in_specs=[spec(a) for a in operands],
        out_specs=[
            pl.BlockSpec(memory_space=pltpu.HBM if isinstance(a, Far) else pltpu.VMEM)
            for a in outs
        ],
        scratch_shapes=list(scratch),
        compiler_params=pltpu.CompilerParams(vmem_limit_bytes=limit),
        cost_estimate=pl.CostEstimate(
            flops=flops,
            bytes_accessed=sum(a.size * a.dtype.itemsize for a in arrays),
            transcendentals=0,
        ),
    )(*arrays)


def shape(*dims, dtype=f32):
    return jax.ShapeDtypeStruct(dims, dtype)


def iota(dims, axis):
    return lax.broadcasted_iota(jnp.int32, dims, axis)


def to_terms(array):
    high = array.astype(bf16).astype(f32)
    return high, array - high


def taps(x, w_ref, flip):
    side, _, shard = x.shape
    size = w_ref.shape[0]
    reach = size // 2
    column = iota((side, side, shard), 1)
    acc = [jnp.zeros((side, shard), f32) for _ in range(side)]
    for b in range(size):
        by = b - reach
        if by:
            moved = jnp.where(
                (column + by >= 0) & (column + by < side), pltpu.roll(x, (-by) % side, 1), 0.0
            )
        else:
            moved = x
        for a in range(size):
            wa, wb = (size - 1 - a, size - 1 - b) if flip else (a, b)
            weight = w_ref[wa, wb : wb + 1, :]
            for p in range(side):
                if 0 <= p + a - reach < side:
                    acc[p] = acc[p] + moved[p + a - reach] * weight
    return acc


def start_kernel(out_ref):
    out_ref[...] = jnp.zeros_like(out_ref)


def conv_kernel(
    _,
    scale_ref,
    bout_ref,
    gain_ref,
    shift_ref,
    x_far,
    dw_far,
    bias_far,
    copies_ref,
    conv_ref,
    head_ref,
    x_ref,
    dw_ref,
    bias_ref,
    rows_ref,
    sems,
):
    images, side = x_ref.shape[:2]
    positions = side * side
    loads = ((x_far, x_ref), (dw_far, dw_ref), (bias_far, bias_ref))
    loads = [pltpu.make_async_copy(far, near, sems.at[i]) for i, (far, near) in enumerate(loads)]
    for copy in loads:
        copy.start()
    for copy in loads:
        copy.wait()

    def image(n, carry):
        x = x_ref[n].astype(f32)
        total = jnp.sum(jnp.sum(x, axis=0), axis=0, keepdims=True)
        head_ref[pl.ds(n, 1), :] = total / positions
        for p, row in enumerate(taps(x, dw_ref, False)):
            rows_ref[pl.ds(pl.multiple_of(n * positions + p * side, side), side), :] = row
        return carry

    lax.fori_loop(0, images, image, 0)
    for i, ref in enumerate((scale_ref, bout_ref, gain_ref, shift_ref)):
        head_ref[images + i : images + i + 1, :] = ref[...]
    turned = (rows_ref[...] + bias_ref[...]).T.astype(bf16)
    conv_ref[...] = turned
    for j in range(CHIPS):
        copies_ref[j] = turned


def ready_kernel(
    mine_ref,
    gain_ref,
    bias_ref,
    w_ref,
    labels_ref,
    head_ref,
    project_far,
    rows_ref,
    part_ref,
    vec_ref,
    own_ref,
    tail_ref,
    head_out_ref,
    project_ref,
    sems,
):
    shard = w_ref.shape[0] // BLOCKS
    core = lax.axis_index("mp") % 2
    moves = []
    for k in range(BLOCKS):
        place = 2 * (k % CHIPS) + (core if k < CHIPS else 1 - core)
        source = pl.ds(pl.multiple_of(place * shard, 64), shard)
        moves.append(
            pltpu.make_async_copy(
                w_ref.at[source], own_ref.at[k * shard : (k + 1) * shard], sems.at[k]
            )
        )
    moves.append(pltpu.make_async_copy(project_far, project_ref, sems.at[BLOCKS]))
    for copy in moves:
        copy.start()
    head_out_ref[...] = head_ref[...]
    half, rows = mine_ref.shape
    step = 256
    first = jnp.zeros((1, rows), f32)
    second = jnp.zeros((1, rows), f32)
    for c in range(half // step):
        at = slice(c * step, (c + 1) * step)
        rows_ref[:, at] = mine_ref[at, :].T
        value = mine_ref[at, :].astype(f32)
        first = first + jnp.sum(value, axis=0, keepdims=True)
        second = second + jnp.sum(value * value, axis=0, keepdims=True)
    part_ref[0:1, :] = first
    part_ref[1:2, :] = second
    vec_ref[...] = jnp.zeros_like(vec_ref)
    for i, ref in enumerate((gain_ref, bias_ref)):
        for j in range(CHIPS):
            low = ref[:, 2 * j * shard : (2 * j + 1) * shard]
            high = ref[:, (2 * j + 1) * shard : (2 * j + 2) * shard]
            vec_ref[i : i + 1, j * shard : (j + 1) * shard] = jnp.where(core == 0, low, high)
            vec_ref[i : i + 1, half + j * shard : half + (j + 1) * shard] = jnp.where(
                core == 0, high, low
            )
    pairs = labels_ref.shape[0]
    row = iota((8, 128), 0)
    tail = jnp.zeros((8, 128), f32)
    for r in range(pairs):
        label = labels_ref[r]
        target = (label // pairs) * 8 + 4 + label % pairs
        tail = jnp.where(row == r, target.astype(f32), tail)
    tail_ref[...] = tail
    for copy in moves:
        copy.wait()


def forward_kernel(
    rows_ref,
    other_ref,
    part_ref,
    vec_ref,
    w_ref,
    b_ref,
    wout_ref,
    slope_ref,
    hidden_ref,
    through_ref,
    stat_ref,
    mixed_ref,
    normed_ref,
):
    half, rows = other_ref.shape
    channels, hidden = w_ref.shape
    images = rows // POSITIONS
    positions = POSITIONS
    step = 256
    first, second = part_ref[0:1, :], part_ref[1:2, :]
    for c in range(half // step):
        value = other_ref[c * step : (c + 1) * step, :].astype(f32)
        first = first + jnp.sum(value, axis=0, keepdims=True)
        second = second + jnp.sum(value * value, axis=0, keepdims=True)
    average = first / channels
    inverse = lax.rsqrt(second / channels - average * average + eps)
    lane = iota((8, rows), 0)
    stat_ref[...] = jnp.where(lane == 0, average, jnp.where(lane == 1, inverse, 0.0))
    turned = stat_ref[...].T
    average = jnp.broadcast_to(turned[:, 0:1], (rows, step))
    inverse = jnp.broadcast_to(turned[:, 1:2], (rows, step))
    for c in range(channels // step):
        at = slice(c * step, (c + 1) * step)
        if c * step < half:
            value = rows_ref[:, at]
        else:
            value = other_ref[c * step - half : (c + 1) * step - half, :].T
        value = (value.astype(f32) - average) * inverse
        normed_ref[0:rows, at] = (value * vec_ref[0:1, at] + vec_ref[1:2, at]).astype(bf16)
    normed_ref[rows : rows + 16, :] = jnp.concatenate(to_terms(vec_ref[...]), axis=0).astype(bf16)
    b_row = b_ref[...][None, :]
    whole = jnp.dot(normed_ref[...], w_ref[...], preferred_element_type=f32)
    for t in range(hidden // step):
        at = slice(t * step, (t + 1) * step)
        product = whole[:, at]
        through_ref[:, at] = product[rows:]
        pre = product[:rows] + b_row[:, at]
        hidden_ref[:, at] = pre
        gate = 0.5 + 0.5 * lax.erf(pre * root_half)
        slope_ref[:, at] = gate + pre * jnp.exp(-0.5 * pre * pre) * inv_root_two_pi
        active = pre * gate
        sums = [
            jnp.sum(active[n * positions : (n + 1) * positions], axis=0, keepdims=True) / positions
            for n in range(images)
        ]
        sums = jnp.concatenate(sums + [jnp.zeros((8 - images, step), f32)], axis=0)
        high, low = to_terms(sums)
        part = jnp.dot(
            jnp.concatenate([high, low], axis=0).astype(bf16),
            wout_ref[at, :],
            preferred_element_type=f32,
        )
        part = part[:8] + part[8:]
        mixed = part if t == 0 else mixed + part
    mixed_ref[...] = mixed


def block_kernel(mixed_ref, _head, _project, out_ref):
    shard = out_ref.shape[2]
    images = out_ref.shape[1] // 2
    for k in range(BLOCKS):
        block = mixed_ref[:images, k * shard : (k + 1) * shard]
        out_ref[k, :images, :] = block
        out_ref[k ^ 1, images:, :] = block


def head_kernel(
    got_ref, own_ref, other_ref, project_ref, project_other_ref, out_ref, pooled_ref
):
    images = pooled_ref.shape[0]
    width = project_ref.shape[1]
    mixed = got_ref[0]
    for j in range(1, BLOCKS):
        mixed = mixed + got_ref[j]
    first = jnp.zeros((8, 1), f32)
    second = jnp.zeros((8, 1), f32)
    product = jnp.zeros((24, width), f32)
    sides = ((own_ref, project_ref, mixed[:images]), (other_ref, project_other_ref, mixed[images:]))
    for head_ref, weight_ref, part in sides:
        gain = head_ref[6:7, :]
        pooled = head_ref[:images, :] + head_ref[4:5, :] * (part + head_ref[5:6, :])
        if head_ref is own_ref:
            pooled_ref[...] = pooled
        head = jnp.concatenate([pooled, head_ref[images:, :]], axis=0)
        first = first + jnp.sum(head, axis=1, keepdims=True)
        second = second + jnp.sum(head * head, axis=1, keepdims=True)
        value = jnp.where(iota(head.shape, 0) < images, head * gain, head)
        high, rest = to_terms(value)
        middle, low = to_terms(rest)
        product = product + jnp.dot(
            jnp.concatenate([high, middle, low], axis=0).astype(bf16),
            weight_ref[...],
            preferred_element_type=f32,
        )
    product = product[:8] + (product[8:16] + product[16:])
    lane = iota((8, 128), 1)
    tail = jnp.where(lane == 0, first, jnp.where(lane == 1, second, 0.0))
    for j in range(CHIPS):
        out_ref[j, :, :width] = product
        out_ref[j, :, width:] = tail


def embed_kernel(got_ref, text_ref, tail_ref, out_ref, own_ref, back_ref, stat_ref):
    width = text_ref.shape[1]
    channels = BLOCKS * SHARD
    sums = got_ref[0]
    for j in range(1, CHIPS):
        sums = sums + got_ref[j]
    mean = sums[:, width : width + 1] / channels
    inverse = lax.rsqrt(sums[:, width + 1 : width + 2] / channels - mean * mean + eps)
    centred = inverse * (sums[:, :width] - mean * sums[6:7, :width])
    emb = centred + sums[7:8, :width]
    back_ref[...] = jnp.concatenate([centred[:4], sums[4:, :width]], axis=0)
    tail = tail_ref[...]
    block = jnp.concatenate([emb[:4], text_ref[...]], axis=0)
    own_ref[...] = block
    block = block.astype(bf16)
    tail = tail.astype(bf16)
    for d in range(out_ref.shape[0]):
        out_ref[d, :, :width] = block
        out_ref[d, :, width:] = tail
    stat_ref[0] = jnp.broadcast_to(mean, (8, 128))
    stat_ref[1] = jnp.broadcast_to(inverse, (8, 128))


def loss_kernel(
    got_ref,
    own_ref,
    rows_ref,
    stat_ref,
    pooled_ref,
    scale_ref,
    gain_ref,
    project_ref,
    text_far,
    block_ref,
    mixed_ref,
    both_ref,
    text_ref,
    sem,
):
    width = project_ref.shape[1]
    count = got_ref.shape[0] * 8
    home = pl.ds(pl.multiple_of(lax.axis_index("dp") * 8, 8), 8)
    got = got_ref[...].astype(f32).reshape(count, width + 128)
    raw = got[:, :width].astype(bf16)
    product = lax.dot_general(raw, raw, (((1,), (1,)), ((), ())), preferred_element_type=f32)
    same = iota((count, count), 0) == iota((count, count), 1)
    square = jnp.where(same, product, 0.0)
    row_len = jnp.sqrt(jnp.sum(square, axis=1, keepdims=True) + eps)
    col_len = jnp.sqrt(jnp.sum(square, axis=0, keepdims=True) + eps)
    logits = logit_scale * (product / (row_len * col_len))
    column = iota((count, count), 1)
    valid = (iota((count, count), 0) % 8 < 4) & (column % 8 >= 4)
    weights = jnp.where(valid, jnp.exp(jnp.where(valid, logits, 0.0)), 0.0)
    row_total = jnp.sum(weights, axis=1, keepdims=True)
    col_total = jnp.sum(weights, axis=0, keepdims=True)
    target = got[:, width : width + 1]
    matched = jnp.where(target == column.astype(f32), 1.0, 0.0)
    grads = loss_scale * (0.5 * (weights / row_total + weights / col_total) - matched)
    grads = jnp.where(valid, grads, 0.0)
    both_ref[...] = (grads + grads.T) / col_len
    high, rest = to_terms(both_ref[home, :])
    middle, low = to_terms(rest)
    grad_unit = jnp.dot(
        jnp.concatenate([high, middle, low], axis=0).astype(bf16), raw, preferred_element_type=f32
    )
    grad_unit = logit_scale * (grad_unit[:8] + (grad_unit[8:16] + grad_unit[16:]))
    own = own_ref[...]
    length = jnp.sqrt(jnp.sum(own * own, axis=1, keepdims=True) + eps)
    own = own / length
    grad = (grad_unit - own * jnp.sum(own * grad_unit, axis=1, keepdims=True)) / length
    text_ref[...] = grad[4:]
    send = pltpu.make_async_copy(text_ref, text_far, sem)
    send.start()
    grad = grad[:4].astype(bf16)
    back = lax.dot_general(
        jnp.concatenate([grad, jnp.zeros_like(grad)], axis=0),
        project_ref[...],
        (((1,), (1,)), ((), ())),
        preferred_element_type=f32,
    )[:4]
    channels = BLOCKS * SHARD
    grad = grad.astype(f32)
    first = jnp.sum(grad * rows_ref[6:7, :], axis=1, keepdims=True) / channels
    second = jnp.sum(grad * rows_ref[:4, :], axis=1, keepdims=True) / channels
    mean, inverse = stat_ref[0][:4, 0:1], stat_ref[1][:4, 0:1]
    centred = (pooled_ref[...] - mean) * inverse
    block = (inverse / POSITIONS) * (back * gain_ref[...] - first - centred * second)
    block_ref[...] = block
    for k in range(BLOCKS):
        mixed_ref[k] = block * scale_ref[...]
    send.wait()


def backward_kernel(
    got_ref,
    wout_ref,
    slope_ref,
    hidden_ref,
    w_ref,
    through_ref,
    b_ref,
    other_ref,
    turned_ref,
    sums_ref,
    mixed_ref,
    pre_ref,
):
    images, shard = got_ref.shape[1:]
    rows, hidden = slope_ref.shape
    channels = w_ref.shape[0]
    positions = rows // images
    mixed_ref[...] = jnp.zeros_like(mixed_ref)
    for k in range(BLOCKS):
        mixed_ref[0:images, k * shard : (k + 1) * shard] = got_ref[k]
    act = lax.dot_general(
        mixed_ref[...].astype(bf16),
        wout_ref[...],
        (((1,), (1,)), ((), ())),
        preferred_element_type=f32,
    )
    b_row = b_ref[...][None, :]
    step = 256
    one = jnp.zeros((rows, 1), f32)
    two = jnp.zeros((rows, 1), f32)
    for t in range(hidden // step):
        at = slice(t * step, (t + 1) * step)
        for n in range(images):
            span = slice(n * positions, (n + 1) * positions)
            pre_ref[span, :] = (act[n : n + 1, at] * slope_ref[span, at]).astype(bf16).astype(f32)
        value = pre_ref[...]
        gain = through_ref[0:1, at] + through_ref[8:9, at]
        bias = through_ref[1:2, at] + through_ref[9:10, at] + b_row[:, at]
        one = one + jnp.sum(value * gain, axis=1, keepdims=True)
        two = two + jnp.sum(value * (hidden_ref[:, at] - bias), axis=1, keepdims=True)
        turned_ref[at, :] = value.T.astype(bf16)
    lane = iota((rows, 128), 1)
    sums = jnp.where(lane == 0, one, jnp.where(lane == 1, two, 0.0)).T[:8]
    sums_ref[...] = sums
    high, low = to_terms(sums)
    other_ref[channels // 2 :, :] = jnp.concatenate([high, low], axis=0).astype(bf16)
    half = channels // 2
    other_ref[:half, :] = jnp.dot(
        w_ref[half:, :], turned_ref[...], preferred_element_type=f32
    ).astype(bf16)


def mine_kernel(w_ref, turned_ref, mine_ref):
    mine_ref[...] = jnp.dot(
        w_ref[: mine_ref.shape[0], :], turned_ref[...], preferred_element_type=f32
    ).astype(bf16)


def pair_kernel(mine_ref, got_ref, sums_ref, out_ref):
    half = mine_ref.shape[0]
    shard = half // CHIPS
    for j in range(CHIPS):
        span = slice(j * shard, (j + 1) * shard)
        out_ref[j, :shard, :] = (mine_ref[span, :].astype(f32) + got_ref[span, :].astype(f32)).astype(
            bf16
        )
    tail = got_ref[half:, :].astype(f32)
    high, low = to_terms(sums_ref[...] + (tail[:8] + tail[8:]))
    tail = jnp.concatenate([high, low], axis=0).astype(bf16)
    for j in range(CHIPS):
        out_ref[j, shard:, :] = tail


def final_kernel(
    got_ref, conv_ref, stat_ref, gain_ref, w_ref, block_ref, out_far, rows_ref, out_ref, sems
):
    shard = conv_ref.shape[0]
    channels = shard * BLOCKS
    index = lax.axis_index("mp")
    pair = gain_ref[:, pl.ds(pl.multiple_of(index // 2 * 2 * shard, 128), 2 * shard)]
    gain = jnp.where(index % 2 == 0, pair[:, :shard], pair[:, shard:])
    gain = jnp.broadcast_to(gain, (8, shard)).T[:, 0:1]
    images, side = out_ref.shape[:2]
    positions = side * side
    total = got_ref[0].astype(f32)
    for j in range(1, CHIPS):
        total = total + got_ref[j].astype(f32)
    first = (total[shard : shard + 1] + total[shard + 8 : shard + 9]) / channels
    second = (total[shard + 1 : shard + 2] + total[shard + 9 : shard + 10]) / channels
    average, inverse = stat_ref[0:1, :], stat_ref[1:2, :]
    centred = (conv_ref[...].astype(f32) - average) * inverse
    grad = inverse * (total[:shard] * gain - first - centred * second)
    rows_ref[...] = grad.T

    def image(n, carry):
        span = pl.ds(pl.multiple_of(n * positions, positions), positions)
        x = rows_ref[span, :].reshape(side, side, shard)
        base = block_ref[pl.ds(n, 1), :]
        for p, row in enumerate(taps(x, w_ref, True)):
            out_ref[n, p] = row + base
        pltpu.make_async_copy(out_ref.at[n], out_far.at[n], sems.at[n]).start()
        return carry

    lax.fori_loop(0, images, image, 0)
    for n in range(images):
        pltpu.make_async_copy(out_ref.at[n], out_far.at[n], sems.at[n]).wait()


def body(
    x_in,
    dw_weight,
    dw_bias,
    ln_gain,
    ln_bias,
    w_in,
    b_in,
    w_out,
    b_out,
    layer_scale,
    head_gain,
    head_bias,
    projection,
    text_emb,
    labels,
):
    images, side, _, shard = x_in.shape
    channels, hidden = w_in.shape
    rows = images * side * side
    pairs, width = text_emb.shape
    shards = lax.axis_size("dp")
    (begun,) = run(start_kernel, [shape(8, 128)], flops=START_FLOPS)
    copies, conv, head_own = run(
        conv_kernel,
        [
            shape(CHIPS, shard, rows, dtype=bf16),
            shape(shard, rows, dtype=bf16),
            shape(8, shard),
        ],
        Far(begun),
        layer_scale[None, :],
        b_out[None, :],
        head_gain[None, :],
        head_bias[None, :],
        Far(x_in),
        Far(dw_weight),
        Far(dw_bias[None, :]),
        scratch=[
            pltpu.VMEM(x_in.shape, bf16),
            pltpu.VMEM(dw_weight.shape, f32),
            pltpu.VMEM((1, shard), f32),
            pltpu.VMEM((rows, shard), f32),
            pltpu.SemaphoreType.DMA((3,)),
        ],
        limit=CONV_LIMIT,
        flops=CONV_FLOPS,
    )
    conv_mine = chip_exchange(copies)
    conv_other = core_swap(conv_mine)
    conv_mine = conv_mine.reshape(channels // 2, rows)
    conv_other = conv_other.reshape(channels // 2, rows)
    own_rows, part, vec, w_own, tail, head_sent, project_sent = run(
        ready_kernel,
        [
            shape(rows, channels // 2, dtype=bf16),
            shape(8, rows),
            shape(8, channels),
            shape(channels, hidden, dtype=bf16),
            shape(8, 128),
            shape(8, shard),
            shape(shard, width, dtype=bf16),
        ],
        conv_mine,
        ln_gain[None, :],
        ln_bias[None, :],
        w_in,
        labels,
        head_own,
        Far(projection),
        scratch=[pltpu.SemaphoreType.DMA((BLOCKS + 1,))],
        flops=READY_FLOPS,
    )
    head_other = core_swap(head_sent)
    project_other = core_swap(project_sent)
    slope, hidden_pre, through, row_stat, mixed = run(
        forward_kernel,
        [
            shape(rows, hidden),
            shape(rows, hidden),
            shape(16, hidden),
            shape(8, rows),
            shape(8, channels),
        ],
        own_rows,
        conv_other,
        part,
        vec,
        w_own,
        b_in,
        w_out,
        scratch=[pltpu.VMEM((rows + 16, channels), bf16)],
        flops=2 * rows * channels * hidden,
    )
    (mixed,) = run(
        block_kernel,
        [shape(BLOCKS, 2 * images, shard)],
        mixed,
        Far(head_other),
        Far(project_other),
    )
    blocks, pooled = run(
        head_kernel,
        [shape(CHIPS, 8, width + 128), shape(images, shard)],
        shard_exchange(mixed),
        head_own,
        head_other,
        projection,
        project_other,
    )
    pair_block, own_block, back_rows, head_stat = run(
        embed_kernel,
        [
            shape(shards, 8, width + 128, dtype=bf16),
            shape(8, width),
            shape(8, width),
            shape(2, 8, 128),
        ],
        chip_exchange(blocks),
        text_emb,
        tail,
    )
    grad_text, grad_block, mixed_block = run(
        loss_kernel,
        [Far(shape(pairs, width)), shape(images, shard), shape(BLOCKS, images, shard)],
        lax.all_to_all(pair_block, "dp", 0, 0),
        own_block,
        back_rows,
        head_stat,
        pooled,
        layer_scale[None, :],
        head_gain[None, :],
        projection,
        scratch=[
            pltpu.VMEM((shards * 8, shards * 8), f32),
            pltpu.VMEM((pairs, width), f32),
            pltpu.SemaphoreType.DMA,
        ],
    )
    other, turned, row_sums = run(
        backward_kernel,
        [
            shape(channels // 2 + 16, rows, dtype=bf16),
            shape(hidden, rows, dtype=bf16),
            shape(8, rows),
        ],
        shard_exchange(mixed_block),
        w_out,
        slope,
        hidden_pre,
        w_own,
        through,
        b_in,
        scratch=[pltpu.VMEM((8, channels), f32), pltpu.VMEM((rows, 256), f32)],
        flops=rows * channels * hidden,
    )
    passed = core_swap(other)
    (mine,) = run(
        mine_kernel,
        [shape(channels // 2, rows, dtype=bf16)],
        w_own,
        turned,
        flops=rows * channels * hidden,
    )
    (blocks,) = run(
        pair_kernel, [shape(CHIPS, shard + 16, rows, dtype=bf16)], mine, passed, row_sums
    )
    (grad_input,) = run(
        final_kernel,
        [Far(shape(images, side, side, shard))],
        chip_exchange(blocks),
        conv,
        row_stat,
        ln_gain[None, :],
        dw_weight,
        grad_block,
        scratch=[
            pltpu.VMEM((rows, shard), f32),
            pltpu.VMEM((images, side, side, shard), f32),
            pltpu.SemaphoreType.DMA((images,)),
        ],
        flops=2 * 49 * rows * shard,
    )
    return (grad_input, grad_text)


def solution(mesh):
    return jax.shard_map(
        body,
        mesh=mesh,
        in_specs=(
            P("dp", None, None, "mp"),
            P(None, None, "mp"),
            P("mp"),
            P(),
            P(),
            P(None, "mp"),
            P("mp"),
            P("mp", None),
            P("mp"),
            P("mp"),
            P("mp"),
            P("mp"),
            P("mp", None),
            P("dp", None),
            P("dp"),
        ),
        out_specs=(P("dp", None, None, "mp"), P("dp", None)),
        check_vma=False,
    )
```

```python
import jax
import jax.numpy as jnp
from jax import lax
from jax.experimental import pallas as pl
from jax.experimental.pallas import tpu as pltpu
from jax.sharding import PartitionSpec as P

eps = 1e-06
logit_scale = 20.0
loss_scale = 512.0
root_half = 0.7071067811865476
inv_root_two_pi = 0.3989422804014327
f32 = jnp.float32
bf16 = jnp.bfloat16
MIB = 1 << 20
CONV_LIMIT = 50 * MIB
CONV_FLOPS = 16 * 10**9
START_FLOPS = 4 * 10**9
READY_FLOPS = 12 * 10**9
CHIPS = 8
BLOCKS = 16
SHARD = 192
POSITIONS = 64


def core_swap(array):
    return lax.ppermute(array, "mp", [(i, i ^ 1) for i in range(BLOCKS)])


def chip_exchange(array):
    groups = [[i for i in range(core, BLOCKS, 2)] for core in range(2)]
    return lax.all_to_all(array, "mp", 0, 0, axis_index_groups=groups)


def shard_exchange(array):
    return lax.all_to_all(array, "mp", 0, 0)


class Far:
    def __init__(self, array):
        self.array = array


def run(kernel, outs, *operands, scratch=(), limit=24 * MIB, flops=0):
    def spec(a):
        if isinstance(a, Far):
            return pl.BlockSpec(memory_space=pltpu.HBM)
        return pl.BlockSpec(memory_space=pltpu.SMEM if a.dtype == jnp.int32 else pltpu.VMEM)

    arrays = [a.array if isinstance(a, Far) else a for a in operands]
    return pl.pallas_call(
        kernel,
        out_shape=[a.array if isinstance(a, Far) else a for a in outs],
        in_specs=[spec(a) for a in operands],
        out_specs=[
            pl.BlockSpec(memory_space=pltpu.HBM if isinstance(a, Far) else pltpu.VMEM)
            for a in outs
        ],
        scratch_shapes=list(scratch),
        compiler_params=pltpu.CompilerParams(vmem_limit_bytes=limit),
        cost_estimate=pl.CostEstimate(
            flops=flops,
            bytes_accessed=sum(a.size * a.dtype.itemsize for a in arrays),
            transcendentals=0,
        ),
    )(*arrays)


def shape(*dims, dtype=f32):
    return jax.ShapeDtypeStruct(dims, dtype)


def iota(dims, axis):
    return lax.broadcasted_iota(jnp.int32, dims, axis)


def to_terms(array):
    high = array.astype(bf16).astype(f32)
    return high, array - high


def taps(x, w_ref, flip):
    side, _, shard = x.shape
    size = w_ref.shape[0]
    reach = size // 2
    column = iota((side, side, shard), 1)
    acc = [jnp.zeros((side, shard), f32) for _ in range(side)]
    for b in range(size):
        by = b - reach
        if by:
            moved = jnp.where(
                (column + by >= 0) & (column + by < side), pltpu.roll(x, (-by) % side, 1), 0.0
            )
        else:
            moved = x
        for a in range(size):
            wa, wb = (size - 1 - a, size - 1 - b) if flip else (a, b)
            weight = w_ref[wa, wb : wb + 1, :]
            for p in range(side):
                if 0 <= p + a - reach < side:
                    acc[p] = acc[p] + moved[p + a - reach] * weight
    return acc


def start_kernel(out_ref):
    out_ref[...] = jnp.zeros_like(out_ref)


def conv_kernel(
    _,
    x_far,
    dw_far,
    bias_far,
    copies_ref,
    conv_ref,
    mean_ref,
    x_ref,
    dw_ref,
    bias_ref,
    rows_ref,
    sems,
):
    images, side = x_ref.shape[:2]
    positions = side * side
    loads = ((x_far, x_ref), (dw_far, dw_ref), (bias_far, bias_ref))
    loads = [pltpu.make_async_copy(far, near, sems.at[i]) for i, (far, near) in enumerate(loads)]
    for copy in loads:
        copy.start()
    for copy in loads:
        copy.wait()

    def image(n, carry):
        x = x_ref[n].astype(f32)
        total = jnp.sum(jnp.sum(x, axis=0), axis=0, keepdims=True)
        mean_ref[pl.ds(n, 1), :] = total / positions
        for p, row in enumerate(taps(x, dw_ref, False)):
            rows_ref[pl.ds(pl.multiple_of(n * positions + p * side, side), side), :] = row
        return carry

    lax.fori_loop(0, images, image, 0)
    turned = (rows_ref[...] + bias_ref[...]).T.astype(bf16)
    conv_ref[...] = turned
    for j in range(CHIPS):
        copies_ref[j] = turned


def ready_kernel(
    mine_ref,
    gain_ref,
    bias_ref,
    w_ref,
    labels_far,
    mean_ref,
    scale_ref,
    bout_ref,
    head_gain_ref,
    head_bias_ref,
    project_far,
    rows_ref,
    part_ref,
    vec_ref,
    own_ref,
    tail_ref,
    head_ref,
    project_ref,
    labels_ref,
    sems,
):
    shard = w_ref.shape[0] // BLOCKS
    core = lax.axis_index("mp") % 2
    moves = []
    for k in range(BLOCKS):
        place = 2 * (k % CHIPS) + (core if k < CHIPS else 1 - core)
        source = pl.ds(pl.multiple_of(place * shard, 64), shard)
        moves.append(
            pltpu.make_async_copy(
                w_ref.at[source], own_ref.at[k * shard : (k + 1) * shard], sems.at[k]
            )
        )
    moves.append(
        pltpu.make_async_copy(project_far, project_ref.at[0:shard], sems.at[BLOCKS])
    )
    load = pltpu.make_async_copy(labels_far, labels_ref, sems.at[BLOCKS + 1])
    load.start()
    for copy in moves:
        copy.start()
    head_ref[0:4, :] = mean_ref[...]
    for i, ref in enumerate((scale_ref, bout_ref, head_gain_ref, head_bias_ref)):
        head_ref[4 + i : 5 + i, :] = ref[...]
    high, rest = to_terms(head_ref[...])
    middle, low = to_terms(rest)
    project_ref[shard:, :] = jnp.zeros_like(project_ref[shard:, :])
    for i, term in enumerate((high, middle, low)):
        sent = jnp.concatenate([term, jnp.zeros_like(term)], axis=0).astype(bf16)
        project_ref[shard:, i * 256 : i * 256 + shard] = sent
    half, rows = mine_ref.shape
    step = 256
    first = jnp.zeros((1, rows), f32)
    second = jnp.zeros((1, rows), f32)
    for c in range(half // step):
        at = slice(c * step, (c + 1) * step)
        rows_ref[:, at] = mine_ref[at, :].T
        value = mine_ref[at, :].astype(f32)
        first = first + jnp.sum(value, axis=0, keepdims=True)
        second = second + jnp.sum(value * value, axis=0, keepdims=True)
    part_ref[0:1, :] = first
    part_ref[1:2, :] = second
    vec_ref[...] = jnp.zeros_like(vec_ref)
    for i, ref in enumerate((gain_ref, bias_ref)):
        for j in range(CHIPS):
            low = ref[:, 2 * j * shard : (2 * j + 1) * shard]
            high = ref[:, (2 * j + 1) * shard : (2 * j + 2) * shard]
            vec_ref[i : i + 1, j * shard : (j + 1) * shard] = jnp.where(core == 0, low, high)
            vec_ref[i : i + 1, half + j * shard : half + (j + 1) * shard] = jnp.where(
                core == 0, high, low
            )
    load.wait()
    pairs = labels_ref.shape[0]
    row = iota((8, 128), 0)
    tail = jnp.zeros((8, 128), f32)
    for r in range(pairs):
        label = labels_ref[r]
        target = (label // pairs) * 8 + 4 + label % pairs
        tail = jnp.where(row == r, target.astype(f32), tail)
    tail_ref[...] = tail
    for copy in moves:
        copy.wait()


def forward_kernel(
    rows_ref,
    other_ref,
    part_ref,
    vec_ref,
    w_ref,
    b_ref,
    wout_ref,
    slope_ref,
    hidden_ref,
    through_ref,
    stat_ref,
    mixed_ref,
    normed_ref,
):
    half, rows = other_ref.shape
    channels, hidden = w_ref.shape
    images = rows // POSITIONS
    positions = POSITIONS
    step = 256
    first, second = part_ref[0:1, :], part_ref[1:2, :]
    for c in range(half // step):
        value = other_ref[c * step : (c + 1) * step, :].astype(f32)
        first = first + jnp.sum(value, axis=0, keepdims=True)
        second = second + jnp.sum(value * value, axis=0, keepdims=True)
    average = first / channels
    inverse = lax.rsqrt(second / channels - average * average + eps)
    lane = iota((8, rows), 0)
    stat_ref[...] = jnp.where(lane == 0, average, jnp.where(lane == 1, inverse, 0.0))
    turned = stat_ref[...].T
    average = jnp.broadcast_to(turned[:, 0:1], (rows, step))
    inverse = jnp.broadcast_to(turned[:, 1:2], (rows, step))
    for c in range(channels // step):
        at = slice(c * step, (c + 1) * step)
        if c * step < half:
            value = rows_ref[:, at]
        else:
            value = other_ref[c * step - half : (c + 1) * step - half, :].T
        value = (value.astype(f32) - average) * inverse
        normed_ref[0:rows, at] = (value * vec_ref[0:1, at] + vec_ref[1:2, at]).astype(bf16)
    normed_ref[rows : rows + 16, :] = jnp.concatenate(to_terms(vec_ref[...]), axis=0).astype(bf16)
    b_row = b_ref[...][None, :]
    whole = jnp.dot(normed_ref[...], w_ref[...], preferred_element_type=f32)
    for t in range(hidden // step):
        at = slice(t * step, (t + 1) * step)
        product = whole[:, at]
        through_ref[:, at] = product[rows:]
        pre = product[:rows] + b_row[:, at]
        hidden_ref[:, at] = pre
        gate = 0.5 + 0.5 * lax.erf(pre * root_half)
        slope_ref[:, at] = gate + pre * jnp.exp(-0.5 * pre * pre) * inv_root_two_pi
        active = pre * gate
        sums = [
            jnp.sum(active[n * positions : (n + 1) * positions], axis=0, keepdims=True) / positions
            for n in range(images)
        ]
        sums = jnp.concatenate(sums + [jnp.zeros((8 - images, step), f32)], axis=0)
        high, low = to_terms(sums)
        part = jnp.dot(
            jnp.concatenate([high, low], axis=0).astype(bf16),
            wout_ref[at, :],
            preferred_element_type=f32,
        )
        part = part[:8] + part[8:]
        mixed = part if t == 0 else mixed + part
    mixed_ref[...] = mixed


def block_kernel(mixed_ref, _project, out_ref):
    shard = out_ref.shape[2]
    images = out_ref.shape[1] // 2
    for k in range(BLOCKS):
        block = mixed_ref[:images, k * shard : (k + 1) * shard]
        out_ref[k, :images, :] = block
        out_ref[k ^ 1, images:, :] = block


def head_kernel(got_ref, own_ref, project_ref, other_ref, out_ref, pooled_ref):
    images = pooled_ref.shape[0]
    width = project_ref.shape[1]
    mixed = got_ref[0]
    for j in range(1, BLOCKS):
        mixed = mixed + got_ref[j]
    first = jnp.zeros((8, 1), f32)
    second = jnp.zeros((8, 1), f32)
    product = jnp.zeros((24, width), f32)
    shard = own_ref.shape[1]
    sent = other_ref[shard:, :].astype(f32)[:8]
    other = sent[:, :shard] + (sent[:, 256 : 256 + shard] + sent[:, 512 : 512 + shard])
    sides = (
        (own_ref[...], project_ref[...], mixed[:images]),
        (other, other_ref[:shard, :], mixed[images:]),
    )
    for i, (rows, weight, part) in enumerate(sides):
        gain = rows[6:7, :]
        pooled = rows[:images, :] + rows[4:5, :] * (part + rows[5:6, :])
        if i == 0:
            pooled_ref[...] = pooled
        head = jnp.concatenate([pooled, rows[images:, :]], axis=0)
        first = first + jnp.sum(head, axis=1, keepdims=True)
        second = second + jnp.sum(head * head, axis=1, keepdims=True)
        value = jnp.where(iota(head.shape, 0) < images, head * gain, head)
        high, rest = to_terms(value)
        middle, low = to_terms(rest)
        product = product + jnp.dot(
            jnp.concatenate([high, middle, low], axis=0).astype(bf16),
            weight,
            preferred_element_type=f32,
        )
    product = product[:8] + (product[8:16] + product[16:])
    lane = iota((8, 128), 1)
    tail = jnp.where(lane == 0, first, jnp.where(lane == 1, second, 0.0))
    for j in range(CHIPS):
        out_ref[j, :, :width] = product
        out_ref[j, :, width:] = tail


def embed_kernel(got_ref, text_ref, tail_ref, out_ref, own_ref, back_ref, stat_ref):
    width = text_ref.shape[1]
    channels = BLOCKS * SHARD
    sums = got_ref[0]
    for j in range(1, CHIPS):
        sums = sums + got_ref[j]
    mean = sums[:, width : width + 1] / channels
    inverse = lax.rsqrt(sums[:, width + 1 : width + 2] / channels - mean * mean + eps)
    centred = inverse * (sums[:, :width] - mean * sums[6:7, :width])
    emb = centred + sums[7:8, :width]
    back_ref[...] = jnp.concatenate([centred[:4], sums[4:, :width]], axis=0)
    tail = tail_ref[...]
    block = jnp.concatenate([emb[:4], text_ref[...]], axis=0)
    own_ref[...] = block
    block = block.astype(bf16)
    tail = tail.astype(bf16)
    for d in range(out_ref.shape[0]):
        out_ref[d, :, :width] = block
        out_ref[d, :, width:] = tail
    stat_ref[0] = jnp.broadcast_to(mean, (8, 128))
    stat_ref[1] = jnp.broadcast_to(inverse, (8, 128))


def loss_kernel(
    got_ref,
    own_ref,
    rows_ref,
    stat_ref,
    pooled_ref,
    scale_ref,
    gain_ref,
    project_ref,
    text_far,
    block_ref,
    mixed_ref,
    both_ref,
    text_ref,
    sem,
):
    width = project_ref.shape[1]
    count = got_ref.shape[0] * 8
    home = pl.ds(pl.multiple_of(lax.axis_index("dp") * 8, 8), 8)
    got = got_ref[...].astype(f32).reshape(count, width + 128)
    raw = got[:, :width].astype(bf16)
    product = lax.dot_general(raw, raw, (((1,), (1,)), ((), ())), preferred_element_type=f32)
    same = iota((count, count), 0) == iota((count, count), 1)
    square = jnp.where(same, product, 0.0)
    row_len = jnp.sqrt(jnp.sum(square, axis=1, keepdims=True) + eps)
    col_len = jnp.sqrt(jnp.sum(square, axis=0, keepdims=True) + eps)
    logits = logit_scale * (product / (row_len * col_len))
    column = iota((count, count), 1)
    valid = (iota((count, count), 0) % 8 < 4) & (column % 8 >= 4)
    weights = jnp.where(valid, jnp.exp(jnp.where(valid, logits, 0.0)), 0.0)
    row_total = jnp.sum(weights, axis=1, keepdims=True)
    col_total = jnp.sum(weights, axis=0, keepdims=True)
    target = got[:, width : width + 1]
    matched = jnp.where(target == column.astype(f32), 1.0, 0.0)
    grads = loss_scale * (0.5 * (weights / row_total + weights / col_total) - matched)
    grads = jnp.where(valid, grads, 0.0)
    both_ref[...] = (grads + grads.T) / col_len
    high, rest = to_terms(both_ref[home, :])
    middle, low = to_terms(rest)
    grad_unit = jnp.dot(
        jnp.concatenate([high, middle, low], axis=0).astype(bf16), raw, preferred_element_type=f32
    )
    grad_unit = logit_scale * (grad_unit[:8] + (grad_unit[8:16] + grad_unit[16:]))
    own = own_ref[...]
    length = jnp.sqrt(jnp.sum(own * own, axis=1, keepdims=True) + eps)
    own = own / length
    grad = (grad_unit - own * jnp.sum(own * grad_unit, axis=1, keepdims=True)) / length
    text_ref[...] = grad[4:]
    send = pltpu.make_async_copy(text_ref, text_far, sem)
    send.start()
    grad = grad[:4].astype(bf16)
    back = lax.dot_general(
        jnp.concatenate([grad, jnp.zeros_like(grad)], axis=0),
        project_ref[...],
        (((1,), (1,)), ((), ())),
        preferred_element_type=f32,
    )[:4]
    channels = BLOCKS * SHARD
    grad = grad.astype(f32)
    first = jnp.sum(grad * rows_ref[6:7, :], axis=1, keepdims=True) / channels
    second = jnp.sum(grad * rows_ref[:4, :], axis=1, keepdims=True) / channels
    mean, inverse = stat_ref[0][:4, 0:1], stat_ref[1][:4, 0:1]
    centred = (pooled_ref[...] - mean) * inverse
    block = (inverse / POSITIONS) * (back * gain_ref[...] - first - centred * second)
    block_ref[...] = block
    for k in range(BLOCKS):
        mixed_ref[k] = block * scale_ref[...]
    send.wait()


def backward_kernel(
    got_ref,
    wout_ref,
    slope_ref,
    hidden_ref,
    w_ref,
    through_ref,
    b_ref,
    other_ref,
    turned_ref,
    sums_ref,
    mixed_ref,
    pre_ref,
):
    images, shard = got_ref.shape[1:]
    rows, hidden = slope_ref.shape
    channels = w_ref.shape[0]
    positions = rows // images
    mixed_ref[...] = jnp.zeros_like(mixed_ref)
    for k in range(BLOCKS):
        mixed_ref[0:images, k * shard : (k + 1) * shard] = got_ref[k]
    act = lax.dot_general(
        mixed_ref[...].astype(bf16),
        wout_ref[...],
        (((1,), (1,)), ((), ())),
        preferred_element_type=f32,
    )
    b_row = b_ref[...][None, :]
    step = 256
    one = jnp.zeros((rows, 1), f32)
    two = jnp.zeros((rows, 1), f32)
    for t in range(hidden // step):
        at = slice(t * step, (t + 1) * step)
        for n in range(images):
            span = slice(n * positions, (n + 1) * positions)
            pre_ref[span, :] = (act[n : n + 1, at] * slope_ref[span, at]).astype(bf16).astype(f32)
        value = pre_ref[...]
        gain = through_ref[0:1, at] + through_ref[8:9, at]
        bias = through_ref[1:2, at] + through_ref[9:10, at] + b_row[:, at]
        one = one + jnp.sum(value * gain, axis=1, keepdims=True)
        two = two + jnp.sum(value * (hidden_ref[:, at] - bias), axis=1, keepdims=True)
        turned_ref[at, :] = value.T.astype(bf16)
    lane = iota((rows, 128), 1)
    sums = jnp.where(lane == 0, one, jnp.where(lane == 1, two, 0.0)).T[:8]
    sums_ref[...] = sums
    high, low = to_terms(sums)
    other_ref[channels // 2 :, :] = jnp.concatenate([high, low], axis=0).astype(bf16)
    half = channels // 2
    other_ref[:half, :] = jnp.dot(
        w_ref[half:, :], turned_ref[...], preferred_element_type=f32
    ).astype(bf16)


def mine_kernel(
    w_ref, turned_ref, conv_ref, stat_ref, gain_ref, mine_ref, scaled_ref, centred_ref, row_ref
):
    shard = conv_ref.shape[0]
    index = lax.axis_index("mp")
    pair = gain_ref[:, pl.ds(pl.multiple_of(index // 2 * 2 * shard, 128), 2 * shard)]
    gain = jnp.where(index % 2 == 0, pair[:, :shard], pair[:, shard:])
    gain = jnp.broadcast_to(gain, (8, shard)).T[:, 0:1]
    average, inverse = stat_ref[0:1, :], stat_ref[1:2, :]
    scaled_ref[...] = gain * inverse
    centred_ref[...] = (conv_ref[...].astype(f32) - average) * (inverse * inverse)
    row_ref[...] = jnp.broadcast_to(inverse, row_ref.shape)
    mine_ref[...] = jnp.dot(
        w_ref[: mine_ref.shape[0], :], turned_ref[...], preferred_element_type=f32
    ).astype(bf16)


def pair_kernel(mine_ref, got_ref, sums_ref, out_ref):
    half = mine_ref.shape[0]
    shard = half // CHIPS
    for j in range(CHIPS):
        span = slice(j * shard, (j + 1) * shard)
        out_ref[j, :shard, :] = (mine_ref[span, :].astype(f32) + got_ref[span, :].astype(f32)).astype(
            bf16
        )
    tail = got_ref[half:, :].astype(f32)
    high, low = to_terms(sums_ref[...] + (tail[:8] + tail[8:]))
    tail = jnp.concatenate([high, low], axis=0).astype(bf16)
    for j in range(CHIPS):
        out_ref[j, shard:, :] = tail


def final_kernel(
    got_ref, scaled_ref, centred_ref, row_ref, w_ref, block_ref, out_far, rows_ref, out_ref, sems
):
    shard = scaled_ref.shape[0]
    channels = shard * BLOCKS
    images, side = out_ref.shape[:2]
    positions = side * side
    total = got_ref[0].astype(f32)
    for j in range(1, CHIPS):
        total = total + got_ref[j].astype(f32)
    first = (total[shard : shard + 1] + total[shard + 8 : shard + 9]) / channels
    second = (total[shard + 1 : shard + 2] + total[shard + 9 : shard + 10]) / channels
    first = first * row_ref[0:1, :]
    grad = total[:shard] * scaled_ref[...] - first - centred_ref[...] * second
    rows_ref[...] = grad.T

    def image(n, carry):
        span = pl.ds(pl.multiple_of(n * positions, positions), positions)
        x = rows_ref[span, :].reshape(side, side, shard)
        base = block_ref[pl.ds(n, 1), :]
        for p, row in enumerate(taps(x, w_ref, True)):
            out_ref[n, p] = row + base
        pltpu.make_async_copy(out_ref.at[n], out_far.at[n], sems.at[n]).start()
        return carry

    lax.fori_loop(0, images, image, 0)
    for n in range(images):
        pltpu.make_async_copy(out_ref.at[n], out_far.at[n], sems.at[n]).wait()


def body(
    x_in,
    dw_weight,
    dw_bias,
    ln_gain,
    ln_bias,
    w_in,
    b_in,
    w_out,
    b_out,
    layer_scale,
    head_gain,
    head_bias,
    projection,
    text_emb,
    labels,
):
    images, side, _, shard = x_in.shape
    channels, hidden = w_in.shape
    rows = images * side * side
    pairs, width = text_emb.shape
    shards = lax.axis_size("dp")
    (begun,) = run(start_kernel, [shape(8, 128)], flops=START_FLOPS)
    copies, conv, input_mean = run(
        conv_kernel,
        [
            shape(CHIPS, shard, rows, dtype=bf16),
            shape(shard, rows, dtype=bf16),
            shape(images, shard),
        ],
        Far(begun),
        Far(x_in),
        Far(dw_weight),
        Far(dw_bias[None, :]),
        scratch=[
            pltpu.VMEM(x_in.shape, bf16),
            pltpu.VMEM(dw_weight.shape, f32),
            pltpu.VMEM((1, shard), f32),
            pltpu.VMEM((rows, shard), f32),
            pltpu.SemaphoreType.DMA((3,)),
        ],
        limit=CONV_LIMIT,
        flops=CONV_FLOPS,
    )
    conv_mine = chip_exchange(copies)
    conv_other = core_swap(conv_mine)
    conv_mine = conv_mine.reshape(channels // 2, rows)
    conv_other = conv_other.reshape(channels // 2, rows)
    own_rows, part, vec, w_own, tail, head_own, project_sent = run(
        ready_kernel,
        [
            shape(rows, channels // 2, dtype=bf16),
            shape(8, rows),
            shape(8, channels),
            shape(channels, hidden, dtype=bf16),
            shape(8, 128),
            shape(8, shard),
            shape(shard + 16, width, dtype=bf16),
        ],
        conv_mine,
        ln_gain[None, :],
        ln_bias[None, :],
        w_in,
        Far(labels),
        input_mean,
        layer_scale[None, :],
        b_out[None, :],
        head_gain[None, :],
        head_bias[None, :],
        Far(projection),
        scratch=[pltpu.SMEM(labels.shape, jnp.int32), pltpu.SemaphoreType.DMA((BLOCKS + 2,))],
        flops=READY_FLOPS,
    )
    project_other = core_swap(project_sent)
    slope, hidden_pre, through, row_stat, mixed = run(
        forward_kernel,
        [
            shape(rows, hidden),
            shape(rows, hidden),
            shape(16, hidden),
            shape(8, rows),
            shape(8, channels),
        ],
        own_rows,
        conv_other,
        part,
        vec,
        w_own,
        b_in,
        w_out,
        scratch=[pltpu.VMEM((rows + 16, channels), bf16)],
        flops=2 * rows * channels * hidden,
    )
    (mixed,) = run(
        block_kernel,
        [shape(BLOCKS, 2 * images, shard)],
        mixed,
        Far(project_other),
    )
    blocks, pooled = run(
        head_kernel,
        [shape(CHIPS, 8, width + 128), shape(images, shard)],
        shard_exchange(mixed),
        head_own,
        projection,
        project_other,
    )
    pair_block, own_block, back_rows, head_stat = run(
        embed_kernel,
        [
            shape(shards, 8, width + 128, dtype=bf16),
            shape(8, width),
            shape(8, width),
            shape(2, 8, 128),
        ],
        chip_exchange(blocks),
        text_emb,
        tail,
    )
    grad_text, grad_block, mixed_block = run(
        loss_kernel,
        [Far(shape(pairs, width)), shape(images, shard), shape(BLOCKS, images, shard)],
        lax.all_to_all(pair_block, "dp", 0, 0),
        own_block,
        back_rows,
        head_stat,
        pooled,
        layer_scale[None, :],
        head_gain[None, :],
        projection,
        scratch=[
            pltpu.VMEM((shards * 8, shards * 8), f32),
            pltpu.VMEM((pairs, width), f32),
            pltpu.SemaphoreType.DMA,
        ],
    )
    other, turned, row_sums = run(
        backward_kernel,
        [
            shape(channels // 2 + 16, rows, dtype=bf16),
            shape(hidden, rows, dtype=bf16),
            shape(8, rows),
        ],
        shard_exchange(mixed_block),
        w_out,
        slope,
        hidden_pre,
        w_own,
        through,
        b_in,
        scratch=[pltpu.VMEM((8, channels), f32), pltpu.VMEM((rows, 256), f32)],
        flops=rows * channels * hidden,
    )
    passed = core_swap(other)
    mine, scaled, centred, row_inverse = run(
        mine_kernel,
        [
            shape(channels // 2, rows, dtype=bf16),
            shape(shard, rows),
            shape(shard, rows),
            shape(8, rows),
        ],
        w_own,
        turned,
        conv,
        row_stat,
        ln_gain[None, :],
        flops=rows * channels * hidden,
    )
    (blocks,) = run(
        pair_kernel, [shape(CHIPS, shard + 16, rows, dtype=bf16)], mine, passed, row_sums
    )
    (grad_input,) = run(
        final_kernel,
        [Far(shape(images, side, side, shard))],
        chip_exchange(blocks),
        scaled,
        centred,
        row_inverse,
        dw_weight,
        grad_block,
        scratch=[
            pltpu.VMEM((rows, shard), f32),
            pltpu.VMEM((images, side, side, shard), f32),
            pltpu.SemaphoreType.DMA((images,)),
        ],
        flops=2 * 49 * rows * shard,
    )
    return (grad_input, grad_text)


def solution(mesh):
    return jax.shard_map(
        body,
        mesh=mesh,
        in_specs=(
            P("dp", None, None, "mp"),
            P(None, None, "mp"),
            P("mp"),
            P(),
            P(),
            P(None, "mp"),
            P("mp"),
            P("mp", None),
            P("mp"),
            P("mp"),
            P("mp"),
            P("mp"),
            P("mp", None),
            P("dp", None),
            P("dp"),
        ),
        out_specs=(P("dp", None, None, "mp"), P("dp", None)),
        check_vma=False,
    )
```

```python
import jax
import jax.numpy as jnp
from jax import lax
from jax.experimental import pallas as pl
from jax.experimental.pallas import tpu as pltpu
from jax.sharding import PartitionSpec as P

eps = 1e-06
logit_scale = 20.0
loss_scale = 512.0
root_half = 0.7071067811865476
inv_root_two_pi = 0.3989422804014327
f32 = jnp.float32
bf16 = jnp.bfloat16
MIB = 1 << 20
CONV_LIMIT = 50 * MIB
CONV_FLOPS = 16 * 10**9
START_FLOPS = 4 * 10**9
READY_FLOPS = 12 * 10**9
CHIPS = 8
BLOCKS = 16
SHARD = 192
POSITIONS = 64


def core_swap(array):
    return lax.ppermute(array, "mp", [(i, i ^ 1) for i in range(BLOCKS)])


def chip_exchange(array):
    groups = [[i for i in range(core, BLOCKS, 2)] for core in range(2)]
    return lax.all_to_all(array, "mp", 0, 0, axis_index_groups=groups)


def shard_exchange(array):
    return lax.all_to_all(array, "mp", 0, 0)


class Far:
    def __init__(self, array):
        self.array = array


def run(kernel, outs, *operands, scratch=(), limit=24 * MIB, flops=0):
    def spec(a):
        if isinstance(a, Far):
            return pl.BlockSpec(memory_space=pltpu.HBM)
        return pl.BlockSpec(memory_space=pltpu.SMEM if a.dtype == jnp.int32 else pltpu.VMEM)

    arrays = [a.array if isinstance(a, Far) else a for a in operands]
    return pl.pallas_call(
        kernel,
        out_shape=[a.array if isinstance(a, Far) else a for a in outs],
        in_specs=[spec(a) for a in operands],
        out_specs=[
            pl.BlockSpec(memory_space=pltpu.HBM if isinstance(a, Far) else pltpu.VMEM)
            for a in outs
        ],
        scratch_shapes=list(scratch),
        compiler_params=pltpu.CompilerParams(vmem_limit_bytes=limit),
        cost_estimate=pl.CostEstimate(
            flops=flops,
            bytes_accessed=sum(a.size * a.dtype.itemsize for a in arrays),
            transcendentals=0,
        ),
    )(*arrays)


def shape(*dims, dtype=f32):
    return jax.ShapeDtypeStruct(dims, dtype)


def iota(dims, axis):
    return lax.broadcasted_iota(jnp.int32, dims, axis)


def to_terms(array):
    high = array.astype(bf16).astype(f32)
    return high, array - high


def taps(x, w_ref, flip):
    side, _, shard = x.shape
    size = w_ref.shape[0]
    reach = size // 2
    column = iota((side, side, shard), 1)
    acc = [jnp.zeros((side, shard), f32) for _ in range(side)]
    for b in range(size):
        by = b - reach
        if by:
            moved = jnp.where(
                (column + by >= 0) & (column + by < side), pltpu.roll(x, (-by) % side, 1), 0.0
            )
        else:
            moved = x
        for a in range(size):
            wa, wb = (size - 1 - a, size - 1 - b) if flip else (a, b)
            weight = w_ref[wa, wb : wb + 1, :]
            for p in range(side):
                if 0 <= p + a - reach < side:
                    acc[p] = acc[p] + moved[p + a - reach] * weight
    return acc


def start_kernel(out_ref):
    out_ref[...] = jnp.zeros_like(out_ref)


def conv_kernel(
    _,
    x_far,
    dw_far,
    bias_far,
    copies_ref,
    conv_ref,
    mean_ref,
    x_ref,
    dw_ref,
    bias_ref,
    rows_ref,
    sems,
):
    images, side = x_ref.shape[:2]
    positions = side * side
    loads = ((x_far, x_ref), (dw_far, dw_ref), (bias_far, bias_ref))
    loads = [pltpu.make_async_copy(far, near, sems.at[i]) for i, (far, near) in enumerate(loads)]
    for copy in loads:
        copy.start()
    for copy in loads:
        copy.wait()

    def image(n, carry):
        x = x_ref[n].astype(f32)
        total = jnp.sum(jnp.sum(x, axis=0), axis=0, keepdims=True)
        mean_ref[pl.ds(n, 1), :] = total / positions
        for p, row in enumerate(taps(x, dw_ref, False)):
            rows_ref[pl.ds(pl.multiple_of(n * positions + p * side, side), side), :] = row
        return carry

    lax.fori_loop(0, images, image, 0)
    turned = (rows_ref[...] + bias_ref[...]).T.astype(bf16)
    conv_ref[...] = turned
    for j in range(CHIPS):
        copies_ref[j] = turned


def ready_kernel(
    mine_ref,
    gain_ref,
    bias_ref,
    w_ref,
    labels_far,
    mean_ref,
    scale_ref,
    bout_ref,
    head_gain_ref,
    head_bias_ref,
    project_far,
    rows_ref,
    part_ref,
    vec_ref,
    own_ref,
    tail_ref,
    head_ref,
    project_ref,
    labels_ref,
    sems,
):
    shard = w_ref.shape[0] // BLOCKS
    core = lax.axis_index("mp") % 2
    moves = []
    for k in range(BLOCKS):
        place = 2 * (k % CHIPS) + (core if k < CHIPS else 1 - core)
        source = pl.ds(pl.multiple_of(place * shard, 64), shard)
        moves.append(
            pltpu.make_async_copy(
                w_ref.at[source], own_ref.at[k * shard : (k + 1) * shard], sems.at[k]
            )
        )
    moves.append(
        pltpu.make_async_copy(project_far, project_ref.at[0:shard], sems.at[BLOCKS])
    )
    load = pltpu.make_async_copy(labels_far, labels_ref, sems.at[BLOCKS + 1])
    load.start()
    for copy in moves:
        copy.start()
    head_ref[0:4, :] = mean_ref[...]
    for i, ref in enumerate((scale_ref, bout_ref, head_gain_ref, head_bias_ref)):
        head_ref[4 + i : 5 + i, :] = ref[...]
    high, rest = to_terms(head_ref[...])
    middle, low = to_terms(rest)
    project_ref[shard:, :] = jnp.zeros_like(project_ref[shard:, :])
    for i, term in enumerate((high, middle, low)):
        sent = jnp.concatenate([term, jnp.zeros_like(term)], axis=0).astype(bf16)
        project_ref[shard:, i * 256 : i * 256 + shard] = sent
    half, rows = mine_ref.shape
    step = 256
    first = jnp.zeros((1, rows), f32)
    second = jnp.zeros((1, rows), f32)
    for c in range(half // step):
        at = slice(c * step, (c + 1) * step)
        rows_ref[:, at] = mine_ref[at, :].T
        value = mine_ref[at, :].astype(f32)
        first = first + jnp.sum(value, axis=0, keepdims=True)
        second = second + jnp.sum(value * value, axis=0, keepdims=True)
    part_ref[0:1, :] = first
    part_ref[1:2, :] = second
    vec_ref[...] = jnp.zeros_like(vec_ref)
    for i, ref in enumerate((gain_ref, bias_ref)):
        for j in range(CHIPS):
            low = ref[:, 2 * j * shard : (2 * j + 1) * shard]
            high = ref[:, (2 * j + 1) * shard : (2 * j + 2) * shard]
            vec_ref[i : i + 1, j * shard : (j + 1) * shard] = jnp.where(core == 0, low, high)
            vec_ref[i : i + 1, half + j * shard : half + (j + 1) * shard] = jnp.where(
                core == 0, high, low
            )
    load.wait()
    pairs = labels_ref.shape[0]
    row = iota((8, 128), 0)
    tail = jnp.zeros((8, 128), f32)
    for r in range(pairs):
        label = labels_ref[r]
        target = (label // pairs) * 8 + 4 + label % pairs
        tail = jnp.where(row == r, target.astype(f32), tail)
    tail_ref[...] = tail
    for copy in moves:
        copy.wait()


def forward_kernel(
    rows_ref,
    other_ref,
    part_ref,
    vec_ref,
    w_ref,
    b_ref,
    wout_ref,
    slope_ref,
    hidden_ref,
    through_ref,
    stat_ref,
    mixed_ref,
    normed_ref,
):
    half, rows = other_ref.shape
    channels, hidden = w_ref.shape
    images = rows // POSITIONS
    positions = POSITIONS
    step = 256
    first, second = part_ref[0:1, :], part_ref[1:2, :]
    for c in range(half // step):
        value = other_ref[c * step : (c + 1) * step, :].astype(f32)
        first = first + jnp.sum(value, axis=0, keepdims=True)
        second = second + jnp.sum(value * value, axis=0, keepdims=True)
    average = first / channels
    inverse = lax.rsqrt(second / channels - average * average + eps)
    lane = iota((8, rows), 0)
    stat_ref[...] = jnp.where(lane == 0, average, jnp.where(lane == 1, inverse, 0.0))
    turned = stat_ref[...].T
    average = jnp.broadcast_to(turned[:, 0:1], (rows, step))
    inverse = jnp.broadcast_to(turned[:, 1:2], (rows, step))
    for c in range(channels // step):
        at = slice(c * step, (c + 1) * step)
        if c * step < half:
            value = rows_ref[:, at]
        else:
            value = other_ref[c * step - half : (c + 1) * step - half, :].T
        value = (value.astype(f32) - average) * inverse
        normed_ref[0:rows, at] = (value * vec_ref[0:1, at] + vec_ref[1:2, at]).astype(bf16)
    normed_ref[rows : rows + 16, :] = jnp.concatenate(to_terms(vec_ref[...]), axis=0).astype(bf16)
    b_row = b_ref[...][None, :]
    whole = jnp.dot(normed_ref[...], w_ref[...], preferred_element_type=f32)
    for t in range(hidden // step):
        at = slice(t * step, (t + 1) * step)
        product = whole[:, at]
        through_ref[:, at] = product[rows:]
        pre = product[:rows] + b_row[:, at]
        hidden_ref[:, at] = pre
        gate = 0.5 + 0.5 * lax.erf(pre * root_half)
        slope_ref[:, at] = gate + pre * jnp.exp(-0.5 * pre * pre) * inv_root_two_pi
        active = pre * gate
        sums = [
            jnp.sum(active[n * positions : (n + 1) * positions], axis=0, keepdims=True) / positions
            for n in range(images)
        ]
        sums = jnp.concatenate(sums + [jnp.zeros((8 - images, step), f32)], axis=0)
        high, low = to_terms(sums)
        part = jnp.dot(
            jnp.concatenate([high, low], axis=0).astype(bf16),
            wout_ref[at, :],
            preferred_element_type=f32,
        )
        part = part[:8] + part[8:]
        mixed = part if t == 0 else mixed + part
    mixed_ref[...] = mixed


def block_kernel(mixed_ref, _project, out_ref):
    shard = out_ref.shape[2]
    images = out_ref.shape[1] // 2
    for k in range(BLOCKS):
        block = mixed_ref[:images, k * shard : (k + 1) * shard]
        out_ref[k, :images, :] = block
        out_ref[k ^ 1, images:, :] = block


def head_kernel(got_ref, own_ref, project_ref, other_ref, out_ref, pooled_ref):
    images = pooled_ref.shape[0]
    width = project_ref.shape[1]
    mixed = got_ref[0]
    for j in range(1, BLOCKS):
        mixed = mixed + got_ref[j]
    first = jnp.zeros((8, 1), f32)
    second = jnp.zeros((8, 1), f32)
    product = jnp.zeros((24, width), f32)
    shard = own_ref.shape[1]
    sent = other_ref[shard:, :].astype(f32)[:8]
    other = sent[:, :shard] + (sent[:, 256 : 256 + shard] + sent[:, 512 : 512 + shard])
    sides = (
        (own_ref[...], project_ref[...], mixed[:images]),
        (other, other_ref[:shard, :], mixed[images:]),
    )
    for i, (rows, weight, part) in enumerate(sides):
        gain = rows[6:7, :]
        pooled = rows[:images, :] + rows[4:5, :] * (part + rows[5:6, :])
        if i == 0:
            pooled_ref[...] = pooled
        head = jnp.concatenate([pooled, rows[images:, :]], axis=0)
        first = first + jnp.sum(head, axis=1, keepdims=True)
        second = second + jnp.sum(head * head, axis=1, keepdims=True)
        value = jnp.where(iota(head.shape, 0) < images, head * gain, head)
        high, rest = to_terms(value)
        middle, low = to_terms(rest)
        product = product + jnp.dot(
            jnp.concatenate([high, middle, low], axis=0).astype(bf16),
            weight,
            preferred_element_type=f32,
        )
    product = product[:8] + (product[8:16] + product[16:])
    lane = iota((8, 128), 1)
    tail = jnp.where(lane == 0, first, jnp.where(lane == 1, second, 0.0))
    for j in range(CHIPS):
        out_ref[j, :, :width] = product
        out_ref[j, :, width:] = tail


def embed_kernel(got_ref, text_ref, tail_ref, out_ref, own_ref, back_ref, stat_ref):
    width = text_ref.shape[1]
    channels = BLOCKS * SHARD
    sums = got_ref[0]
    for j in range(1, CHIPS):
        sums = sums + got_ref[j]
    mean = sums[:, width : width + 1] / channels
    inverse = lax.rsqrt(sums[:, width + 1 : width + 2] / channels - mean * mean + eps)
    centred = inverse * (sums[:, :width] - mean * sums[6:7, :width])
    emb = centred + sums[7:8, :width]
    back_ref[...] = jnp.concatenate([centred[:4], sums[4:, :width]], axis=0)
    tail = tail_ref[...]
    block = jnp.concatenate([emb[:4], text_ref[...]], axis=0)
    own_ref[...] = block
    block = block.astype(bf16)
    tail = tail.astype(bf16)
    for d in range(out_ref.shape[0]):
        out_ref[d, :, :width] = block
        out_ref[d, :, width:] = tail
    stat_ref[0] = jnp.broadcast_to(mean, (8, 128))
    stat_ref[1] = jnp.broadcast_to(inverse, (8, 128))


def loss_kernel(
    got_ref,
    own_ref,
    rows_ref,
    stat_ref,
    pooled_ref,
    scale_ref,
    gain_ref,
    project_ref,
    text_far,
    block_ref,
    mixed_ref,
    both_ref,
    text_ref,
    sem,
):
    width = project_ref.shape[1]
    count = got_ref.shape[0] * 8
    home = pl.ds(pl.multiple_of(lax.axis_index("dp") * 8, 8), 8)
    got = got_ref[...].astype(f32).reshape(count, width + 128)
    raw = got[:, :width].astype(bf16)
    product = lax.dot_general(raw, raw, (((1,), (1,)), ((), ())), preferred_element_type=f32)
    same = iota((count, count), 0) == iota((count, count), 1)
    square = jnp.where(same, product, 0.0)
    row_len = jnp.sqrt(jnp.sum(square, axis=1, keepdims=True) + eps)
    col_len = jnp.sqrt(jnp.sum(square, axis=0, keepdims=True) + eps)
    logits = logit_scale * (product / (row_len * col_len))
    column = iota((count, count), 1)
    valid = (iota((count, count), 0) % 8 < 4) & (column % 8 >= 4)
    weights = jnp.where(valid, jnp.exp(jnp.where(valid, logits, 0.0)), 0.0)
    row_total = jnp.sum(weights, axis=1, keepdims=True)
    col_total = jnp.sum(weights, axis=0, keepdims=True)
    target = got[:, width : width + 1]
    matched = jnp.where(target == column.astype(f32), 1.0, 0.0)
    grads = loss_scale * (0.5 * (weights / row_total + weights / col_total) - matched)
    grads = jnp.where(valid, grads, 0.0)
    both_ref[...] = (grads + grads.T) / col_len
    high, rest = to_terms(both_ref[home, :])
    middle, low = to_terms(rest)
    grad_unit = jnp.dot(
        jnp.concatenate([high, middle, low], axis=0).astype(bf16), raw, preferred_element_type=f32
    )
    grad_unit = logit_scale * (grad_unit[:8] + (grad_unit[8:16] + grad_unit[16:]))
    own = own_ref[...]
    length = jnp.sqrt(jnp.sum(own * own, axis=1, keepdims=True) + eps)
    own = own / length
    grad = (grad_unit - own * jnp.sum(own * grad_unit, axis=1, keepdims=True)) / length
    text_ref[...] = grad[4:]
    send = pltpu.make_async_copy(text_ref, text_far, sem)
    send.start()
    grad = grad[:4].astype(bf16)
    back = lax.dot_general(
        jnp.concatenate([grad, jnp.zeros_like(grad)], axis=0),
        project_ref[...],
        (((1,), (1,)), ((), ())),
        preferred_element_type=f32,
    )[:4]
    channels = BLOCKS * SHARD
    grad = grad.astype(f32)
    first = jnp.sum(grad * rows_ref[6:7, :], axis=1, keepdims=True) / channels
    second = jnp.sum(grad * rows_ref[:4, :], axis=1, keepdims=True) / channels
    mean, inverse = stat_ref[0][:4, 0:1], stat_ref[1][:4, 0:1]
    centred = (pooled_ref[...] - mean) * inverse
    block = (inverse / POSITIONS) * (back * gain_ref[...] - first - centred * second)
    block_ref[...] = block
    for k in range(BLOCKS):
        mixed_ref[k] = block * scale_ref[...]
    send.wait()


def backward_kernel(
    got_ref,
    wout_ref,
    slope_ref,
    hidden_ref,
    w_ref,
    through_ref,
    b_ref,
    other_ref,
    turned_ref,
    sums_ref,
    mixed_ref,
    pre_ref,
):
    images, shard = got_ref.shape[1:]
    rows, hidden = slope_ref.shape
    channels = w_ref.shape[0]
    positions = rows // images
    mixed_ref[...] = jnp.zeros_like(mixed_ref)
    for k in range(BLOCKS):
        mixed_ref[0:images, k * shard : (k + 1) * shard] = got_ref[k]
    act = lax.dot_general(
        mixed_ref[...].astype(bf16),
        wout_ref[...],
        (((1,), (1,)), ((), ())),
        preferred_element_type=f32,
    )
    b_row = b_ref[...][None, :]
    step = 256
    one = jnp.zeros((rows, 1), f32)
    two = jnp.zeros((rows, 1), f32)
    for t in range(hidden // step):
        at = slice(t * step, (t + 1) * step)
        for n in range(images):
            span = slice(n * positions, (n + 1) * positions)
            pre_ref[span, :] = (act[n : n + 1, at] * slope_ref[span, at]).astype(bf16).astype(f32)
        value = pre_ref[...]
        gain = through_ref[0:1, at] + through_ref[8:9, at]
        bias = through_ref[1:2, at] + through_ref[9:10, at] + b_row[:, at]
        one = one + jnp.sum(value * gain, axis=1, keepdims=True)
        two = two + jnp.sum(value * (hidden_ref[:, at] - bias), axis=1, keepdims=True)
        turned_ref[at, :] = value.T.astype(bf16)
    lane = iota((rows, 128), 1)
    sums = jnp.where(lane == 0, one, jnp.where(lane == 1, two, 0.0)).T[:8]
    sums_ref[...] = sums
    high, low = to_terms(sums)
    half = channels // 2
    part = other_ref.shape[0] - 16
    other_ref[part:, :] = jnp.concatenate([high, low], axis=0).astype(bf16)
    other_ref[:part, :] = jnp.dot(
        w_ref[half : half + part, :], turned_ref[...], preferred_element_type=f32
    ).astype(bf16)


def rest_kernel(w_ref, turned_ref, other_ref):
    other_ref[...] = jnp.dot(
        w_ref[w_ref.shape[0] - other_ref.shape[0] :, :],
        turned_ref[...],
        preferred_element_type=f32,
    ).astype(bf16)


def mine_kernel(
    _, w_ref, turned_ref, conv_ref, stat_ref, gain_ref, mine_ref, scaled_ref, centred_ref, row_ref
):
    shard = conv_ref.shape[0]
    index = lax.axis_index("mp")
    pair = gain_ref[:, pl.ds(pl.multiple_of(index // 2 * 2 * shard, 128), 2 * shard)]
    gain = jnp.where(index % 2 == 0, pair[:, :shard], pair[:, shard:])
    gain = jnp.broadcast_to(gain, (8, shard)).T[:, 0:1]
    average, inverse = stat_ref[0:1, :], stat_ref[1:2, :]
    scaled_ref[...] = gain * inverse
    centred_ref[...] = (conv_ref[...].astype(f32) - average) * (inverse * inverse)
    row_ref[...] = jnp.broadcast_to(inverse, row_ref.shape)
    mine_ref[...] = jnp.dot(
        w_ref[: mine_ref.shape[0], :], turned_ref[...], preferred_element_type=f32
    ).astype(bf16)


def pair_kernel(mine_ref, got_ref, later_ref, sums_ref, out_ref):
    part = later_ref.shape[0]
    shard = mine_ref.shape[0] // CHIPS
    for j in range(CHIPS):
        span = slice(j * shard, (j + 1) * shard)
        if j * shard < part:
            got = got_ref[span, :]
        else:
            got = later_ref[j * shard - part : (j + 1) * shard - part, :]
        out_ref[j, :shard, :] = (mine_ref[span, :].astype(f32) + got.astype(f32)).astype(bf16)
    tail = got_ref[part:, :].astype(f32)
    high, low = to_terms(sums_ref[...] + (tail[:8] + tail[8:]))
    tail = jnp.concatenate([high, low], axis=0).astype(bf16)
    for j in range(CHIPS):
        out_ref[j, shard:, :] = tail


def final_kernel(
    got_ref, scaled_ref, centred_ref, row_ref, w_ref, block_ref, out_far, rows_ref, out_ref, sems
):
    shard = scaled_ref.shape[0]
    channels = shard * BLOCKS
    images, side = out_ref.shape[:2]
    positions = side * side
    total = got_ref[0].astype(f32)
    for j in range(1, CHIPS):
        total = total + got_ref[j].astype(f32)
    first = (total[shard : shard + 1] + total[shard + 8 : shard + 9]) / channels
    second = (total[shard + 1 : shard + 2] + total[shard + 9 : shard + 10]) / channels
    first = first * row_ref[0:1, :]
    grad = total[:shard] * scaled_ref[...] - first - centred_ref[...] * second
    rows_ref[...] = grad.T

    def image(n, carry):
        span = pl.ds(pl.multiple_of(n * positions, positions), positions)
        x = rows_ref[span, :].reshape(side, side, shard)
        base = block_ref[pl.ds(n, 1), :]
        for p, row in enumerate(taps(x, w_ref, True)):
            out_ref[n, p] = row + base
        pltpu.make_async_copy(out_ref.at[n], out_far.at[n], sems.at[n]).start()
        return carry

    lax.fori_loop(0, images, image, 0)
    for n in range(images):
        pltpu.make_async_copy(out_ref.at[n], out_far.at[n], sems.at[n]).wait()


def body(
    x_in,
    dw_weight,
    dw_bias,
    ln_gain,
    ln_bias,
    w_in,
    b_in,
    w_out,
    b_out,
    layer_scale,
    head_gain,
    head_bias,
    projection,
    text_emb,
    labels,
):
    images, side, _, shard = x_in.shape
    channels, hidden = w_in.shape
    rows = images * side * side
    pairs, width = text_emb.shape
    shards = lax.axis_size("dp")
    (begun,) = run(start_kernel, [shape(8, 128)], flops=START_FLOPS)
    copies, conv, input_mean = run(
        conv_kernel,
        [
            shape(CHIPS, shard, rows, dtype=bf16),
            shape(shard, rows, dtype=bf16),
            shape(images, shard),
        ],
        Far(begun),
        Far(x_in),
        Far(dw_weight),
        Far(dw_bias[None, :]),
        scratch=[
            pltpu.VMEM(x_in.shape, bf16),
            pltpu.VMEM(dw_weight.shape, f32),
            pltpu.VMEM((1, shard), f32),
            pltpu.VMEM((rows, shard), f32),
            pltpu.SemaphoreType.DMA((3,)),
        ],
        limit=CONV_LIMIT,
        flops=CONV_FLOPS,
    )
    conv_mine = chip_exchange(copies)
    conv_other = core_swap(conv_mine)
    conv_mine = conv_mine.reshape(channels // 2, rows)
    conv_other = conv_other.reshape(channels // 2, rows)
    own_rows, part, vec, w_own, tail, head_own, project_sent = run(
        ready_kernel,
        [
            shape(rows, channels // 2, dtype=bf16),
            shape(8, rows),
            shape(8, channels),
            shape(channels, hidden, dtype=bf16),
            shape(8, 128),
            shape(8, shard),
            shape(shard + 16, width, dtype=bf16),
        ],
        conv_mine,
        ln_gain[None, :],
        ln_bias[None, :],
        w_in,
        Far(labels),
        input_mean,
        layer_scale[None, :],
        b_out[None, :],
        head_gain[None, :],
        head_bias[None, :],
        Far(projection),
        scratch=[pltpu.SMEM(labels.shape, jnp.int32), pltpu.SemaphoreType.DMA((BLOCKS + 2,))],
        flops=READY_FLOPS,
    )
    project_other = core_swap(project_sent)
    slope, hidden_pre, through, row_stat, mixed = run(
        forward_kernel,
        [
            shape(rows, hidden),
            shape(rows, hidden),
            shape(16, hidden),
            shape(8, rows),
            shape(8, channels),
        ],
        own_rows,
        conv_other,
        part,
        vec,
        w_own,
        b_in,
        w_out,
        scratch=[pltpu.VMEM((rows + 16, channels), bf16)],
        flops=2 * rows * channels * hidden,
    )
    (mixed,) = run(
        block_kernel,
        [shape(BLOCKS, 2 * images, shard)],
        mixed,
        Far(project_other),
    )
    blocks, pooled = run(
        head_kernel,
        [shape(CHIPS, 8, width + 128), shape(images, shard)],
        shard_exchange(mixed),
        head_own,
        projection,
        project_other,
    )
    pair_block, own_block, back_rows, head_stat = run(
        embed_kernel,
        [
            shape(shards, 8, width + 128, dtype=bf16),
            shape(8, width),
            shape(8, width),
            shape(2, 8, 128),
        ],
        chip_exchange(blocks),
        text_emb,
        tail,
    )
    grad_text, grad_block, mixed_block = run(
        loss_kernel,
        [Far(shape(pairs, width)), shape(images, shard), shape(BLOCKS, images, shard)],
        lax.all_to_all(pair_block, "dp", 0, 0),
        own_block,
        back_rows,
        head_stat,
        pooled,
        layer_scale[None, :],
        head_gain[None, :],
        projection,
        scratch=[
            pltpu.VMEM((shards * 8, shards * 8), f32),
            pltpu.VMEM((pairs, width), f32),
            pltpu.SemaphoreType.DMA,
        ],
    )
    other, turned, row_sums = run(
        backward_kernel,
        [
            shape(channels // 4 + 16, rows, dtype=bf16),
            shape(hidden, rows, dtype=bf16),
            shape(8, rows),
        ],
        shard_exchange(mixed_block),
        w_out,
        slope,
        hidden_pre,
        w_own,
        through,
        b_in,
        scratch=[pltpu.VMEM((8, channels), f32), pltpu.VMEM((rows, 256), f32)],
        flops=rows * channels * hidden,
    )
    passed = core_swap(other)
    (later,) = run(
        rest_kernel,
        [shape(channels // 4, rows, dtype=bf16)],
        w_own,
        turned,
        flops=rows * channels * hidden // 2,
    )
    passed_later = core_swap(later)
    mine, scaled, centred, row_inverse = run(
        mine_kernel,
        [
            shape(channels // 2, rows, dtype=bf16),
            shape(shard, rows),
            shape(shard, rows),
            shape(8, rows),
        ],
        Far(later),
        w_own,
        turned,
        conv,
        row_stat,
        ln_gain[None, :],
        flops=rows * channels * hidden,
    )
    (blocks,) = run(
        pair_kernel, [shape(CHIPS, shard + 16, rows, dtype=bf16)], mine, passed, passed_later, row_sums
    )
    (grad_input,) = run(
        final_kernel,
        [Far(shape(images, side, side, shard))],
        chip_exchange(blocks),
        scaled,
        centred,
        row_inverse,
        dw_weight,
        grad_block,
        scratch=[
            pltpu.VMEM((rows, shard), f32),
            pltpu.VMEM((images, side, side, shard), f32),
            pltpu.SemaphoreType.DMA((images,)),
        ],
        flops=2 * 49 * rows * shard,
    )
    return (grad_input, grad_text)


def solution(mesh):
    return jax.shard_map(
        body,
        mesh=mesh,
        in_specs=(
            P("dp", None, None, "mp"),
            P(None, None, "mp"),
            P("mp"),
            P(),
            P(),
            P(None, "mp"),
            P("mp"),
            P("mp", None),
            P("mp"),
            P("mp"),
            P("mp"),
            P("mp"),
            P("mp", None),
            P("dp", None),
            P("dp"),
        ),
        out_specs=(P("dp", None, None, "mp"), P("dp", None)),
        check_vma=False,
    )
```

```python
import jax
import jax.numpy as jnp
from jax import lax
from jax.experimental import pallas as pl
from jax.experimental.pallas import tpu as pltpu
from jax.sharding import PartitionSpec as P

eps = 1e-06
logit_scale = 20.0
loss_scale = 512.0
root_half = 0.7071067811865476
inv_root_two_pi = 0.3989422804014327
f32 = jnp.float32
bf16 = jnp.bfloat16
MIB = 1 << 20
CONV_LIMIT = 50 * MIB
CONV_FLOPS = 16 * 10**9
START_FLOPS = 4 * 10**9
READY_FLOPS = 12 * 10**9
CHIPS = 8
BLOCKS = 16
SHARD = 192
POSITIONS = 64


def core_swap(array):
    return lax.ppermute(array, "mp", [(i, i ^ 1) for i in range(BLOCKS)])


def chip_exchange(array):
    groups = [[i for i in range(core, BLOCKS, 2)] for core in range(2)]
    return lax.all_to_all(array, "mp", 0, 0, axis_index_groups=groups)


def shard_exchange(array):
    return lax.all_to_all(array, "mp", 0, 0)


class Far:
    def __init__(self, array):
        self.array = array


def run(kernel, outs, *operands, scratch=(), limit=24 * MIB, flops=0):
    def spec(a):
        if isinstance(a, Far):
            return pl.BlockSpec(memory_space=pltpu.HBM)
        return pl.BlockSpec(memory_space=pltpu.SMEM if a.dtype == jnp.int32 else pltpu.VMEM)

    arrays = [a.array if isinstance(a, Far) else a for a in operands]
    return pl.pallas_call(
        kernel,
        out_shape=[a.array if isinstance(a, Far) else a for a in outs],
        in_specs=[spec(a) for a in operands],
        out_specs=[
            pl.BlockSpec(memory_space=pltpu.HBM if isinstance(a, Far) else pltpu.VMEM)
            for a in outs
        ],
        scratch_shapes=list(scratch),
        compiler_params=pltpu.CompilerParams(vmem_limit_bytes=limit),
        cost_estimate=pl.CostEstimate(
            flops=flops,
            bytes_accessed=sum(a.size * a.dtype.itemsize for a in arrays),
            transcendentals=0,
        ),
    )(*arrays)


def shape(*dims, dtype=f32):
    return jax.ShapeDtypeStruct(dims, dtype)


def iota(dims, axis):
    return lax.broadcasted_iota(jnp.int32, dims, axis)


def to_terms(array):
    high = array.astype(bf16).astype(f32)
    return high, array - high


def taps(x, w_ref, flip):
    side, _, shard = x.shape
    size = w_ref.shape[0]
    reach = size // 2
    column = iota((side, side, shard), 1)
    acc = [jnp.zeros((side, shard), f32) for _ in range(side)]
    for b in range(size):
        by = b - reach
        if by:
            moved = jnp.where(
                (column + by >= 0) & (column + by < side), pltpu.roll(x, (-by) % side, 1), 0.0
            )
        else:
            moved = x
        for a in range(size):
            wa, wb = (size - 1 - a, size - 1 - b) if flip else (a, b)
            weight = w_ref[wa, wb : wb + 1, :]
            for p in range(side):
                if 0 <= p + a - reach < side:
                    acc[p] = acc[p] + moved[p + a - reach] * weight
    return acc


def start_kernel(out_ref):
    out_ref[...] = jnp.zeros_like(out_ref)


def conv_kernel(
    _,
    x_far,
    dw_far,
    bias_far,
    copies_ref,
    conv_ref,
    mean_ref,
    x_ref,
    dw_ref,
    bias_ref,
    rows_ref,
    sems,
):
    images, side = x_ref.shape[:2]
    positions = side * side
    loads = ((x_far, x_ref), (dw_far, dw_ref), (bias_far, bias_ref))
    loads = [pltpu.make_async_copy(far, near, sems.at[i]) for i, (far, near) in enumerate(loads)]
    for copy in loads:
        copy.start()
    for copy in loads:
        copy.wait()

    def image(n, carry):
        x = x_ref[n].astype(f32)
        total = jnp.sum(jnp.sum(x, axis=0), axis=0, keepdims=True)
        mean_ref[pl.ds(n, 1), :] = total / positions
        for p, row in enumerate(taps(x, dw_ref, False)):
            rows_ref[pl.ds(pl.multiple_of(n * positions + p * side, side), side), :] = row
        return carry

    lax.fori_loop(0, images, image, 0)
    turned = (rows_ref[...] + bias_ref[...]).T.astype(bf16)
    conv_ref[...] = turned
    for j in range(CHIPS):
        copies_ref[j] = turned


def ready_kernel(
    mine_ref,
    gain_ref,
    bias_ref,
    w_ref,
    labels_far,
    mean_ref,
    scale_ref,
    bout_ref,
    head_gain_ref,
    head_bias_ref,
    project_far,
    rows_ref,
    part_ref,
    vec_ref,
    own_ref,
    tail_ref,
    head_ref,
    project_ref,
    labels_ref,
    sems,
):
    shard = w_ref.shape[0] // BLOCKS
    core = lax.axis_index("mp") % 2
    moves = []
    for k in range(BLOCKS):
        place = 2 * (k % CHIPS) + (core if k < CHIPS else 1 - core)
        source = pl.ds(pl.multiple_of(place * shard, 64), shard)
        moves.append(
            pltpu.make_async_copy(
                w_ref.at[source], own_ref.at[k * shard : (k + 1) * shard], sems.at[k]
            )
        )
    moves.append(
        pltpu.make_async_copy(project_far, project_ref.at[0:shard], sems.at[BLOCKS])
    )
    load = pltpu.make_async_copy(labels_far, labels_ref, sems.at[BLOCKS + 1])
    load.start()
    for copy in moves:
        copy.start()
    head_ref[0:4, :] = mean_ref[...]
    for i, ref in enumerate((scale_ref, bout_ref, head_gain_ref, head_bias_ref)):
        head_ref[4 + i : 5 + i, :] = ref[...]
    high, rest = to_terms(head_ref[...])
    middle, low = to_terms(rest)
    project_ref[shard:, :] = jnp.zeros_like(project_ref[shard:, :])
    for i, term in enumerate((high, middle, low)):
        sent = jnp.concatenate([term, jnp.zeros_like(term)], axis=0).astype(bf16)
        project_ref[shard:, i * 256 : i * 256 + shard] = sent
    half, rows = mine_ref.shape
    step = 256
    first = jnp.zeros((1, rows), f32)
    second = jnp.zeros((1, rows), f32)
    for c in range(half // step):
        at = slice(c * step, (c + 1) * step)
        rows_ref[:, at] = mine_ref[at, :].T
        value = mine_ref[at, :].astype(f32)
        first = first + jnp.sum(value, axis=0, keepdims=True)
        second = second + jnp.sum(value * value, axis=0, keepdims=True)
    part_ref[0:1, :] = first
    part_ref[1:2, :] = second
    vec_ref[...] = jnp.zeros_like(vec_ref)
    for i, ref in enumerate((gain_ref, bias_ref)):
        for j in range(CHIPS):
            low = ref[:, 2 * j * shard : (2 * j + 1) * shard]
            high = ref[:, (2 * j + 1) * shard : (2 * j + 2) * shard]
            vec_ref[i : i + 1, j * shard : (j + 1) * shard] = jnp.where(core == 0, low, high)
            vec_ref[i : i + 1, half + j * shard : half + (j + 1) * shard] = jnp.where(
                core == 0, high, low
            )
    load.wait()
    pairs = labels_ref.shape[0]
    row = iota((8, 128), 0)
    tail = jnp.zeros((8, 128), f32)
    for r in range(pairs):
        label = labels_ref[r]
        target = (label // pairs) * 8 + 4 + label % pairs
        tail = jnp.where(row == r, target.astype(f32), tail)
    tail_ref[...] = tail
    for copy in moves:
        copy.wait()


def forward_kernel(
    rows_ref,
    other_ref,
    part_ref,
    vec_ref,
    w_ref,
    b_ref,
    wout_ref,
    slope_ref,
    hidden_ref,
    through_ref,
    stat_ref,
    mixed_ref,
    normed_ref,
):
    half, rows = other_ref.shape
    channels, hidden = w_ref.shape
    images = rows // POSITIONS
    positions = POSITIONS
    step = 256
    first, second = part_ref[0:1, :], part_ref[1:2, :]
    for c in range(half // step):
        value = other_ref[c * step : (c + 1) * step, :].astype(f32)
        first = first + jnp.sum(value, axis=0, keepdims=True)
        second = second + jnp.sum(value * value, axis=0, keepdims=True)
    average = first / channels
    inverse = lax.rsqrt(second / channels - average * average + eps)
    lane = iota((8, rows), 0)
    stat_ref[...] = jnp.where(lane == 0, average, jnp.where(lane == 1, inverse, 0.0))
    turned = stat_ref[...].T
    average = jnp.broadcast_to(turned[:, 0:1], (rows, step))
    inverse = jnp.broadcast_to(turned[:, 1:2], (rows, step))
    for c in range(channels // step):
        at = slice(c * step, (c + 1) * step)
        if c * step < half:
            value = rows_ref[:, at]
        else:
            value = other_ref[c * step - half : (c + 1) * step - half, :].T
        value = (value.astype(f32) - average) * inverse
        normed_ref[0:rows, at] = (value * vec_ref[0:1, at] + vec_ref[1:2, at]).astype(bf16)
    normed_ref[rows : rows + 16, :] = jnp.concatenate(to_terms(vec_ref[...]), axis=0).astype(bf16)
    b_row = b_ref[...][None, :]
    whole = jnp.dot(normed_ref[...], w_ref[...], preferred_element_type=f32)
    for t in range(hidden // step):
        at = slice(t * step, (t + 1) * step)
        product = whole[:, at]
        through_ref[:, at] = product[rows:]
        pre = product[:rows] + b_row[:, at]
        hidden_ref[:, at] = pre
        gate = 0.5 + 0.5 * lax.erf(pre * root_half)
        slope_ref[:, at] = gate + pre * jnp.exp(-0.5 * pre * pre) * inv_root_two_pi
        active = pre * gate
        sums = [
            jnp.sum(active[n * positions : (n + 1) * positions], axis=0, keepdims=True) / positions
            for n in range(images)
        ]
        sums = jnp.concatenate(sums + [jnp.zeros((8 - images, step), f32)], axis=0)
        high, low = to_terms(sums)
        part = jnp.dot(
            jnp.concatenate([high, low], axis=0).astype(bf16),
            wout_ref[at, :],
            preferred_element_type=f32,
        )
        part = part[:8] + part[8:]
        mixed = part if t == 0 else mixed + part
    mixed_ref[...] = mixed


def block_kernel(mixed_ref, _project, out_ref):
    shard = out_ref.shape[2]
    images = out_ref.shape[1] // 2
    for k in range(BLOCKS):
        block = mixed_ref[:images, k * shard : (k + 1) * shard]
        out_ref[k, :images, :] = block
        out_ref[k ^ 1, images:, :] = block


def head_kernel(got_ref, own_ref, project_ref, other_ref, out_ref, pooled_ref):
    images = pooled_ref.shape[0]
    width = project_ref.shape[1]
    mixed = got_ref[0]
    for j in range(1, BLOCKS):
        mixed = mixed + got_ref[j]
    first = jnp.zeros((8, 1), f32)
    second = jnp.zeros((8, 1), f32)
    product = jnp.zeros((24, width), f32)
    shard = own_ref.shape[1]
    sent = other_ref[shard:, :].astype(f32)[:8]
    other = sent[:, :shard] + (sent[:, 256 : 256 + shard] + sent[:, 512 : 512 + shard])
    sides = (
        (own_ref[...], project_ref[...], mixed[:images]),
        (other, other_ref[:shard, :], mixed[images:]),
    )
    for i, (rows, weight, part) in enumerate(sides):
        gain = rows[6:7, :]
        pooled = rows[:images, :] + rows[4:5, :] * (part + rows[5:6, :])
        if i == 0:
            pooled_ref[...] = pooled
        head = jnp.concatenate([pooled, rows[images:, :]], axis=0)
        first = first + jnp.sum(head, axis=1, keepdims=True)
        second = second + jnp.sum(head * head, axis=1, keepdims=True)
        value = jnp.where(iota(head.shape, 0) < images, head * gain, head)
        high, rest = to_terms(value)
        middle, low = to_terms(rest)
        product = product + jnp.dot(
            jnp.concatenate([high, middle, low], axis=0).astype(bf16),
            weight,
            preferred_element_type=f32,
        )
    product = product[:8] + (product[8:16] + product[16:])
    lane = iota((8, 128), 1)
    tail = jnp.where(lane == 0, first, jnp.where(lane == 1, second, 0.0))
    for j in range(CHIPS):
        out_ref[j, :, :width] = product
        out_ref[j, :, width:] = tail


def embed_kernel(got_ref, text_ref, tail_ref, out_ref, own_ref, back_ref, stat_ref):
    width = text_ref.shape[1]
    channels = BLOCKS * SHARD
    sums = got_ref[0]
    for j in range(1, CHIPS):
        sums = sums + got_ref[j]
    mean = sums[:, width : width + 1] / channels
    inverse = lax.rsqrt(sums[:, width + 1 : width + 2] / channels - mean * mean + eps)
    centred = inverse * (sums[:, :width] - mean * sums[6:7, :width])
    emb = centred + sums[7:8, :width]
    back_ref[...] = jnp.concatenate([centred[:4], sums[4:, :width]], axis=0)
    tail = tail_ref[...]
    block = jnp.concatenate([emb[:4], text_ref[...]], axis=0)
    own_ref[...] = block
    block = block.astype(bf16)
    tail = tail.astype(bf16)
    for d in range(out_ref.shape[0]):
        out_ref[d, :, :width] = block
        out_ref[d, :, width:] = tail
    stat_ref[0] = jnp.broadcast_to(mean, (8, 128))
    stat_ref[1] = jnp.broadcast_to(inverse, (8, 128))


def loss_kernel(
    got_ref,
    own_ref,
    rows_ref,
    stat_ref,
    pooled_ref,
    scale_ref,
    gain_ref,
    project_ref,
    text_far,
    block_ref,
    mixed_ref,
    both_ref,
    text_ref,
    sem,
):
    width = project_ref.shape[1]
    count = got_ref.shape[0] * 8
    home = pl.ds(pl.multiple_of(lax.axis_index("dp") * 8, 8), 8)
    got = got_ref[...].astype(f32).reshape(count, width + 128)
    raw = got[:, :width].astype(bf16)
    product = lax.dot_general(raw, raw, (((1,), (1,)), ((), ())), preferred_element_type=f32)
    same = iota((count, count), 0) == iota((count, count), 1)
    square = jnp.where(same, product, 0.0)
    row_len = jnp.sqrt(jnp.sum(square, axis=1, keepdims=True) + eps)
    col_len = jnp.sqrt(jnp.sum(square, axis=0, keepdims=True) + eps)
    logits = logit_scale * (product / (row_len * col_len))
    column = iota((count, count), 1)
    valid = (iota((count, count), 0) % 8 < 4) & (column % 8 >= 4)
    weights = jnp.where(valid, jnp.exp(jnp.where(valid, logits, 0.0)), 0.0)
    row_total = jnp.sum(weights, axis=1, keepdims=True)
    col_total = jnp.sum(weights, axis=0, keepdims=True)
    target = got[:, width : width + 1]
    matched = jnp.where(target == column.astype(f32), 1.0, 0.0)
    grads = loss_scale * (0.5 * (weights / row_total + weights / col_total) - matched)
    grads = jnp.where(valid, grads, 0.0)
    both_ref[...] = (grads + grads.T) / col_len
    high, rest = to_terms(both_ref[home, :])
    middle, low = to_terms(rest)
    grad_unit = jnp.dot(
        jnp.concatenate([high, middle, low], axis=0).astype(bf16), raw, preferred_element_type=f32
    )
    grad_unit = logit_scale * (grad_unit[:8] + (grad_unit[8:16] + grad_unit[16:]))
    own = own_ref[...]
    length = jnp.sqrt(jnp.sum(own * own, axis=1, keepdims=True) + eps)
    own = own / length
    grad = (grad_unit - own * jnp.sum(own * grad_unit, axis=1, keepdims=True)) / length
    text_ref[...] = grad[4:]
    send = pltpu.make_async_copy(text_ref, text_far, sem)
    send.start()
    grad = grad[:4].astype(bf16)
    back = lax.dot_general(
        jnp.concatenate([grad, jnp.zeros_like(grad)], axis=0),
        project_ref[...],
        (((1,), (1,)), ((), ())),
        preferred_element_type=f32,
    )[:4]
    channels = BLOCKS * SHARD
    grad = grad.astype(f32)
    first = jnp.sum(grad * rows_ref[6:7, :], axis=1, keepdims=True) / channels
    second = jnp.sum(grad * rows_ref[:4, :], axis=1, keepdims=True) / channels
    mean, inverse = stat_ref[0][:4, 0:1], stat_ref[1][:4, 0:1]
    centred = (pooled_ref[...] - mean) * inverse
    block = (inverse / POSITIONS) * (back * gain_ref[...] - first - centred * second)
    block_ref[...] = block
    for k in range(BLOCKS):
        mixed_ref[k] = block * scale_ref[...]
    send.wait()


def backward_kernel(
    got_ref,
    wout_ref,
    slope_ref,
    hidden_ref,
    w_ref,
    through_ref,
    b_ref,
    other_ref,
    turned_ref,
    sums_ref,
    mixed_ref,
    pre_ref,
):
    images, shard = got_ref.shape[1:]
    rows, hidden = slope_ref.shape
    channels = w_ref.shape[0]
    positions = rows // images
    mixed_ref[...] = jnp.zeros_like(mixed_ref)
    for k in range(BLOCKS):
        mixed_ref[0:images, k * shard : (k + 1) * shard] = got_ref[k]
    act = lax.dot_general(
        mixed_ref[...].astype(bf16),
        wout_ref[...],
        (((1,), (1,)), ((), ())),
        preferred_element_type=f32,
    )
    b_row = b_ref[...][None, :]
    step = 256
    one = jnp.zeros((rows, 1), f32)
    two = jnp.zeros((rows, 1), f32)
    for t in range(hidden // step):
        at = slice(t * step, (t + 1) * step)
        for n in range(images):
            span = slice(n * positions, (n + 1) * positions)
            pre_ref[span, :] = (act[n : n + 1, at] * slope_ref[span, at]).astype(bf16).astype(f32)
        value = pre_ref[...]
        gain = through_ref[0:1, at] + through_ref[8:9, at]
        bias = through_ref[1:2, at] + through_ref[9:10, at] + b_row[:, at]
        one = one + jnp.sum(value * gain, axis=1, keepdims=True)
        two = two + jnp.sum(value * (hidden_ref[:, at] - bias), axis=1, keepdims=True)
        turned_ref[at, :] = value.T.astype(bf16)
    lane = iota((rows, 128), 1)
    sums = jnp.where(lane == 0, one, jnp.where(lane == 1, two, 0.0)).T[:8]
    sums_ref[...] = sums
    high, low = to_terms(sums)
    half = channels // 2
    part = other_ref.shape[0] - 16
    other_ref[part:, :] = jnp.concatenate([high, low], axis=0).astype(bf16)
    other_ref[:part, :] = jnp.dot(
        w_ref[half : half + part, :], turned_ref[...], preferred_element_type=f32
    ).astype(bf16)


def rest_kernel(w_ref, turned_ref, other_ref):
    other_ref[...] = jnp.dot(
        w_ref[w_ref.shape[0] - other_ref.shape[0] :, :],
        turned_ref[...],
        preferred_element_type=f32,
    ).astype(bf16)


def mine_kernel(
    _, w_ref, turned_ref, conv_ref, stat_ref, gain_ref, mine_ref, scaled_ref, centred_ref, row_ref
):
    shard = conv_ref.shape[0]
    index = lax.axis_index("mp")
    pair = gain_ref[:, pl.ds(pl.multiple_of(index // 2 * 2 * shard, 128), 2 * shard)]
    gain = jnp.where(index % 2 == 0, pair[:, :shard], pair[:, shard:])
    gain = jnp.broadcast_to(gain, (8, shard)).T[:, 0:1]
    average, inverse = stat_ref[0:1, :], stat_ref[1:2, :]
    scaled_ref[...] = gain * inverse
    centred_ref[...] = (conv_ref[...].astype(f32) - average) * (inverse * inverse)
    row_ref[...] = jnp.broadcast_to(inverse, row_ref.shape)
    mine_ref[...] = jnp.dot(
        w_ref[: mine_ref.shape[0], :], turned_ref[...], preferred_element_type=f32
    ).astype(bf16)


def pair_kernel(mine_ref, got_ref, later_ref, sums_ref, out_ref):
    part = mine_ref.shape[0] - later_ref.shape[0]
    shard = mine_ref.shape[0] // CHIPS
    for j in range(CHIPS):
        span = slice(j * shard, (j + 1) * shard)
        if j * shard < part:
            got = got_ref[span, :]
        else:
            got = later_ref[j * shard - part : (j + 1) * shard - part, :]
        out_ref[j, :shard, :] = (mine_ref[span, :].astype(f32) + got.astype(f32)).astype(bf16)
    tail = got_ref[part:, :].astype(f32)
    high, low = to_terms(sums_ref[...] + (tail[:8] + tail[8:]))
    tail = jnp.concatenate([high, low], axis=0).astype(bf16)
    for j in range(CHIPS):
        out_ref[j, shard:, :] = tail


def final_kernel(
    got_ref, scaled_ref, centred_ref, row_ref, w_ref, block_ref, out_far, rows_ref, out_ref, sems
):
    shard = scaled_ref.shape[0]
    channels = shard * BLOCKS
    images, side = out_ref.shape[:2]
    positions = side * side
    total = got_ref[0].astype(f32)
    for j in range(1, CHIPS):
        total = total + got_ref[j].astype(f32)
    first = (total[shard : shard + 1] + total[shard + 8 : shard + 9]) / channels
    second = (total[shard + 1 : shard + 2] + total[shard + 9 : shard + 10]) / channels
    first = first * row_ref[0:1, :]
    grad = total[:shard] * scaled_ref[...] - first - centred_ref[...] * second
    rows_ref[...] = grad.T

    def image(n, carry):
        span = pl.ds(pl.multiple_of(n * positions, positions), positions)
        x = rows_ref[span, :].reshape(side, side, shard)
        base = block_ref[pl.ds(n, 1), :]
        for p, row in enumerate(taps(x, w_ref, True)):
            out_ref[n, p] = row + base
        pltpu.make_async_copy(out_ref.at[n], out_far.at[n], sems.at[n]).start()
        return carry

    lax.fori_loop(0, images, image, 0)
    for n in range(images):
        pltpu.make_async_copy(out_ref.at[n], out_far.at[n], sems.at[n]).wait()


def body(
    x_in,
    dw_weight,
    dw_bias,
    ln_gain,
    ln_bias,
    w_in,
    b_in,
    w_out,
    b_out,
    layer_scale,
    head_gain,
    head_bias,
    projection,
    text_emb,
    labels,
):
    images, side, _, shard = x_in.shape
    channels, hidden = w_in.shape
    rows = images * side * side
    pairs, width = text_emb.shape
    shards = lax.axis_size("dp")
    (begun,) = run(start_kernel, [shape(8, 128)], flops=START_FLOPS)
    copies, conv, input_mean = run(
        conv_kernel,
        [
            shape(CHIPS, shard, rows, dtype=bf16),
            shape(shard, rows, dtype=bf16),
            shape(images, shard),
        ],
        Far(begun),
        Far(x_in),
        Far(dw_weight),
        Far(dw_bias[None, :]),
        scratch=[
            pltpu.VMEM(x_in.shape, bf16),
            pltpu.VMEM(dw_weight.shape, f32),
            pltpu.VMEM((1, shard), f32),
            pltpu.VMEM((rows, shard), f32),
            pltpu.SemaphoreType.DMA((3,)),
        ],
        limit=CONV_LIMIT,
        flops=CONV_FLOPS,
    )
    conv_mine = chip_exchange(copies)
    conv_other = core_swap(conv_mine)
    conv_mine = conv_mine.reshape(channels // 2, rows)
    conv_other = conv_other.reshape(channels // 2, rows)
    own_rows, part, vec, w_own, tail, head_own, project_sent = run(
        ready_kernel,
        [
            shape(rows, channels // 2, dtype=bf16),
            shape(8, rows),
            shape(8, channels),
            shape(channels, hidden, dtype=bf16),
            shape(8, 128),
            shape(8, shard),
            shape(shard + 16, width, dtype=bf16),
        ],
        conv_mine,
        ln_gain[None, :],
        ln_bias[None, :],
        w_in,
        Far(labels),
        input_mean,
        layer_scale[None, :],
        b_out[None, :],
        head_gain[None, :],
        head_bias[None, :],
        Far(projection),
        scratch=[pltpu.SMEM(labels.shape, jnp.int32), pltpu.SemaphoreType.DMA((BLOCKS + 2,))],
        flops=READY_FLOPS,
    )
    project_other = core_swap(project_sent)
    slope, hidden_pre, through, row_stat, mixed = run(
        forward_kernel,
        [
            shape(rows, hidden),
            shape(rows, hidden),
            shape(16, hidden),
            shape(8, rows),
            shape(8, channels),
        ],
        own_rows,
        conv_other,
        part,
        vec,
        w_own,
        b_in,
        w_out,
        scratch=[pltpu.VMEM((rows + 16, channels), bf16)],
        flops=2 * rows * channels * hidden,
    )
    (mixed,) = run(
        block_kernel,
        [shape(BLOCKS, 2 * images, shard)],
        mixed,
        Far(project_other),
    )
    blocks, pooled = run(
        head_kernel,
        [shape(CHIPS, 8, width + 128), shape(images, shard)],
        shard_exchange(mixed),
        head_own,
        projection,
        project_other,
    )
    pair_block, own_block, back_rows, head_stat = run(
        embed_kernel,
        [
            shape(shards, 8, width + 128, dtype=bf16),
            shape(8, width),
            shape(8, width),
            shape(2, 8, 128),
        ],
        chip_exchange(blocks),
        text_emb,
        tail,
    )
    grad_text, grad_block, mixed_block = run(
        loss_kernel,
        [Far(shape(pairs, width)), shape(images, shard), shape(BLOCKS, images, shard)],
        lax.all_to_all(pair_block, "dp", 0, 0),
        own_block,
        back_rows,
        head_stat,
        pooled,
        layer_scale[None, :],
        head_gain[None, :],
        projection,
        scratch=[
            pltpu.VMEM((shards * 8, shards * 8), f32),
            pltpu.VMEM((pairs, width), f32),
            pltpu.SemaphoreType.DMA,
        ],
    )
    other, turned, row_sums = run(
        backward_kernel,
        [
            shape(5 * shard + 16, rows, dtype=bf16),
            shape(hidden, rows, dtype=bf16),
            shape(8, rows),
        ],
        shard_exchange(mixed_block),
        w_out,
        slope,
        hidden_pre,
        w_own,
        through,
        b_in,
        scratch=[pltpu.VMEM((8, channels), f32), pltpu.VMEM((rows, 256), f32)],
        flops=rows * channels * hidden,
    )
    passed = core_swap(other)
    (later,) = run(
        rest_kernel,
        [shape(3 * shard, rows, dtype=bf16)],
        w_own,
        turned,
        flops=rows * channels * hidden // 2,
    )
    passed_later = core_swap(later)
    mine, scaled, centred, row_inverse = run(
        mine_kernel,
        [
            shape(channels // 2, rows, dtype=bf16),
            shape(shard, rows),
            shape(shard, rows),
            shape(8, rows),
        ],
        Far(later),
        w_own,
        turned,
        conv,
        row_stat,
        ln_gain[None, :],
        flops=rows * channels * hidden,
    )
    (blocks,) = run(
        pair_kernel, [shape(CHIPS, shard + 16, rows, dtype=bf16)], mine, passed, passed_later, row_sums
    )
    (grad_input,) = run(
        final_kernel,
        [Far(shape(images, side, side, shard))],
        chip_exchange(blocks),
        scaled,
        centred,
        row_inverse,
        dw_weight,
        grad_block,
        scratch=[
            pltpu.VMEM((rows, shard), f32),
            pltpu.VMEM((images, side, side, shard), f32),
            pltpu.SemaphoreType.DMA((images,)),
        ],
        flops=2 * 49 * rows * shard,
    )
    return (grad_input, grad_text)


def solution(mesh):
    return jax.shard_map(
        body,
        mesh=mesh,
        in_specs=(
            P("dp", None, None, "mp"),
            P(None, None, "mp"),
            P("mp"),
            P(),
            P(),
            P(None, "mp"),
            P("mp"),
            P("mp", None),
            P("mp"),
            P("mp"),
            P("mp"),
            P("mp"),
            P("mp", None),
            P("dp", None),
            P("dp"),
        ),
        out_specs=(P("dp", None, None, "mp"), P("dp", None)),
        check_vma=False,
    )
```
